512 devices in a mesh: hist: 16 (over z, core), items: 32 (over x, y).
Axes of the slice: x: 4, y: 8, z: 8, core: 2. Of those that a mesh axis runs over, the one named last changes fastest.
Arguments:
- history: bfloat16 [32, 2048, 512], P('items', 'hist'), may hold values from -6 to 6
- ln_gain: float32 [512], replicated, may hold values from 0.5 to 1.5
- w_in: bfloat16 [512, 2048], replicated, may hold values from -0.25 to 0.25
- w_out: bfloat16 [512, 512], replicated, may hold values from -0.25 to 0.25
- item_table: bfloat16 [131072, 512], P(('hist', 'items')), may hold values from -6 to 6
- sessions: int32 [32, 16], P('items'), may hold values from 0 to 7, never falling along the last dimension, each value on 1 to 3 neighbouring positions
- pos_owner: int32 [32, 2048, 1], P('items', 'hist'), may hold values from 0 to 511; in each aligned block of 128 rows (0 to 127, 128 to 255, ..., all dimensions but the last counted through in order) at most 2 rows name the same one
- pos_row: int32 [32, 2048], P('items', 'hist'), may hold values from 0 to 255
- neg_rows: int32 [32, 512, 1], P('items'), may hold values from 0 to 254, as said below
Outputs:
- history_grad: bfloat16 [32, 2048, 512], P('items', 'hist')
- table_grad: bfloat16 [131072, 512], P(('hist', 'items'))
The draws below stay inside these ranges and needn't reach their ends.
Inputs may be any that keep to these rules, and one draw needn't show every extreme that they name: Within a history, sessions are numbered in order, and each session covers 1 to 3 consecutive blocks. `pos_owner`: among the 128 positions of one device, at most 2 name the same owner. `neg_rows`: entry m under owner o is a row of owner o; rows r are drawn with probability 1 / (L 2^b), b = floor(log2(r + 1)), L = floor(log2(256)).
All inputs are finite; a program needn't handle non-finite values.
Results may differ from the reference program's by a relative error of at most 0.018.
Values may be sent and summed in bfloat16 or wider, within the bound.
No kernel may reach another device: no remote copies, remote signals or barrier semaphores. Data moves between devices by JAX's collectives and lax.ppermute only.
A program may use at most 64 MiB of HBM per device.

```python
import math
import jax
import jax.numpy as jnp
import numpy as np
from jax import lax

D = 512
HEADS = 8
BLOCK = 128
TOK_DEV = 128
R_DEV = 256
NEG_OWN = 1
OWNERS = 512
SEQS = 32
LENGTH = 2048
NBLK = 16
SESSIONS = 8
MOST_BLK = 3
CAP = 2
ROWS = 131072


def draw_neg_rows(key, part):
    key = jax.random.fold_in(key, 11)
    first_key, second_key = jax.random.split(key)
    levels = R_DEV.bit_length() - 1
    shape_all = (SEQS, OWNERS, NEG_OWN)
    exponent = jax.random.randint(first_key, shape_all, 0, levels)
    bucket_size = jnp.left_shift(jnp.ones(shape_all, jnp.int32), exponent)
    offset = jax.random.randint(second_key, shape_all, 0, 1 << 30) % bucket_size
    drawn = (bucket_size - 1 + offset).astype(jnp.int32)
    drawn = drawn.at[0, 0, 0].set((1 << levels) - 2)
    drawn = drawn.at[0, 1, 0].set(0)
    return drawn


def place_ends(values, own_key, smallest, high):
    index_at = [jax.random.randint(jax.random.fold_in(own_key, axis), (), 0, length) for axis, length in enumerate(values.shape)]
    main_axis = values.shape.index(max(values.shape))
    neighbour = index_at[:main_axis] + [(index_at[main_axis] + 1) % values.shape[main_axis]] + index_at[main_axis + 1:]
    return values.at[tuple(index_at)].set(smallest).at[tuple(neighbour)].set(high)


def level_of(own_key, dims, cuts, least, largest):
    loudness = 1.0
    for dim, shards_of in cuts:
        heights = jax.random.uniform(jax.random.fold_in(jax.random.fold_in(own_key, 6), dim), (shards_of,), jnp.float32, least / len(cuts), largest / len(cuts))
        loudness = loudness * jnp.repeat(jnp.exp(heights), dims[dim] // shards_of).reshape((-1,) + (1,) * (len(dims) - 1 - dim))
    return loudness


def length_profile(amount, total, most, lean):
    weights = [(1 << 20) // math.isqrt(grade ** lean) + 1 for grade in range(2, amount + 1)]
    surplus, given = total - most - (amount - 1), [1] * (amount - 1)
    while surplus > 0:
        movable = [i for i in range(amount - 1) if given[i] < most]
        mass, left = sum([weights[i] for i in movable]), surplus
        for i in movable:
            extra = min(most - given[i], max(1, left * weights[i] // mass), surplus)
            given[i] = given[i] + extra
            surplus = surplus - extra
    return np.array([most] + given)


def uneven_parts(own_key, number_of, total, reach, lean):
    if number_of == 2:
        one = jax.random.randint(own_key, (), max(1, total - reach), min(reach, total - 1) + 1)
        return jnp.stack([one, total - one])
    sizes = jnp.asarray(length_profile(number_of, total, reach, lean), jnp.int32)
    couples = (number_of - 1) // 2
    source_of, receiver = sizes[1:1 + 2 * couples:2], sizes[2:2 + 2 * couples:2]
    room = jnp.minimum(source_of - 1, reach - receiver)
    shifted = jax.random.randint(jax.random.fold_in(own_key, 1), (couples,), 0, 1 << 20) % (room + 1)
    sizes = sizes.at[1:1 + 2 * couples:2].set(source_of - shifted).at[2:2 + 2 * couples:2].set(receiver + shifted)
    return sizes[jax.random.permutation(jax.random.fold_in(own_key, 2), number_of)]


def shared_out(stream_key, own, number, rows, count, top, bound, lean):
    order = jax.random.permutation(stream_key, count)
    crowded, ordinary = load_shares(count, rows * top, bound, lean, True), load_shares(count, rows * top, bound, lean, False)
    places = jnp.arange(count)

    def named(sizes, turn):
        used = int((sizes > 0).sum())
        fixed = max(1, used // 4)
        moved = fixed + (places - fixed + turn * (used - fixed)) % max(1, count - fixed)
        return jnp.zeros((count,), jnp.int32).at[order[jnp.where(places < fixed, places, moved)]].set(jnp.asarray(sizes, jnp.int32))

    sizes = jnp.where(number % 4 == 0, named(crowded, number // 4), named(ordinary, number - number // 4 - 1))
    mixed = jax.random.permutation(jax.random.fold_in(own, 3), count)
    giver, sink = mixed[0:count // 2 * 2:2], mixed[1:count // 2 * 2:2]
    room = jnp.minimum(sizes[giver] - 1, bound - sizes[sink]) // 2
    room = jnp.where((giver == order[0]) | (sink == order[0]) | (sizes[sink] == 0), 0, jnp.maximum(room, 0))
    moved = jax.random.randint(jax.random.fold_in(own, 4), (count // 2,), 0, 1 << 20) % (room + 1)
    sizes = sizes.at[giver].add(-moved).at[sink].add(moved)
    members = jnp.searchsorted(jnp.cumsum(sizes), jnp.arange(rows * top), side="right").astype(jnp.int32)
    table = members.reshape(top, rows).T
    table = table[jax.random.permutation(jax.random.fold_in(own, 1), rows)]
    turn = jax.random.randint(jax.random.fold_in(own, 2), (rows, 1), 0, top)
    return jnp.take_along_axis(table, (jnp.arange(top)[None, :] + turn) % top, axis=1)


def load_shares(amount, total, reach, slope, full):
    portions = [(1 << 20) // math.isqrt(standing ** slope) + 1 for standing in range(1, amount + 1)]
    largest = reach if full else min(reach, max(-(-total // amount), total * portions[0] // sum(portions)))
    least = 1 if total - largest >= amount - 1 else 0
    holding, surplus = [largest] + [least] * (amount - 1), total - largest - least * (amount - 1)
    while surplus > 0:
        free = [i for i in range(1, amount) if holding[i] < largest] or [i for i in range(1, amount) if holding[i] < reach]
        whole, left = sum([portions[i] for i in free]), surplus
        for i in free:
            more = min(reach - holding[i], max(1, left * portions[i] // whole), surplus)
            holding[i] = holding[i] + more
            surplus = surplus - more
    return np.array(holding)


def noise(stream_key, dims, spread, most, shards=(), held_as=jnp.bfloat16):
    factor_of = level_of(stream_key, dims, shards, -0.22, 0.18) if shards else 1.0
    result = jax.random.normal(stream_key, dims, jnp.float32) * spread * factor_of
    return jnp.minimum(jnp.maximum(result, -most), most).astype(held_as)


def setup_inputs(seed: int = 0) -> dict:
    keys = jax.random.split(jax.random.key(seed), 10)
    history = noise(keys[0], (SEQS, LENGTH, D), 1.0, 6.0, ((0, 32), (1, 16)))
    ln_gain = jnp.clip(1.0 + 0.1 * jax.random.normal(keys[1], (D,), jnp.float32), 0.5, 1.5)
    w_in = noise(keys[2], (D, 4 * D), D ** -0.5, 0.25)
    w_out = noise(keys[3], (D, D), D ** -0.5, 0.25)
    item_table = noise(keys[4], (ROWS, D), 1.0, 6.0, ((0, 512),))
    sessions = jax.vmap(lambda own: jnp.searchsorted(jnp.cumsum(uneven_parts(own, SESSIONS, NBLK, MOST_BLK, 1)), jnp.arange(NBLK), side="right"))(jax.random.split(keys[5], SEQS)).reshape((SEQS, NBLK)).astype(jnp.int32)
    pos_owner_keys = jax.random.split(jax.random.fold_in(keys[6], 1), SEQS * LENGTH // TOK_DEV)
    pos_owner_turns = jax.random.permutation(jax.random.fold_in(keys[6], 3), SEQS * LENGTH // TOK_DEV)
    pos_owner = jax.vmap(lambda own, number: shared_out(jax.random.fold_in(keys[6], 2), own, number, TOK_DEV, OWNERS, 1, CAP, 2))(pos_owner_keys, pos_owner_turns).reshape((SEQS, LENGTH, 1))
    pos_row = place_ends(jax.random.randint(keys[7], (SEQS, LENGTH), 0, R_DEV), jax.random.fold_in(keys[7], 1), 0, R_DEV - 1).astype(jnp.int32)
    neg_rows = draw_neg_rows(jax.random.fold_in(keys[9], 71), 0)
    return dict(history=history, ln_gain=ln_gain, w_in=w_in, w_out=w_out, item_table=item_table, sessions=sessions, pos_owner=pos_owner, pos_row=pos_row, neg_rows=neg_rows)


TAU = 0.05

def silu_slope(value):
    sigma = jax.nn.sigmoid(value)
    return sigma * (1.0 + value * (1.0 - sigma))

def layer_stats(values):
    center = values - lax.optimization_barrier(jnp.mean(values, axis=-1, keepdims=True))
    scale_inv = lax.rsqrt(lax.optimization_barrier(jnp.mean(center * center, axis=-1, keepdims=True)) + 1e-05)
    return (center * scale_inv, scale_inv)

def norm_back(upstream, normed, scale_inv):
    return scale_inv * (upstream - lax.optimization_barrier(jnp.mean(upstream, axis=-1, keepdims=True)) - normed * lax.optimization_barrier(jnp.mean(upstream * normed, axis=-1, keepdims=True)))

def item_norm(rows_in):
    values = rows_in.astype(jnp.float32)
    lengths = jnp.sqrt(lax.optimization_barrier(jnp.sum(values * values, axis=-1, keepdims=True)) + 1e-06)
    return (values / lengths, lengths)

def sample_shift(neg_flat, levels, per_owner):
    powers = jnp.left_shift(jnp.ones((levels - 1,), jnp.int32), jnp.arange(1, levels, dtype=jnp.int32))
    exponent = lax.optimization_barrier(jnp.sum((neg_flat[:, None] + 1 >= powers[None, :]).astype(jnp.float32), axis=1))
    return math.log(levels) - math.log(per_owner) + exponent * math.log(2.0)

def split_heads(matrix):
    return matrix.astype(jnp.float32).reshape(matrix.shape[0], HEADS, -1)

def sequence_pass(history, session_ids, owner_ids, owner_rows, negative_rows, ln_gain, w_in, w_out, item_table):
    hist_f = history.astype(jnp.float32)
    normed_x, scale_x = layer_stats(hist_f)
    normed_in = (normed_x * ln_gain).astype(jnp.bfloat16)
    projected = jnp.dot(normed_in, w_in, preferred_element_type=jnp.float32)
    activated = jax.nn.silu(projected).astype(jnp.bfloat16)
    gate_u, value_v, query_q, key_k = jnp.split(activated, 4, axis=1)
    start_blk = lax.optimization_barrier(jnp.sum((session_ids[None, :] < session_ids[:, None]).astype(jnp.int32), axis=1))
    places = jnp.arange(LENGTH, dtype=jnp.int32)
    place_sess = jnp.repeat(session_ids, BLOCK)
    counts = (places - BLOCK * jnp.repeat(start_blk, BLOCK) + 1).astype(jnp.float32)
    inverse = 1.0 / counts
    lead = (MOST_BLK - 1) * BLOCK
    window = MOST_BLK * BLOCK
    key_pad = jnp.concatenate([jnp.zeros((lead, D), jnp.bfloat16), key_k])
    value_pad = jnp.concatenate([jnp.zeros((lead, D), jnp.bfloat16), value_v])
    sess_pad = jnp.concatenate([jnp.full((lead,), -1, jnp.int32), place_sess])
    score_scale = 1.0 / math.sqrt(D // HEADS)

    def pieces(index):
        first = index * BLOCK
        q_blk = lax.dynamic_slice_in_dim(query_q, first, BLOCK)
        k_win = lax.dynamic_slice_in_dim(key_pad, first, window)
        v_win = lax.dynamic_slice_in_dim(value_pad, first, window)
        s_win = lax.dynamic_slice_in_dim(sess_pad, first, window)
        q_sess = lax.dynamic_slice_in_dim(place_sess, first, BLOCK)
        q_place = first + jnp.arange(BLOCK, dtype=jnp.int32)
        k_place = first - lead + jnp.arange(window, dtype=jnp.int32)
        allowed = ((k_place[None, :] <= q_place[:, None]) & (s_win[None, :] == q_sess[:, None]) & (s_win[None, :] >= 0)).astype(jnp.float32)
        inv_blk = lax.dynamic_slice_in_dim(inverse, first, BLOCK)
        scores = jnp.einsum('qhd,khd->hqk', split_heads(q_blk), split_heads(k_win)) * score_scale
        return (q_blk, k_win, v_win, allowed, inv_blk, scores)

    def forward_block(index):
        q_blk, k_win, v_win, allowed, inv_blk, scores = pieces(index)
        weights = (jax.nn.silu(scores) * allowed * inv_blk[:, None]).astype(jnp.bfloat16)
        return jnp.einsum('hqk,khd->qhd', weights.astype(jnp.float32), split_heads(v_win)).reshape(BLOCK, D)
    attended = lax.map(forward_block, jnp.arange(NBLK, dtype=jnp.int32)).reshape(LENGTH, D)
    attn_hat, scale_a = layer_stats(attended)
    gated = (attn_hat * gate_u.astype(jnp.float32)).astype(jnp.bfloat16)
    user_out = jnp.dot(gated, w_out, preferred_element_type=jnp.float32) + hist_f
    user_len = jnp.sqrt(lax.optimization_barrier(jnp.sum(user_out * user_out, axis=-1, keepdims=True)) + 1e-06)
    user_unit = user_out / user_len
    user_bf = user_unit.astype(jnp.bfloat16)
    pos_ids = owner_ids * R_DEV + owner_rows
    neg_ids = (jnp.arange(OWNERS, dtype=jnp.int32)[:, None] * R_DEV + negative_rows).reshape(-1)
    pos_unit, pos_len = item_norm(item_table[pos_ids])
    neg_unit, neg_len = item_norm(item_table[neg_ids])
    pos_bf = pos_unit.astype(jnp.bfloat16)
    neg_bf = neg_unit.astype(jnp.bfloat16)
    levels = R_DEV.bit_length() - 1
    shift_terms = sample_shift(negative_rows.reshape(-1), levels, NEG_OWN)
    pos_logit = lax.optimization_barrier(jnp.sum(user_bf.astype(jnp.float32) * pos_bf.astype(jnp.float32), axis=-1)) / TAU
    neg_logit = jnp.dot(user_bf, neg_bf.T, preferred_element_type=jnp.float32) / TAU + shift_terms[None, :]
    pos_exp = jnp.exp(pos_logit)
    neg_exp = jnp.exp(neg_logit)
    denominator = pos_exp + lax.optimization_barrier(jnp.sum(neg_exp, axis=1))
    pos_delta = pos_exp / denominator - 1.0
    neg_prob = (neg_exp / denominator[:, None]).astype(jnp.bfloat16)
    unit_grad = (pos_delta[:, None] * pos_bf.astype(jnp.float32) + jnp.dot(neg_prob, neg_bf, preferred_element_type=jnp.float32)) / TAU
    user_grad = (unit_grad - user_unit * lax.optimization_barrier(jnp.sum(user_unit * unit_grad, axis=-1, keepdims=True))) / user_len
    raw_pos = pos_delta[:, None] * user_bf.astype(jnp.float32) / TAU
    pos_grad = (raw_pos - pos_unit * lax.optimization_barrier(jnp.sum(pos_unit * raw_pos, axis=-1, keepdims=True))) / pos_len
    raw_neg = jnp.dot(neg_prob.T, user_bf, preferred_element_type=jnp.float32) / TAU
    neg_grad = (raw_neg - neg_unit * lax.optimization_barrier(jnp.sum(neg_unit * raw_neg, axis=-1, keepdims=True))) / neg_len
    user_grad_bf = user_grad.astype(jnp.bfloat16)
    gated_grad = jnp.dot(user_grad_bf, w_out.T, preferred_element_type=jnp.float32)
    gate_grad = gated_grad * attn_hat
    hat_grad = gated_grad * gate_u.astype(jnp.float32)
    attended_grad = norm_back(hat_grad, attn_hat, scale_a).astype(jnp.bfloat16)

    def backward_block(carry, index):
        key_acc, value_acc = carry
        q_blk, k_win, v_win, allowed, inv_blk, scores = pieces(index)
        first = index * BLOCK
        g_blk = lax.dynamic_slice_in_dim(attended_grad, first, BLOCK)
        weights = (jax.nn.silu(scores) * allowed * inv_blk[:, None]).astype(jnp.bfloat16)
        weight_grad = jnp.einsum('qhd,khd->hqk', split_heads(g_blk), split_heads(v_win))
        score_grad = (weight_grad * silu_slope(scores) * allowed * inv_blk[:, None] * score_scale).astype(jnp.bfloat16)
        query_grad = jnp.einsum('hqk,khd->qhd', score_grad.astype(jnp.float32), split_heads(k_win)).reshape(BLOCK, D)
        key_grad = jnp.einsum('hqk,qhd->khd', score_grad.astype(jnp.float32), split_heads(q_blk)).reshape(window, D)
        value_grad = jnp.einsum('hqk,qhd->khd', weights.astype(jnp.float32), split_heads(g_blk)).reshape(window, D)
        key_acc = lax.dynamic_update_slice_in_dim(key_acc, lax.dynamic_slice_in_dim(key_acc, first, window) + key_grad, first, 0)
        value_acc = lax.dynamic_update_slice_in_dim(value_acc, lax.dynamic_slice_in_dim(value_acc, first, window) + value_grad, first, 0)
        return ((key_acc, value_acc), query_grad)
    zero_acc = jnp.zeros((lead + LENGTH, D), jnp.float32)
    (key_acc, value_acc), query_parts = lax.scan(backward_block, (zero_acc, zero_acc), jnp.arange(NBLK, dtype=jnp.int32))
    query_grad = query_parts.reshape(LENGTH, D)
    act_grad = jnp.concatenate([gate_grad, value_acc[lead:], query_grad, key_acc[lead:]], axis=1)
    proj_grad = (act_grad * silu_slope(projected)).astype(jnp.bfloat16)
    in_grad = jnp.dot(proj_grad, w_in.T, preferred_element_type=jnp.float32)
    history_grad = norm_back(in_grad * ln_gain, normed_x, scale_x) + user_grad
    return (history_grad.astype(jnp.bfloat16), pos_ids, pos_grad, neg_ids, neg_grad)

def reference(history, ln_gain, w_in, w_out, item_table, sessions, pos_owner, pos_row, neg_rows):

    def one_history(total, inputs):
        hist_seq, sess_seq, owner_seq, row_seq, neg_seq = inputs
        grad_seq, pos_ids, pos_grad, neg_ids, neg_grad = sequence_pass(hist_seq, sess_seq, owner_seq, row_seq, neg_seq, ln_gain, w_in, w_out, item_table)
        total = total.at[pos_ids].add(pos_grad).at[neg_ids].add(neg_grad)
        return (total, grad_seq)
    total, history_grad = lax.scan(one_history, jnp.zeros((ROWS, D), jnp.float32), (history, sessions, pos_owner[:, :, 0], pos_row, neg_rows))
    return (history_grad, total.astype(jnp.bfloat16))
```

```python
import math

import jax
import jax.numpy as jnp
from jax import lax
from jax.experimental import pallas as pl
from jax.experimental.pallas import tpu as pltpu
from jax.sharding import PartitionSpec as P

HEADS = 8
TAU = 0.05
CAP = 2
CHUNKS = 4
LANES = 128
SLOTS = CAP + 1
PIECES = 2
NBANK = SLOTS * CHUNKS
F32 = jnp.float32
BF16 = jnp.bfloat16
VMEM = pl.BlockSpec(memory_space=pltpu.VMEM)
HBM = pl.BlockSpec(memory_space=pltpu.HBM)
SMEM = pl.BlockSpec(memory_space=pltpu.SMEM)


def call(kernel, outs, in_specs, args, flops, scratch=(), mib=60, out_specs=None):
    moved = sum(a.size * a.dtype.itemsize for a in args) + sum(
        math.prod(o.shape) * o.dtype.itemsize for o in outs
    )
    pinned = [i for i, spec in enumerate(in_specs) if spec is None]
    scratch = list(scratch)

    def body(*refs):
        refs = list(refs)
        count = len(pinned)
        if not count:
            return kernel(*refs)
        held, sems = refs[-count - 1 : -1], refs[-1]
        refs = refs[: -count - 1]
        copies = []
        for j, i in enumerate(pinned):
            copies.append(pltpu.make_async_copy(refs[i], held[j], sems.at[j]))
            copies[-1].start()
            refs[i] = held[j]

        def loaded():
            for copy in copies:
                copy.wait()

        return kernel(loaded, *refs)

    if pinned:
        scratch += [pltpu.VMEM(args[i].shape, args[i].dtype) for i in pinned]
        scratch.append(pltpu.SemaphoreType.DMA((len(pinned),)))
    return pl.pallas_call(
        body,
        out_shape=tuple(outs),
        in_specs=[HBM if spec is None else spec for spec in in_specs],
        out_specs=out_specs or tuple(VMEM for _ in outs),
        scratch_shapes=scratch,
        compiler_params=pltpu.CompilerParams(vmem_limit_bytes=mib * 2**20),
        cost_estimate=pl.CostEstimate(flops=flops, bytes_accessed=moved, transcendentals=0),
    )(
        *[
            pltpu.with_memory_space_constraint(a, pltpu.HBM) if spec is None else a
            for a, spec in zip(args, in_specs)
        ]
    )


def shaped(shape, dtype):
    return jax.ShapeDtypeStruct(shape, dtype)


def dot(a, b, contract=(1, 0)):
    return lax.dot_general(
        a, b, (((contract[0],), (contract[1],)), ((), ())), preferred_element_type=F32
    )


def layer_stats(values):
    center = values - jnp.mean(values, axis=-1, keepdims=True)
    scale_inv = lax.rsqrt(jnp.mean(center * center, axis=-1, keepdims=True) + 1e-05)
    return center * scale_inv, scale_inv


def norm_back(upstream, normed, scale_inv):
    return scale_inv * (
        upstream
        - jnp.mean(upstream, axis=-1, keepdims=True)
        - normed * jnp.mean(upstream * normed, axis=-1, keepdims=True)
    )


def item_norm(rows_in):
    values = rows_in.astype(F32)
    lengths = jnp.sqrt(jnp.sum(values * values, axis=-1, keepdims=True) + 1e-06)
    return values / lengths, lengths


def sigmoid(value):
    return 1.0 / (1.0 + jnp.exp(-value))


def ask_kernel(owner_ref, row_ref, neg_ref, ask_ref, slot_row_ref, slot_col_ref):
    n = owner_ref.shape[1]
    owners = ask_ref.shape[0]
    lead = lax.broadcasted_iota(jnp.int32, (n, n), 0)
    lane = lax.broadcasted_iota(jnp.int32, (n, n), 1)

    def column(row):
        spread = jnp.broadcast_to(row.astype(F32), (n, n))
        return jnp.sum(jnp.where(lead == lane, spread, 0.0), axis=1, keepdims=True)

    owner_r = jnp.broadcast_to(owner_ref[...].astype(F32), (n, n))
    owner_c = column(owner_ref[...])
    same = owner_r == owner_c
    rank_r = jnp.sum(jnp.where(same & (lead < lane), 1.0, 0.0), axis=0, keepdims=True)
    rank_c = jnp.sum(jnp.where(same & (lane < lead), 1.0, 0.0), axis=1, keepdims=True)
    slot_r = owner_ref[...] * CAP + rank_r.astype(jnp.int32)
    slot_row_ref[...] = slot_r
    slot_col_ref[...] = (owner_c * CAP + rank_c).astype(jnp.int32)
    rows = jnp.broadcast_to(column(row_ref[...]), (n, LANES))
    by_owner = lax.broadcasted_iota(jnp.int32, (owners, n), 0) * CAP
    asked = None
    for k in range(CAP):
        hot = jnp.where(slot_r == by_owner + k, 1.0, 0.0).astype(BF16)
        part = dot(hot, jnp.where(lane == k, rows, 0.0).astype(BF16))
        asked = part if asked is None else asked + part
    for c in range(owners // n):
        negative = column(neg_ref[:, c * n : (c + 1) * n])
        ask_ref[c * n : (c + 1) * n, :] = jnp.where(
            lane == CAP, negative, asked[c * n : (c + 1) * n]
        ).astype(jnp.int32)


def spread_slot(wide, base, k, rows):
    for c in range(CHUNKS):
        wide[pl.ds(base + k * CHUNKS + c, rows.shape[0], stride=NBANK), :] = rows[
            :, c * LANES : (c + 1) * LANES
        ]


def slot_rows(wide, base, k, count):
    return jnp.concatenate(
        [wide[pl.ds(base + k * CHUNKS + c, count, stride=NBANK), :] for c in range(CHUNKS)], axis=1
    ).astype(BF16)


def piece(ref, i):
    size = ref.shape[0] // PIECES
    return ref.at[pl.ds(i * size, size), :]


def serve_kernel(asks_ref, table_ref, out_ref, wide, narrow, sems):
    owners = asks_ref.shape[0] // PIECES
    rows = table_ref.shape[0]
    table = table_ref[...]
    row_id = lax.broadcasted_iota(jnp.int32, (owners, rows), 1)
    copies = []
    for i in range(PIECES):
        base = i * owners * NBANK
        for k in range(SLOTS):
            asked = asks_ref[i * owners : (i + 1) * owners, k : k + 1]
            hot = jnp.where(asked == row_id, 1.0, 0.0).astype(BF16)
            spread_slot(wide, base, k, dot(hot, table))
        narrow[base : base + owners * NBANK, :] = wide[base : base + owners * NBANK, :].astype(BF16)
        copies.append(pltpu.make_async_copy(piece(narrow, i), piece(out_ref, i), sems.at[i]))
        copies[-1].start()
    for copy in copies:
        copy.wait()


def pair_masks(n):
    lane = lax.broadcasted_iota(jnp.int32, (n, LANES), 1)
    return lane < (LANES // 2)


def both_heads(part, low):
    zero = jnp.zeros_like(part)
    return jnp.concatenate([jnp.where(low, part, zero), jnp.where(low, zero, part)], axis=0)


def same_before(place_ref, sess_ref, ahead):
    block = place_ref[0] + ahead
    inside = block < sess_ref.shape[1]
    block = jnp.minimum(block, sess_ref.shape[1] - 1)
    here = sess_ref[0, block]
    near = inside & (block >= 1) & (sess_ref[0, jnp.maximum(block - 1, 0)] == here)
    far = inside & (block >= 2) & (sess_ref[0, jnp.maximum(block - 2, 0)] == here)
    return jnp.where(near, 1, 0), jnp.where(far, 1, 0)


def window_scale(place_ref, sess_ref, n):
    near, far = same_before(place_ref, sess_ref, 0)
    place = lax.broadcasted_iota(jnp.int32, (n, 3 * n), 0)
    lane = lax.broadcasted_iota(jnp.int32, (n, 3 * n), 1)
    count = place + 1 + n * (near + far)
    allowed = jnp.where(
        lane < n, far, jnp.where(lane < 2 * n, near, jnp.where(lane - 2 * n <= place, 1, 0))
    )
    scale = allowed.astype(F32) * (1.0 / count.astype(F32))
    return jnp.concatenate([scale, scale], axis=0)


def forward_kernel(
    place_ref,
    sess_ref,
    far_ref,
    near_ref,
    own_ref,
    gain_ref,
    w_in_ref,
    w_out_ref,
    unit_ref,
    length_ref,
    hat_ref,
    scale_ref,
    gate_ref,
    query_ref,
    slope_gq_ref,
    slope_vk_ref,
    keys_ref,
    values_ref,
):
    n, width = own_ref.shape
    gain = gain_ref[...]
    hist_f = own_ref[...].astype(F32)

    def normed_in(values):
        return (layer_stats(values)[0] * gain).astype(BF16)

    projected = dot(normed_in(hist_f), w_in_ref[...])
    sigma = sigmoid(projected)
    slope = sigma * (1.0 + projected * (1.0 - sigma))
    slope_gq_ref[:, :width] = slope[:, :width]
    slope_vk_ref[:, :width] = slope[:, width : 2 * width]
    slope_gq_ref[:, width:] = slope[:, 2 * width : 3 * width]
    slope_vk_ref[:, width:] = slope[:, 3 * width :]
    act = (projected * sigma).astype(BF16)
    gate_ref[...] = act[:, :width]
    query_ref[...] = act[:, 2 * width : 3 * width]
    before = jnp.concatenate(
        [normed_in(far_ref[...].astype(F32)), normed_in(near_ref[...].astype(F32))], axis=0
    )
    values_before = dot(before, w_in_ref[:, width : 2 * width])
    keys_before = dot(before, w_in_ref[:, 3 * width :])
    values_ref[: 2 * n, :] = (values_before * sigmoid(values_before)).astype(BF16)
    keys_ref[: 2 * n, :] = (keys_before * sigmoid(keys_before)).astype(BF16)
    values_ref[2 * n :, :] = act[:, width : 2 * width]
    keys_ref[2 * n :, :] = act[:, 3 * width :]
    scale = window_scale(place_ref, sess_ref, n)
    low = pair_masks(n)
    score_scale = 1.0 / math.sqrt(width // HEADS)
    attended = []
    for pair in range(HEADS // 2):
        lanes = slice(pair * LANES, (pair + 1) * LANES)
        queries = both_heads(act[:, 2 * width + pair * LANES : 2 * width + (pair + 1) * LANES], low)
        scores = dot(queries, keys_ref[:, lanes], (1, 1)) * score_scale
        weights = (scores * sigmoid(scores) * scale).astype(BF16)
        both = dot(weights, values_ref[:, lanes])
        attended.append(jnp.where(low, both[:n], both[n:]))
    attn_hat, scale_a = layer_stats(jnp.concatenate(attended, axis=1))
    hat_ref[...] = attn_hat
    scale_ref[...] = jnp.broadcast_to(scale_a, scale_ref.shape)
    gated = (attn_hat * act[:, :width].astype(F32)).astype(BF16)
    user_out = dot(gated, w_out_ref[...]) + hist_f
    user_len = jnp.sqrt(jnp.sum(user_out * user_out, axis=-1, keepdims=True) + 1e-06)
    unit_ref[...] = user_out / user_len
    length_ref[...] = jnp.broadcast_to(user_len, length_ref.shape)


def softmax_kernel(
    loaded,
    fetched_ref,
    neg_row_ref,
    slot_row_ref,
    slot_col_ref,
    unit_ref,
    length_ref,
    send_ref,
    user_grad_ref,
    narrow,
    wide,
    sems,
):
    n = unit_ref.shape[0]
    owners = neg_row_ref.shape[1] // PIECES
    wide[...] = fetched_ref[...].astype(F32)
    neg_units, neg_lens, neg_bfs = [], [], []
    for i in range(PIECES):
        unit, length = item_norm(slot_rows(wide, i * owners * NBANK, CAP, owners))
        neg_units.append(unit)
        neg_lens.append(length)
        neg_bfs.append(unit.astype(BF16))
    neg_bf = jnp.concatenate(neg_bfs, axis=0)
    loaded()
    user_unit = unit_ref[...]
    user_bf = user_unit.astype(BF16)
    user_f = user_bf.astype(F32)
    neg_row = neg_row_ref[...] + 1
    exponent = jnp.zeros(neg_row.shape, F32)
    for level in range(1, 8):
        exponent = exponent + jnp.where(neg_row >= (1 << level), 1.0, 0.0)
    shift = math.log(8) + exponent * math.log(2.0)
    neg_exp = jnp.exp(dot(user_bf, neg_bf, (1, 1)) / TAU + shift)
    slot_col = slot_col_ref[...]
    lane = lax.broadcasted_iota(jnp.int32, (n, owners), 1) * CAP
    hots, rows = [], []
    for i in range(PIECES):
        for k in range(CAP):
            hots.append(jnp.where(slot_col == lane + (i * owners * CAP + k), 1.0, 0.0).astype(BF16))
            rows.append(slot_rows(wide, i * owners * NBANK, k, owners))
    pos_rows = dot(jnp.concatenate(hots, axis=1), jnp.concatenate(rows, axis=0))
    pos_unit, pos_len = item_norm(pos_rows)
    pos_bf = pos_unit.astype(BF16).astype(F32)
    pos_exp = jnp.exp(jnp.sum(user_f * pos_bf, axis=-1, keepdims=True) / TAU)
    denominator = pos_exp + jnp.sum(neg_exp, axis=-1, keepdims=True)
    pos_delta = pos_exp / denominator - 1.0
    neg_prob = (neg_exp / denominator).astype(BF16)
    raw_pos = pos_delta * user_f / TAU
    pos_grad = (raw_pos - pos_unit * jnp.sum(pos_unit * raw_pos, axis=-1, keepdims=True)) / pos_len
    pos_grad = pos_grad.astype(BF16)
    slot_row = slot_row_ref[...]
    lead = lax.broadcasted_iota(jnp.int32, (owners, n), 0) * CAP
    copies = []
    for i in range(PIECES):
        base = i * owners * NBANK
        for k in range(CAP):
            hot = jnp.where(slot_row == lead + (i * owners * CAP + k), 1.0, 0.0).astype(BF16)
            spread_slot(wide, base, k, dot(hot, pos_grad))
        raw_neg = dot(neg_prob[:, i * owners : (i + 1) * owners], user_bf, (0, 0)) / TAU
        along = jnp.sum(neg_units[i] * raw_neg, axis=-1, keepdims=True)
        spread_slot(wide, base, CAP, (raw_neg - neg_units[i] * along) / neg_lens[i])
        narrow[base : base + owners * NBANK, :] = wide[base : base + owners * NBANK, :].astype(BF16)
        copies.append(pltpu.make_async_copy(piece(narrow, i), piece(send_ref, i), sems.at[i]))
        copies[-1].start()
    unit_grad = (pos_delta * pos_bf + dot(neg_prob, neg_bf)) / TAU
    user_grad_ref[...] = (
        unit_grad - user_unit * jnp.sum(user_unit * unit_grad, axis=-1, keepdims=True)
    ) / length_ref[:, 0:1]
    for copy in copies:
        copy.wait()


def heads_back_kernel(
    place_ref,
    sess_ref,
    user_grad_ref,
    w_out_ref,
    gate_ref,
    query_ref,
    hat_ref,
    scale_ref,
    keys_ref,
    values_ref,
    slope_ref,
    w_in_ref,
    own_ref,
    near_ref,
    far_ref,
    in_part_ref,
):
    n, width = hat_ref.shape
    attn_hat = hat_ref[...]
    gated_grad = dot(user_grad_ref[...].astype(BF16), w_out_ref[...], (1, 1))
    hat_grad = gated_grad * gate_ref[...].astype(F32)
    upstream = norm_back(hat_grad, attn_hat, scale_ref[:, 0:1]).astype(BF16)
    scale = window_scale(place_ref, sess_ref, n)
    low = pair_masks(n)
    score_scale = 1.0 / math.sqrt(width // HEADS)
    query_grads = []
    for pair in range(HEADS // 2):
        first = pair * LANES
        lanes = slice(first, first + LANES)
        later = slice(width + first, width + first + LANES)
        queries = both_heads(query_ref[:, lanes], low)
        grads = both_heads(upstream[:, lanes], low)
        keys = keys_ref[:, lanes]
        scores = dot(queries, keys, (1, 1)) * score_scale
        weight_grad = dot(grads, values_ref[:, lanes], (1, 1))
        sigma = sigmoid(scores)
        weights = (scores * sigma * scale).astype(BF16)
        slope = sigma * (1.0 + scores * (1.0 - sigma))
        score_grad = (weight_grad * slope * (scale * score_scale)).astype(BF16)
        both = dot(score_grad, keys)
        query_grads.append(jnp.where(low, both[:n], both[n:]))
        key_grad = dot(score_grad, queries, (0, 0))
        value_grad = dot(weights, grads, (0, 0))
        far_ref[:, lanes] = value_grad[:n].astype(BF16)
        near_ref[:, lanes] = value_grad[n : 2 * n].astype(BF16)
        own_ref[:, lanes] = value_grad[2 * n :]
        far_ref[:, later] = key_grad[:n].astype(BF16)
        near_ref[:, later] = key_grad[n : 2 * n].astype(BF16)
        own_ref[:, later] = key_grad[2 * n :]
    gate_part = (gated_grad * attn_hat * slope_ref[:, :width]).astype(BF16)
    query_part = (jnp.concatenate(query_grads, axis=1) * slope_ref[:, width:]).astype(BF16)
    in_part_ref[...] = dot(gate_part, w_in_ref[:, :width], (1, 1)) + dot(
        query_part, w_in_ref[:, 2 * width : 3 * width], (1, 1)
    )


def last_kernel(
    loaded,
    returned_ref,
    near_ref,
    far_ref,
    asks_ref,
    own_grad_ref,
    slope_ref,
    in_part_ref,
    w_in_ref,
    gain_ref,
    hist_ref,
    user_grad_ref,
    table_grad_ref,
    history_grad_ref,
    wide,
):
    width = hist_ref.shape[1]
    owners = asks_ref.shape[0] // PIECES
    rows = table_grad_ref.shape[0]
    wide[...] = returned_ref[...].astype(F32)
    loaded()
    asks = jnp.transpose(asks_ref[...].astype(F32))
    row_id = lax.broadcasted_iota(jnp.int32, (rows, owners), 0).astype(F32)
    total = None
    for i in range(PIECES):
        hots, parts = [], []
        for k in range(SLOTS):
            asked = asks[k : k + 1, i * owners : (i + 1) * owners]
            hots.append(jnp.where(asked == row_id, 1.0, 0.0).astype(BF16))
            parts.append(slot_rows(wide, i * owners * NBANK, k, owners))
        part = dot(jnp.concatenate(hots, axis=1), jnp.concatenate(parts, axis=0))
        total = part if total is None else total + part
    table_grad_ref[...] = total.astype(BF16)
    come = near_ref[...].astype(F32) + far_ref[...].astype(F32)
    proj_grad = ((own_grad_ref[...] + come) * slope_ref[...]).astype(BF16)
    in_grad = (
        in_part_ref[...]
        + dot(proj_grad[:, :width], w_in_ref[:, width : 2 * width], (1, 1))
        + dot(proj_grad[:, width:], w_in_ref[:, 3 * width :], (1, 1))
    )
    normed_x, scale_x = layer_stats(hist_ref[...].astype(F32))
    back = norm_back(in_grad * gain_ref[...], normed_x, scale_x)
    history_grad_ref[...] = (back + user_grad_ref[...]).astype(BF16)


def passed_along(shard, axis, by):
    count = lax.axis_size(axis)
    pairs = [(i, i + by) for i in range(count) if 0 <= i + by < count]
    return lax.ppermute(shard, axis, pairs)


def on_device(history, ln_gain, w_in, w_out, item_table, sessions, pos_owner, pos_row, neg_rows):
    n, width = history.shape[1:]
    items = lax.axis_size("items")
    hists = lax.axis_size("hist")
    owners = hists * items
    rows = item_table.shape[0]
    axes = ("hist", "items")
    place = jnp.stack([lax.axis_index("hist"), lax.axis_index("items")]).astype(jnp.int32)
    own = history[0]
    gain = ln_gain.reshape(1, width)
    neg_row = neg_rows.reshape(1, owners)

    def exchange(shard, chunk):
        shape = shard.shape
        split = shard.reshape((owners,) + chunk)
        return lax.all_to_all(split, axes, split_axis=0, concat_axis=0, tiled=True).reshape(shape)

    ask, slot_row, slot_col = call(
        ask_kernel,
        [shaped((owners, LANES), jnp.int32), shaped((1, n), jnp.int32), shaped((n, 1), jnp.int32)],
        [VMEM, VMEM, VMEM],
        (pos_owner.reshape(1, n), pos_row, neg_row),
        2 * CAP * owners * n * LANES,
    )
    asks = exchange(ask, (1, LANES))
    near = passed_along(own, "hist", 1)
    far = passed_along(own, "hist", 2)

    big = owners * NBANK
    staging = [
        pltpu.VMEM((big, LANES), BF16),
        pltpu.VMEM((big, LANES), F32),
        pltpu.SemaphoreType.DMA((PIECES,)),
    ]
    outward = [staging[1], staging[0], staging[2]]
    (served,) = call(
        serve_kernel,
        [shaped((big, LANES), BF16)],
        [VMEM, VMEM],
        (asks, item_table),
        2 * SLOTS * owners * rows * width,
        outward,
        out_specs=(HBM,),
    )
    fetched = exchange(served, (SLOTS, CHUNKS, LANES))

    unit, length, attn_hat, scale_a, gate, query, slope_gq, slope_vk, keys, values = call(
        forward_kernel,
        [
            shaped((n, width), F32),
            shaped((n, LANES), F32),
            shaped((n, width), F32),
            shaped((n, LANES), F32),
            shaped((n, width), BF16),
            shaped((n, width), BF16),
            shaped((n, 2 * width), F32),
            shaped((n, 2 * width), F32),
            shaped((3 * n, width), BF16),
            shaped((3 * n, width), BF16),
        ],
        [SMEM, SMEM] + [VMEM] * 6,
        (place, sessions, far, near, own, gain, w_in, w_out),
        2 * n * width * width * 12,
    )

    send, user_grad = call(
        softmax_kernel,
        [shaped((big, LANES), BF16), shaped((n, width), F32)],
        [VMEM] + [None] * 5,
        (fetched, neg_row, slot_row, slot_col, unit, length),
        2 * n * width * owners * 7,
        staging,
        mib=40,
        out_specs=(HBM, VMEM),
    )
    returned = exchange(send, (SLOTS, CHUNKS, LANES))

    own_grad, near_grad, far_grad, in_part = call(
        heads_back_kernel,
        [
            shaped((n, 2 * width), F32),
            shaped((n, 2 * width), BF16),
            shaped((n, 2 * width), BF16),
            shaped((n, width), F32),
        ],
        [SMEM, SMEM] + [VMEM] * 10,
        (
            place,
            sessions,
            user_grad,
            w_out,
            gate,
            query,
            attn_hat,
            scale_a,
            keys,
            values,
            slope_gq,
            w_in,
        ),
        2 * n * width * width * 12,
    )
    near_back = passed_along(near_grad, "hist", -1)
    far_back = passed_along(far_grad, "hist", -2)
    table_grad, history_grad = call(
        last_kernel,
        [shaped((rows, width), BF16), shaped((n, width), BF16)],
        [VMEM] * 3 + [None] * 8,
        (
            returned,
            near_back,
            far_back,
            asks,
            own_grad,
            slope_vk,
            in_part,
            w_in,
            gain,
            own,
            user_grad,
        ),
        2 * SLOTS * owners * rows * width,
        [staging[1]],
        mib=40,
    )
    return history_grad[None], table_grad


def solution(mesh):
    return jax.shard_map(
        on_device,
        mesh=mesh,
        in_specs=(
            P("items", "hist", None),
            P(),
            P(),
            P(),
            P(("hist", "items"), None),
            P("items", None),
            P("items", "hist", None),
            P("items", "hist"),
            P("items", None, None),
        ),
        out_specs=(P("items", "hist", None), P(("hist", "items"), None)),
        check_vma=False,
    )
```

```python
import math

import jax
import jax.numpy as jnp
from jax import lax
from jax.experimental import pallas as pl
from jax.experimental.pallas import tpu as pltpu
from jax.sharding import PartitionSpec as P

HEADS = 8
TAU = 0.05
CAP = 2
CHUNKS = 4
LANES = 128
SLOTS = CAP + 1
PIECES = 2
NBANK = SLOTS * CHUNKS
F32 = jnp.float32
BF16 = jnp.bfloat16
VMEM = pl.BlockSpec(memory_space=pltpu.VMEM)
HBM = pl.BlockSpec(memory_space=pltpu.HBM)
SMEM = pl.BlockSpec(memory_space=pltpu.SMEM)


def call(kernel, outs, in_specs, args, flops, scratch=(), mib=60, out_specs=None):
    moved = sum(a.size * a.dtype.itemsize for a in args) + sum(
        math.prod(o.shape) * o.dtype.itemsize for o in outs
    )
    pinned = [i for i, spec in enumerate(in_specs) if spec is None]
    scratch = list(scratch)

    def body(*refs):
        refs = list(refs)
        count = len(pinned)
        if not count:
            return kernel(*refs)
        held, sems = refs[-count - 1 : -1], refs[-1]
        refs = refs[: -count - 1]
        copies = []
        for j, i in enumerate(pinned):
            copies.append(pltpu.make_async_copy(refs[i], held[j], sems.at[j]))
            copies[-1].start()
            refs[i] = held[j]

        def loaded():
            for copy in copies:
                copy.wait()

        return kernel(loaded, *refs)

    if pinned:
        scratch += [pltpu.VMEM(args[i].shape, args[i].dtype) for i in pinned]
        scratch.append(pltpu.SemaphoreType.DMA((len(pinned),)))
    return pl.pallas_call(
        body,
        out_shape=tuple(outs),
        in_specs=[HBM if spec is None else spec for spec in in_specs],
        out_specs=out_specs or tuple(VMEM for _ in outs),
        scratch_shapes=scratch,
        compiler_params=pltpu.CompilerParams(vmem_limit_bytes=mib * 2**20),
        cost_estimate=pl.CostEstimate(flops=flops, bytes_accessed=moved, transcendentals=0),
    )(
        *[
            pltpu.with_memory_space_constraint(a, pltpu.HBM) if spec is None else a
            for a, spec in zip(args, in_specs)
        ]
    )


def shaped(shape, dtype):
    return jax.ShapeDtypeStruct(shape, dtype)


def dot(a, b, contract=(1, 0)):
    return lax.dot_general(
        a, b, (((contract[0],), (contract[1],)), ((), ())), preferred_element_type=F32
    )


def layer_stats(values):
    center = values - jnp.mean(values, axis=-1, keepdims=True)
    scale_inv = lax.rsqrt(jnp.mean(center * center, axis=-1, keepdims=True) + 1e-05)
    return center * scale_inv, scale_inv


def norm_back(upstream, normed, scale_inv):
    return scale_inv * (
        upstream
        - jnp.mean(upstream, axis=-1, keepdims=True)
        - normed * jnp.mean(upstream * normed, axis=-1, keepdims=True)
    )


def item_norm(rows_in):
    values = rows_in.astype(F32)
    lengths = jnp.sqrt(jnp.sum(values * values, axis=-1, keepdims=True) + 1e-06)
    return values / lengths, lengths


def sigmoid(value):
    return 1.0 / (1.0 + jnp.exp(-value))


def ask_kernel(owner_ref, row_ref, neg_ref, ask_ref, slot_row_ref, slot_col_ref):
    n = owner_ref.shape[1]
    owners = ask_ref.shape[0]
    lead = lax.broadcasted_iota(jnp.int32, (n, n), 0)
    lane = lax.broadcasted_iota(jnp.int32, (n, n), 1)

    def column(row):
        spread = jnp.broadcast_to(row.astype(F32), (n, n))
        return jnp.sum(jnp.where(lead == lane, spread, 0.0), axis=1, keepdims=True)

    owner_r = jnp.broadcast_to(owner_ref[...].astype(F32), (n, n))
    owner_c = column(owner_ref[...])
    same = owner_r == owner_c
    rank_r = jnp.sum(jnp.where(same & (lead < lane), 1.0, 0.0), axis=0, keepdims=True)
    rank_c = jnp.sum(jnp.where(same & (lane < lead), 1.0, 0.0), axis=1, keepdims=True)
    slot_r = owner_ref[...] * CAP + rank_r.astype(jnp.int32)
    slot_row_ref[...] = slot_r
    slot_col_ref[...] = (owner_c * CAP + rank_c).astype(jnp.int32)
    rows = jnp.broadcast_to(column(row_ref[...]), (n, LANES))
    by_owner = lax.broadcasted_iota(jnp.int32, (owners, n), 0) * CAP
    asked = None
    for k in range(CAP):
        hot = jnp.where(slot_r == by_owner + k, 1.0, 0.0).astype(BF16)
        part = dot(hot, jnp.where(lane == k, rows, 0.0).astype(BF16))
        asked = part if asked is None else asked + part
    for c in range(owners // n):
        negative = column(neg_ref[:, c * n : (c + 1) * n])
        ask_ref[c * n : (c + 1) * n, :] = jnp.where(
            lane == CAP, negative, asked[c * n : (c + 1) * n]
        ).astype(jnp.int32)


def spread_slot(wide, base, k, rows):
    for c in range(CHUNKS):
        wide[pl.ds(base + k * CHUNKS + c, rows.shape[0], stride=NBANK), :] = rows[
            :, c * LANES : (c + 1) * LANES
        ]


def slot_rows(wide, base, k, count):
    return jnp.concatenate(
        [wide[pl.ds(base + k * CHUNKS + c, count, stride=NBANK), :] for c in range(CHUNKS)], axis=1
    ).astype(BF16)


def piece(ref, i):
    size = ref.shape[0] // PIECES
    return ref.at[pl.ds(i * size, size), :]


def serve_kernel(asks_ref, table_ref, out_ref, wide, narrow, sems):
    owners = asks_ref.shape[0] // PIECES
    rows = table_ref.shape[0]
    table = table_ref[...]
    row_id = lax.broadcasted_iota(jnp.int32, (owners, rows), 1)
    copies = []
    for i in range(PIECES):
        base = i * owners * NBANK
        for k in range(SLOTS):
            asked = asks_ref[i * owners : (i + 1) * owners, k : k + 1]
            hot = jnp.where(asked == row_id, 1.0, 0.0).astype(BF16)
            spread_slot(wide, base, k, dot(hot, table))
        narrow[base : base + owners * NBANK, :] = wide[base : base + owners * NBANK, :].astype(BF16)
        copies.append(pltpu.make_async_copy(piece(narrow, i), piece(out_ref, i), sems.at[i]))
        copies[-1].start()
    for copy in copies:
        copy.wait()


def pair_masks(n):
    lane = lax.broadcasted_iota(jnp.int32, (n, LANES), 1)
    return lane < (LANES // 2)


def both_heads(part, low):
    zero = jnp.zeros_like(part)
    return jnp.concatenate([jnp.where(low, part, zero), jnp.where(low, zero, part)], axis=0)


def same_before(place_ref, sess_ref, ahead):
    block = place_ref[0] + ahead
    inside = block < sess_ref.shape[1]
    block = jnp.minimum(block, sess_ref.shape[1] - 1)
    here = sess_ref[0, block]
    near = inside & (block >= 1) & (sess_ref[0, jnp.maximum(block - 1, 0)] == here)
    far = inside & (block >= 2) & (sess_ref[0, jnp.maximum(block - 2, 0)] == here)
    return jnp.where(near, 1, 0), jnp.where(far, 1, 0)


def window_scale(place_ref, sess_ref, n):
    near, far = same_before(place_ref, sess_ref, 0)
    place = lax.broadcasted_iota(jnp.int32, (n, 3 * n), 0)
    lane = lax.broadcasted_iota(jnp.int32, (n, 3 * n), 1)
    count = place + 1 + n * (near + far)
    allowed = jnp.where(
        lane < n, far, jnp.where(lane < 2 * n, near, jnp.where(lane - 2 * n <= place, 1, 0))
    )
    scale = allowed.astype(F32) * (1.0 / count.astype(F32))
    return jnp.concatenate([scale, scale], axis=0)


def forward_kernel(
    place_ref,
    sess_ref,
    far_ref,
    near_ref,
    own_ref,
    gain_ref,
    w_in_ref,
    w_out_ref,
    unit_ref,
    length_ref,
    hat_ref,
    scale_ref,
    gate_ref,
    query_ref,
    slope_gq_ref,
    slope_vk_ref,
    keys_ref,
    values_ref,
):
    n, width = own_ref.shape
    gain = gain_ref[...]
    hist_f = own_ref[...].astype(F32)

    def normed_in(values):
        return (layer_stats(values)[0] * gain).astype(BF16)

    projected = dot(normed_in(hist_f), w_in_ref[...])
    sigma = sigmoid(projected)
    slope = sigma * (1.0 + projected * (1.0 - sigma))
    slope_gq_ref[:, :width] = slope[:, :width]
    slope_vk_ref[:, :width] = slope[:, width : 2 * width]
    slope_gq_ref[:, width:] = slope[:, 2 * width : 3 * width]
    slope_vk_ref[:, width:] = slope[:, 3 * width :]
    act = (projected * sigma).astype(BF16)
    gate_ref[...] = act[:, :width]
    query_ref[...] = act[:, 2 * width : 3 * width]
    before = jnp.concatenate(
        [normed_in(far_ref[...].astype(F32)), normed_in(near_ref[...].astype(F32))], axis=0
    )
    values_before = dot(before, w_in_ref[:, width : 2 * width])
    keys_before = dot(before, w_in_ref[:, 3 * width :])
    values_ref[: 2 * n, :] = (values_before * sigmoid(values_before)).astype(BF16)
    keys_ref[: 2 * n, :] = (keys_before * sigmoid(keys_before)).astype(BF16)
    values_ref[2 * n :, :] = act[:, width : 2 * width]
    keys_ref[2 * n :, :] = act[:, 3 * width :]
    scale = window_scale(place_ref, sess_ref, n)
    low = pair_masks(n)
    score_scale = 1.0 / math.sqrt(width // HEADS)
    attended = []
    for pair in range(HEADS // 2):
        lanes = slice(pair * LANES, (pair + 1) * LANES)
        queries = both_heads(act[:, 2 * width + pair * LANES : 2 * width + (pair + 1) * LANES], low)
        scores = dot(queries, keys_ref[:, lanes], (1, 1)) * score_scale
        weights = (scores * sigmoid(scores) * scale).astype(BF16)
        both = dot(weights, values_ref[:, lanes])
        attended.append(jnp.where(low, both[:n], both[n:]))
    attn_hat, scale_a = layer_stats(jnp.concatenate(attended, axis=1))
    hat_ref[...] = attn_hat
    scale_ref[...] = jnp.broadcast_to(scale_a, scale_ref.shape)
    gated = (attn_hat * act[:, :width].astype(F32)).astype(BF16)
    user_out = dot(gated, w_out_ref[...]) + hist_f
    user_len = jnp.sqrt(jnp.sum(user_out * user_out, axis=-1, keepdims=True) + 1e-06)
    unit_ref[...] = user_out / user_len
    length_ref[...] = jnp.broadcast_to(user_len, length_ref.shape)


def softmax_kernel(
    loaded,
    fetched_ref,
    neg_row_ref,
    slot_row_ref,
    slot_col_ref,
    unit_ref,
    length_ref,
    send_ref,
    user_grad_ref,
    narrow,
    wide,
    sems,
):
    n = unit_ref.shape[0]
    owners = neg_row_ref.shape[1] // PIECES
    wide[...] = fetched_ref[...].astype(F32)
    neg_units, neg_lens, neg_bfs = [], [], []
    for i in range(PIECES):
        unit, length = item_norm(slot_rows(wide, i * owners * NBANK, CAP, owners))
        neg_units.append(unit)
        neg_lens.append(length)
        neg_bfs.append(unit.astype(BF16))
    neg_bf = jnp.concatenate(neg_bfs, axis=0)
    loaded()
    user_unit = unit_ref[...]
    user_bf = user_unit.astype(BF16)
    user_f = user_bf.astype(F32)
    neg_row = neg_row_ref[...] + 1
    exponent = jnp.zeros(neg_row.shape, F32)
    for level in range(1, 8):
        exponent = exponent + jnp.where(neg_row >= (1 << level), 1.0, 0.0)
    shift = math.log(8) + exponent * math.log(2.0)
    neg_exp = jnp.exp(dot(user_bf, neg_bf, (1, 1)) / TAU + shift)
    slot_col = slot_col_ref[...]
    lane = lax.broadcasted_iota(jnp.int32, (n, owners), 1) * CAP
    hots, rows = [], []
    for i in range(PIECES):
        for k in range(CAP):
            hots.append(jnp.where(slot_col == lane + (i * owners * CAP + k), 1.0, 0.0).astype(BF16))
            rows.append(slot_rows(wide, i * owners * NBANK, k, owners))
    pos_rows = dot(jnp.concatenate(hots, axis=1), jnp.concatenate(rows, axis=0))
    pos_unit, pos_len = item_norm(pos_rows)
    pos_bf = pos_unit.astype(BF16).astype(F32)
    pos_exp = jnp.exp(jnp.sum(user_f * pos_bf, axis=-1, keepdims=True) / TAU)
    denominator = pos_exp + jnp.sum(neg_exp, axis=-1, keepdims=True)
    pos_delta = pos_exp / denominator - 1.0
    neg_prob = (neg_exp / denominator).astype(BF16)
    raw_pos = pos_delta * user_f / TAU
    pos_grad = (raw_pos - pos_unit * jnp.sum(pos_unit * raw_pos, axis=-1, keepdims=True)) / pos_len
    pos_grad = pos_grad.astype(BF16)
    slot_row = slot_row_ref[...]
    lead = lax.broadcasted_iota(jnp.int32, (owners, n), 0) * CAP
    copies = []
    for i in range(PIECES):
        base = i * owners * NBANK
        for k in range(CAP):
            hot = jnp.where(slot_row == lead + (i * owners * CAP + k), 1.0, 0.0).astype(BF16)
            spread_slot(wide, base, k, dot(hot, pos_grad))
        raw_neg = dot(neg_prob[:, i * owners : (i + 1) * owners], user_bf, (0, 0)) / TAU
        along = jnp.sum(neg_units[i] * raw_neg, axis=-1, keepdims=True)
        spread_slot(wide, base, CAP, (raw_neg - neg_units[i] * along) / neg_lens[i])
        narrow[base : base + owners * NBANK, :] = wide[base : base + owners * NBANK, :].astype(BF16)
        copies.append(pltpu.make_async_copy(piece(narrow, i), piece(send_ref, i), sems.at[i]))
        copies[-1].start()
    unit_grad = (pos_delta * pos_bf + dot(neg_prob, neg_bf)) / TAU
    user_grad_ref[...] = (
        unit_grad - user_unit * jnp.sum(user_unit * unit_grad, axis=-1, keepdims=True)
    ) / length_ref[:, 0:1]
    for copy in copies:
        copy.wait()


def heads_back_kernel(
    loaded,
    place_ref,
    sess_ref,
    user_grad_ref,
    w_out_ref,
    gate_ref,
    query_ref,
    hat_ref,
    scale_ref,
    keys_ref,
    values_ref,
    slope_ref,
    w_in_ref,
    own_ref,
    near_ref,
    far_ref,
    in_part_ref,
):
    n, width = hat_ref.shape
    loaded()
    attn_hat = hat_ref[...]
    gated_grad = dot(user_grad_ref[...].astype(BF16), w_out_ref[...], (1, 1))
    hat_grad = gated_grad * gate_ref[...].astype(F32)
    upstream = norm_back(hat_grad, attn_hat, scale_ref[:, 0:1]).astype(BF16)
    scale = window_scale(place_ref, sess_ref, n)
    low = pair_masks(n)
    score_scale = 1.0 / math.sqrt(width // HEADS)
    query_grads = []
    for pair in range(HEADS // 2):
        first = pair * LANES
        lanes = slice(first, first + LANES)
        later = slice(width + first, width + first + LANES)
        queries = both_heads(query_ref[:, lanes], low)
        grads = both_heads(upstream[:, lanes], low)
        keys = keys_ref[:, lanes]
        scores = dot(queries, keys, (1, 1)) * score_scale
        weight_grad = dot(grads, values_ref[:, lanes], (1, 1))
        sigma = sigmoid(scores)
        weights = (scores * sigma * scale).astype(BF16)
        slope = sigma * (1.0 + scores * (1.0 - sigma))
        score_grad = (weight_grad * slope * (scale * score_scale)).astype(BF16)
        both = dot(score_grad, keys)
        query_grads.append(jnp.where(low, both[:n], both[n:]))
        key_grad = dot(score_grad, queries, (0, 0))
        value_grad = dot(weights, grads, (0, 0))
        far_ref[:, lanes] = value_grad[:n].astype(BF16)
        near_ref[:, lanes] = value_grad[n : 2 * n].astype(BF16)
        own_ref[:, lanes] = value_grad[2 * n :]
        far_ref[:, later] = key_grad[:n].astype(BF16)
        near_ref[:, later] = key_grad[n : 2 * n].astype(BF16)
        own_ref[:, later] = key_grad[2 * n :]
    gate_part = (gated_grad * attn_hat * slope_ref[:, :width]).astype(BF16)
    query_part = (jnp.concatenate(query_grads, axis=1) * slope_ref[:, width:]).astype(BF16)
    in_part_ref[...] = dot(gate_part, w_in_ref[:, :width], (1, 1)) + dot(
        query_part, w_in_ref[:, 2 * width : 3 * width], (1, 1)
    )


def last_kernel(
    loaded,
    returned_ref,
    near_ref,
    far_ref,
    asks_ref,
    own_grad_ref,
    slope_ref,
    in_part_ref,
    w_in_ref,
    gain_ref,
    hist_ref,
    user_grad_ref,
    table_grad_ref,
    history_grad_ref,
    wide,
):
    width = hist_ref.shape[1]
    owners = asks_ref.shape[0] // PIECES
    rows = table_grad_ref.shape[0]
    wide[...] = returned_ref[...].astype(F32)
    loaded()
    asks = jnp.transpose(asks_ref[...].astype(F32))
    row_id = lax.broadcasted_iota(jnp.int32, (rows, owners), 0).astype(F32)
    total = None
    for i in range(PIECES):
        hots, parts = [], []
        for k in range(SLOTS):
            asked = asks[k : k + 1, i * owners : (i + 1) * owners]
            hots.append(jnp.where(asked == row_id, 1.0, 0.0).astype(BF16))
            parts.append(slot_rows(wide, i * owners * NBANK, k, owners))
        part = dot(jnp.concatenate(hots, axis=1), jnp.concatenate(parts, axis=0))
        total = part if total is None else total + part
    table_grad_ref[...] = total.astype(BF16)
    come = near_ref[...].astype(F32) + far_ref[...].astype(F32)
    proj_grad = ((own_grad_ref[...] + come) * slope_ref[...]).astype(BF16)
    in_grad = (
        in_part_ref[...]
        + dot(proj_grad[:, :width], w_in_ref[:, width : 2 * width], (1, 1))
        + dot(proj_grad[:, width:], w_in_ref[:, 3 * width :], (1, 1))
    )
    normed_x, scale_x = layer_stats(hist_ref[...].astype(F32))
    back = norm_back(in_grad * gain_ref[...], normed_x, scale_x)
    history_grad_ref[...] = (back + user_grad_ref[...]).astype(BF16)


def passed_along(shard, axis, by):
    count = lax.axis_size(axis)
    pairs = [(i, i + by) for i in range(count) if 0 <= i + by < count]
    return lax.ppermute(shard, axis, pairs)


def on_device(history, ln_gain, w_in, w_out, item_table, sessions, pos_owner, pos_row, neg_rows):
    n, width = history.shape[1:]
    items = lax.axis_size("items")
    hists = lax.axis_size("hist")
    owners = hists * items
    rows = item_table.shape[0]
    axes = ("hist", "items")
    place = jnp.stack([lax.axis_index("hist"), lax.axis_index("items")]).astype(jnp.int32)
    own = history[0]
    gain = ln_gain.reshape(1, width)
    neg_row = neg_rows.reshape(1, owners)

    def exchange(shard, chunk):
        shape = shard.shape
        split = shard.reshape((owners,) + chunk)
        return lax.all_to_all(split, axes, split_axis=0, concat_axis=0, tiled=True).reshape(shape)

    ask, slot_row, slot_col = call(
        ask_kernel,
        [shaped((owners, LANES), jnp.int32), shaped((1, n), jnp.int32), shaped((n, 1), jnp.int32)],
        [VMEM, VMEM, VMEM],
        (pos_owner.reshape(1, n), pos_row, neg_row),
        2 * CAP * owners * n * LANES,
    )
    asks = exchange(ask, (1, LANES))
    near = passed_along(own, "hist", 1)
    far = passed_along(own, "hist", 2)

    big = owners * NBANK
    staging = [
        pltpu.VMEM((big, LANES), BF16),
        pltpu.VMEM((big, LANES), F32),
        pltpu.SemaphoreType.DMA((PIECES,)),
    ]
    outward = [staging[1], staging[0], staging[2]]
    (served,) = call(
        serve_kernel,
        [shaped((big, LANES), BF16)],
        [VMEM, VMEM],
        (asks, item_table),
        2 * SLOTS * owners * rows * width,
        outward,
        out_specs=(HBM,),
    )
    served, near, far = lax.optimization_barrier((served, near, far))
    fetched = exchange(served, (SLOTS, CHUNKS, LANES))

    unit, length, attn_hat, scale_a, gate, query, slope_gq, slope_vk, keys, values = call(
        forward_kernel,
        [
            shaped((n, width), F32),
            shaped((n, LANES), F32),
            shaped((n, width), F32),
            shaped((n, LANES), F32),
            shaped((n, width), BF16),
            shaped((n, width), BF16),
            shaped((n, 2 * width), F32),
            shaped((n, 2 * width), F32),
            shaped((3 * n, width), BF16),
            shaped((3 * n, width), BF16),
        ],
        [SMEM, SMEM] + [VMEM] * 6,
        (place, sessions, far, near, own, gain, w_in, w_out),
        2 * n * width * width * 12,
    )

    send, user_grad = call(
        softmax_kernel,
        [shaped((big, LANES), BF16), pltpu.HBM((n, width), F32)],
        [VMEM] + [None] * 5,
        (fetched, neg_row, slot_row, slot_col, unit, length),
        2 * n * width * owners * 7,
        staging,
        mib=40,
        out_specs=(HBM, VMEM),
    )
    returned = exchange(send, (SLOTS, CHUNKS, LANES))

    own_grad, near_grad, far_grad, in_part = call(
        heads_back_kernel,
        [
            shaped((n, 2 * width), F32),
            shaped((n, 2 * width), BF16),
            shaped((n, 2 * width), BF16),
            shaped((n, width), F32),
        ],
        [SMEM, SMEM] + [None] * 10,
        (
            place,
            sessions,
            user_grad,
            w_out,
            gate,
            query,
            attn_hat,
            scale_a,
            keys,
            values,
            slope_gq,
            w_in,
        ),
        2 * n * width * width * 12,
    )
    near_back = passed_along(near_grad, "hist", -1)
    far_back = passed_along(far_grad, "hist", -2)
    table_grad, history_grad = call(
        last_kernel,
        [shaped((rows, width), BF16), shaped((n, width), BF16)],
        [VMEM] * 3 + [None] * 8,
        (
            returned,
            near_back,
            far_back,
            asks,
            own_grad,
            slope_vk,
            in_part,
            w_in,
            gain,
            own,
            user_grad,
        ),
        2 * SLOTS * owners * rows * width,
        [staging[1]],
        mib=40,
    )
    return history_grad[None], table_grad


def solution(mesh):
    return jax.shard_map(
        on_device,
        mesh=mesh,
        in_specs=(
            P("items", "hist", None),
            P(),
            P(),
            P(),
            P(("hist", "items"), None),
            P("items", None),
            P("items", "hist", None),
            P("items", "hist"),
            P("items", None, None),
        ),
        out_specs=(P("items", "hist", None), P(("hist", "items"), None)),
        check_vma=False,
    )
```

```python
import math

import jax
import jax.numpy as jnp
from jax import lax
from jax.experimental import pallas as pl
from jax.experimental.pallas import tpu as pltpu
from jax.sharding import PartitionSpec as P

HEADS = 8
TAU = 0.05
CAP = 2
CHUNKS = 4
LANES = 128
SLOTS = CAP + 1
PIECES = 4
NBANK = SLOTS * CHUNKS
F32 = jnp.float32
BF16 = jnp.bfloat16
VMEM = pl.BlockSpec(memory_space=pltpu.VMEM)
HBM = pl.BlockSpec(memory_space=pltpu.HBM)
SMEM = pl.BlockSpec(memory_space=pltpu.SMEM)


def call(kernel, outs, in_specs, args, flops, scratch=(), mib=60, out_specs=None):
    moved = sum(a.size * a.dtype.itemsize for a in args) + sum(
        math.prod(o.shape) * o.dtype.itemsize for o in outs
    )
    pinned = [i for i, spec in enumerate(in_specs) if spec is None]
    scratch = list(scratch)

    def body(*refs):
        refs = list(refs)
        count = len(pinned)
        if not count:
            return kernel(*refs)
        held, sems = refs[-count - 1 : -1], refs[-1]
        refs = refs[: -count - 1]
        copies = []
        for j, i in enumerate(pinned):
            copies.append(pltpu.make_async_copy(refs[i], held[j], sems.at[j]))
            copies[-1].start()
            refs[i] = held[j]

        waiting = list(copies)

        def loaded(count=len(copies)):
            for copy in waiting[:count]:
                copy.wait()
            del waiting[:count]

        return kernel(loaded, *refs)

    if pinned:
        scratch += [pltpu.VMEM(args[i].shape, args[i].dtype) for i in pinned]
        scratch.append(pltpu.SemaphoreType.DMA((len(pinned),)))
    return pl.pallas_call(
        body,
        out_shape=tuple(outs),
        in_specs=[HBM if spec is None else spec for spec in in_specs],
        out_specs=out_specs or tuple(VMEM for _ in outs),
        scratch_shapes=scratch,
        compiler_params=pltpu.CompilerParams(vmem_limit_bytes=mib * 2**20),
        cost_estimate=pl.CostEstimate(flops=flops, bytes_accessed=moved, transcendentals=0),
    )(
        *[
            pltpu.with_memory_space_constraint(a, pltpu.HBM) if spec is None else a
            for a, spec in zip(args, in_specs)
        ]
    )


def shaped(shape, dtype):
    return jax.ShapeDtypeStruct(shape, dtype)


def dot(a, b, contract=(1, 0)):
    return lax.dot_general(
        a, b, (((contract[0],), (contract[1],)), ((), ())), preferred_element_type=F32
    )


def layer_stats(values):
    center = values - jnp.mean(values, axis=-1, keepdims=True)
    scale_inv = lax.rsqrt(jnp.mean(center * center, axis=-1, keepdims=True) + 1e-05)
    return center * scale_inv, scale_inv


def norm_back(upstream, normed, scale_inv):
    return scale_inv * (
        upstream
        - jnp.mean(upstream, axis=-1, keepdims=True)
        - normed * jnp.mean(upstream * normed, axis=-1, keepdims=True)
    )


def item_norm(rows_in):
    values = rows_in.astype(F32)
    lengths = jnp.sqrt(jnp.sum(values * values, axis=-1, keepdims=True) + 1e-06)
    return values / lengths, lengths


def sigmoid(value):
    return 1.0 / (1.0 + jnp.exp(-value))


def ask_kernel(owner_ref, row_ref, neg_ref, ask_ref, slot_row_ref, slot_col_ref):
    n = owner_ref.shape[1]
    owners = ask_ref.shape[0]
    lead = lax.broadcasted_iota(jnp.int32, (n, n), 0)
    lane = lax.broadcasted_iota(jnp.int32, (n, n), 1)

    def column(row):
        spread = jnp.broadcast_to(row.astype(F32), (n, n))
        return jnp.sum(jnp.where(lead == lane, spread, 0.0), axis=1, keepdims=True)

    owner_r = jnp.broadcast_to(owner_ref[...].astype(F32), (n, n))
    owner_c = column(owner_ref[...])
    same = owner_r == owner_c
    rank_r = jnp.sum(jnp.where(same & (lead < lane), 1.0, 0.0), axis=0, keepdims=True)
    rank_c = jnp.sum(jnp.where(same & (lane < lead), 1.0, 0.0), axis=1, keepdims=True)
    slot_r = owner_ref[...] * CAP + rank_r.astype(jnp.int32)
    slot_row_ref[...] = slot_r
    slot_col_ref[...] = (owner_c * CAP + rank_c).astype(jnp.int32)
    rows = jnp.broadcast_to(column(row_ref[...]), (n, LANES))
    by_owner = lax.broadcasted_iota(jnp.int32, (owners, n), 0) * CAP
    asked = None
    for k in range(CAP):
        hot = jnp.where(slot_r == by_owner + k, 1.0, 0.0).astype(BF16)
        part = dot(hot, jnp.where(lane == k, rows, 0.0).astype(BF16))
        asked = part if asked is None else asked + part
    for c in range(owners // n):
        negative = column(neg_ref[:, c * n : (c + 1) * n])
        ask_ref[c * n : (c + 1) * n, :] = jnp.where(
            lane == CAP, negative, asked[c * n : (c + 1) * n]
        ).astype(jnp.int32)


def spread_slot(wide, base, k, rows):
    for c in range(CHUNKS):
        wide[pl.ds(base + k * CHUNKS + c, rows.shape[0], stride=NBANK), :] = rows[
            :, c * LANES : (c + 1) * LANES
        ]


def slot_rows(wide, base, k, count):
    return jnp.concatenate(
        [wide[pl.ds(base + k * CHUNKS + c, count, stride=NBANK), :] for c in range(CHUNKS)], axis=1
    ).astype(BF16)


def piece(ref, i):
    size = ref.shape[0] // PIECES
    return ref.at[pl.ds(i * size, size), :]


def serve_kernel(loaded, asks_ref, table_ref, out_ref, wide, narrow, sems):
    owners = asks_ref.shape[0] // PIECES
    rows = table_ref.shape[0]
    loaded()
    table = table_ref[...]
    row_id = lax.broadcasted_iota(jnp.int32, (owners, rows), 1)
    copies = []
    for i in range(PIECES):
        base = i * owners * NBANK
        for k in range(SLOTS):
            asked = asks_ref[i * owners : (i + 1) * owners, k : k + 1]
            hot = jnp.where(asked == row_id, 1.0, 0.0).astype(BF16)
            spread_slot(wide, base, k, dot(hot, table))
        narrow[base : base + owners * NBANK, :] = wide[base : base + owners * NBANK, :].astype(BF16)
        copies.append(pltpu.make_async_copy(piece(narrow, i), piece(out_ref, i), sems.at[i]))
        copies[-1].start()
    for copy in copies:
        copy.wait()


def pair_masks(n):
    lane = lax.broadcasted_iota(jnp.int32, (n, LANES), 1)
    return lane < (LANES // 2)


def both_heads(part, low):
    zero = jnp.zeros_like(part)
    return jnp.concatenate([jnp.where(low, part, zero), jnp.where(low, zero, part)], axis=0)


def same_before(place_ref, sess_ref, ahead):
    block = place_ref[0] + ahead
    inside = block < sess_ref.shape[1]
    block = jnp.minimum(block, sess_ref.shape[1] - 1)
    here = sess_ref[0, block]
    near = inside & (block >= 1) & (sess_ref[0, jnp.maximum(block - 1, 0)] == here)
    far = inside & (block >= 2) & (sess_ref[0, jnp.maximum(block - 2, 0)] == here)
    return jnp.where(near, 1, 0), jnp.where(far, 1, 0)


def window_scale(place_ref, sess_ref, n):
    near, far = same_before(place_ref, sess_ref, 0)
    place = lax.broadcasted_iota(jnp.int32, (n, 3 * n), 0)
    lane = lax.broadcasted_iota(jnp.int32, (n, 3 * n), 1)
    count = place + 1 + n * (near + far)
    allowed = jnp.where(
        lane < n, far, jnp.where(lane < 2 * n, near, jnp.where(lane - 2 * n <= place, 1, 0))
    )
    scale = allowed.astype(F32) * (1.0 / count.astype(F32))
    return jnp.concatenate([scale, scale], axis=0)


def forward_kernel(
    loaded,
    place_ref,
    sess_ref,
    far_ref,
    near_ref,
    own_ref,
    gain_ref,
    w_in_ref,
    w_out_ref,
    unit_ref,
    length_ref,
    hat_ref,
    scale_ref,
    gate_ref,
    query_ref,
    slope_gq_ref,
    slope_vk_ref,
    keys_ref,
    values_ref,
):
    n, width = own_ref.shape
    loaded()
    gain = gain_ref[...]
    hist_f = own_ref[...].astype(F32)

    def normed_in(values):
        return (layer_stats(values)[0] * gain).astype(BF16)

    projected = dot(normed_in(hist_f), w_in_ref[...])
    sigma = sigmoid(projected)
    slope = sigma * (1.0 + projected * (1.0 - sigma))
    slope_gq_ref[:, :width] = slope[:, :width]
    slope_vk_ref[:, :width] = slope[:, width : 2 * width]
    slope_gq_ref[:, width:] = slope[:, 2 * width : 3 * width]
    slope_vk_ref[:, width:] = slope[:, 3 * width :]
    act = (projected * sigma).astype(BF16)
    gate_ref[...] = act[:, :width]
    query_ref[...] = act[:, 2 * width : 3 * width]
    before = jnp.concatenate(
        [normed_in(far_ref[...].astype(F32)), normed_in(near_ref[...].astype(F32))], axis=0
    )
    values_before = dot(before, w_in_ref[:, width : 2 * width])
    keys_before = dot(before, w_in_ref[:, 3 * width :])
    values_ref[: 2 * n, :] = (values_before * sigmoid(values_before)).astype(BF16)
    keys_ref[: 2 * n, :] = (keys_before * sigmoid(keys_before)).astype(BF16)
    values_ref[2 * n :, :] = act[:, width : 2 * width]
    keys_ref[2 * n :, :] = act[:, 3 * width :]
    scale = window_scale(place_ref, sess_ref, n)
    low = pair_masks(n)
    score_scale = 1.0 / math.sqrt(width // HEADS)
    attended = []
    for pair in range(HEADS // 2):
        lanes = slice(pair * LANES, (pair + 1) * LANES)
        queries = both_heads(act[:, 2 * width + pair * LANES : 2 * width + (pair + 1) * LANES], low)
        scores = dot(queries, keys_ref[:, lanes], (1, 1)) * score_scale
        weights = (scores * sigmoid(scores) * scale).astype(BF16)
        both = dot(weights, values_ref[:, lanes])
        attended.append(jnp.where(low, both[:n], both[n:]))
    attn_hat, scale_a = layer_stats(jnp.concatenate(attended, axis=1))
    hat_ref[...] = attn_hat
    scale_ref[...] = jnp.broadcast_to(scale_a, scale_ref.shape)
    gated = (attn_hat * act[:, :width].astype(F32)).astype(BF16)
    user_out = dot(gated, w_out_ref[...]) + hist_f
    user_len = jnp.sqrt(jnp.sum(user_out * user_out, axis=-1, keepdims=True) + 1e-06)
    unit_ref[...] = user_out / user_len
    length_ref[...] = jnp.broadcast_to(user_len, length_ref.shape)


def softmax_kernel(
    loaded,
    fetched_ref,
    neg_row_ref,
    slot_row_ref,
    slot_col_ref,
    unit_ref,
    length_ref,
    send_ref,
    user_grad_ref,
    narrow,
    wide,
    sems,
    held,
    held_sem,
):
    n = unit_ref.shape[0]
    owners = neg_row_ref.shape[1]
    wide[...] = fetched_ref[...].astype(F32)
    neg_unit, neg_len = item_norm(slot_rows(wide, 0, CAP, owners))
    neg_bf = neg_unit.astype(BF16)
    loaded()
    user_unit = unit_ref[...]
    user_bf = user_unit.astype(BF16)
    user_f = user_bf.astype(F32)
    neg_row = neg_row_ref[...] + 1
    exponent = jnp.zeros(neg_row.shape, F32)
    for level in range(1, 8):
        exponent = exponent + jnp.where(neg_row >= (1 << level), 1.0, 0.0)
    shift = math.log(8) + exponent * math.log(2.0)
    neg_exp = jnp.exp(dot(user_bf, neg_bf, (1, 1)) / TAU + shift)
    slot_col = slot_col_ref[...]
    lane = lax.broadcasted_iota(jnp.int32, (n, owners), 1) * CAP
    hots, rows = [], []
    for k in range(CAP):
        hots.append(jnp.where(slot_col == lane + k, 1.0, 0.0).astype(BF16))
        rows.append(slot_rows(wide, 0, k, owners))
    pos_rows = dot(jnp.concatenate(hots, axis=1), jnp.concatenate(rows, axis=0))
    pos_unit, pos_len = item_norm(pos_rows)
    pos_bf = pos_unit.astype(BF16).astype(F32)
    pos_exp = jnp.exp(jnp.sum(user_f * pos_bf, axis=-1, keepdims=True) / TAU)
    denominator = pos_exp + jnp.sum(neg_exp, axis=-1, keepdims=True)
    pos_delta = pos_exp / denominator - 1.0
    neg_prob = (neg_exp / denominator).astype(BF16)
    unit_grad = (pos_delta * pos_bf + dot(neg_prob, neg_bf)) / TAU
    held[...] = (
        unit_grad - user_unit * jnp.sum(user_unit * unit_grad, axis=-1, keepdims=True)
    ) / length_ref[:, 0:1]
    copies = [pltpu.make_async_copy(held, user_grad_ref, held_sem)]
    copies[0].start()
    raw_pos = pos_delta * user_f / TAU
    pos_grad = (raw_pos - pos_unit * jnp.sum(pos_unit * raw_pos, axis=-1, keepdims=True)) / pos_len
    pos_grad = pos_grad.astype(BF16)
    slot_row = slot_row_ref[...]
    owners = owners // PIECES
    lead = lax.broadcasted_iota(jnp.int32, (owners, n), 0) * CAP
    for i in range(PIECES):
        base = i * owners * NBANK
        for k in range(CAP):
            hot = jnp.where(slot_row == lead + (i * owners * CAP + k), 1.0, 0.0).astype(BF16)
            spread_slot(wide, base, k, dot(hot, pos_grad))
        own = slice(i * owners, (i + 1) * owners)
        raw_neg = dot(neg_prob[:, own], user_bf, (0, 0)) / TAU
        along = jnp.sum(neg_unit[own] * raw_neg, axis=-1, keepdims=True)
        spread_slot(wide, base, CAP, (raw_neg - neg_unit[own] * along) / neg_len[own])
        narrow[base : base + owners * NBANK, :] = wide[base : base + owners * NBANK, :].astype(BF16)
        copies.append(pltpu.make_async_copy(piece(narrow, i), piece(send_ref, i), sems.at[i]))
        copies[-1].start()
    for copy in copies:
        copy.wait()


def heads_back_kernel(
    loaded,
    place_ref,
    sess_ref,
    user_grad_ref,
    w_out_ref,
    gate_ref,
    query_ref,
    hat_ref,
    scale_ref,
    keys_ref,
    values_ref,
    slope_ref,
    w_in_ref,
    own_ref,
    near_ref,
    far_ref,
    in_part_ref,
):
    n, width = hat_ref.shape
    loaded()
    attn_hat = hat_ref[...]
    gated_grad = dot(user_grad_ref[...].astype(BF16), w_out_ref[...], (1, 1))
    hat_grad = gated_grad * gate_ref[...].astype(F32)
    upstream = norm_back(hat_grad, attn_hat, scale_ref[:, 0:1]).astype(BF16)
    scale = window_scale(place_ref, sess_ref, n)
    low = pair_masks(n)
    score_scale = 1.0 / math.sqrt(width // HEADS)
    query_grads = []
    for pair in range(HEADS // 2):
        first = pair * LANES
        lanes = slice(first, first + LANES)
        later = slice(width + first, width + first + LANES)
        queries = both_heads(query_ref[:, lanes], low)
        grads = both_heads(upstream[:, lanes], low)
        keys = keys_ref[:, lanes]
        scores = dot(queries, keys, (1, 1)) * score_scale
        weight_grad = dot(grads, values_ref[:, lanes], (1, 1))
        sigma = sigmoid(scores)
        weights = (scores * sigma * scale).astype(BF16)
        slope = sigma * (1.0 + scores * (1.0 - sigma))
        score_grad = (weight_grad * slope * (scale * score_scale)).astype(BF16)
        both = dot(score_grad, keys)
        query_grads.append(jnp.where(low, both[:n], both[n:]))
        key_grad = dot(score_grad, queries, (0, 0))
        value_grad = dot(weights, grads, (0, 0))
        far_ref[:, lanes] = value_grad[:n].astype(BF16)
        near_ref[:, lanes] = value_grad[n : 2 * n].astype(BF16)
        own_ref[:, lanes] = value_grad[2 * n :]
        far_ref[:, later] = key_grad[:n].astype(BF16)
        near_ref[:, later] = key_grad[n : 2 * n].astype(BF16)
        own_ref[:, later] = key_grad[2 * n :]
    gate_part = (gated_grad * attn_hat * slope_ref[:, :width]).astype(BF16)
    query_part = (jnp.concatenate(query_grads, axis=1) * slope_ref[:, width:]).astype(BF16)
    in_part_ref[...] = dot(gate_part, w_in_ref[:, :width], (1, 1)) + dot(
        query_part, w_in_ref[:, 2 * width : 3 * width], (1, 1)
    )


def last_kernel(
    loaded,
    returned_ref,
    near_ref,
    far_ref,
    asks_ref,
    own_grad_ref,
    slope_ref,
    in_part_ref,
    w_in_ref,
    gain_ref,
    hist_ref,
    user_grad_ref,
    table_grad_ref,
    history_grad_ref,
    wide,
    held,
    held_sem,
):
    width = hist_ref.shape[1]
    owners = asks_ref.shape[0] // 2
    rows = table_grad_ref.shape[0]
    wide[...] = returned_ref[...].astype(F32)
    loaded(1)
    asks = jnp.transpose(asks_ref[...].astype(F32))
    row_id = lax.broadcasted_iota(jnp.int32, (rows, owners), 0).astype(F32)
    total = None
    for i in range(2):
        hots, parts = [], []
        for k in range(SLOTS):
            asked = asks[k : k + 1, i * owners : (i + 1) * owners]
            hots.append(jnp.where(asked == row_id, 1.0, 0.0).astype(BF16))
            parts.append(slot_rows(wide, i * owners * NBANK, k, owners))
        part = dot(jnp.concatenate(hots, axis=1), jnp.concatenate(parts, axis=0))
        total = part if total is None else total + part
    held[...] = total.astype(BF16)
    copy = pltpu.make_async_copy(held, table_grad_ref, held_sem)
    copy.start()
    loaded()
    come = near_ref[...].astype(F32) + far_ref[...].astype(F32)
    proj_grad = ((own_grad_ref[...] + come) * slope_ref[...]).astype(BF16)
    in_grad = (
        in_part_ref[...]
        + dot(proj_grad[:, :width], w_in_ref[:, width : 2 * width], (1, 1))
        + dot(proj_grad[:, width:], w_in_ref[:, 3 * width :], (1, 1))
    )
    normed_x, scale_x = layer_stats(hist_ref[...].astype(F32))
    back = norm_back(in_grad * gain_ref[...], normed_x, scale_x)
    history_grad_ref[...] = (back + user_grad_ref[...]).astype(BF16)
    copy.wait()


def passed_along(shard, axis, by):
    count = lax.axis_size(axis)
    pairs = [(i, i + by) for i in range(count) if 0 <= i + by < count]
    return lax.ppermute(shard, axis, pairs)


def on_device(history, ln_gain, w_in, w_out, item_table, sessions, pos_owner, pos_row, neg_rows):
    n, width = history.shape[1:]
    items = lax.axis_size("items")
    hists = lax.axis_size("hist")
    owners = hists * items
    rows = item_table.shape[0]
    axes = ("hist", "items")
    place = jnp.stack([lax.axis_index("hist"), lax.axis_index("items")]).astype(jnp.int32)
    own = history[0]
    gain = ln_gain.reshape(1, width)
    neg_row = neg_rows.reshape(1, owners)

    def exchange(shard, chunk):
        shape = shard.shape
        split = shard.reshape((owners,) + chunk)
        return lax.all_to_all(split, axes, split_axis=0, concat_axis=0, tiled=True).reshape(shape)

    ask, slot_row, slot_col = call(
        ask_kernel,
        [shaped((owners, LANES), jnp.int32), shaped((1, n), jnp.int32), shaped((n, 1), jnp.int32)],
        [VMEM, VMEM, VMEM],
        (pos_owner.reshape(1, n), pos_row, neg_row),
        2 * CAP * owners * n * LANES,
    )
    asks = exchange(ask, (1, LANES))
    near = passed_along(own, "hist", 1)
    far = passed_along(own, "hist", 2)

    big = owners * NBANK
    staging = [
        pltpu.VMEM((big, LANES), BF16),
        pltpu.VMEM((big, LANES), F32),
        pltpu.SemaphoreType.DMA((PIECES,)),
    ]
    outward = [staging[1], staging[0], staging[2]]
    (served,) = call(
        serve_kernel,
        [shaped((big, LANES), BF16)],
        [VMEM, None],
        (asks, item_table),
        2 * SLOTS * owners * rows * width,
        outward,
        mib=40,
        out_specs=(HBM,),
    )
    served, near, far = lax.optimization_barrier((served, near, far))
    fetched = exchange(served, (SLOTS, CHUNKS, LANES))

    unit, length, attn_hat, scale_a, gate, query, slope_gq, slope_vk, keys, values = call(
        forward_kernel,
        [
            pltpu.HBM((n, width), F32),
            pltpu.HBM((n, LANES), F32),
            pltpu.HBM((n, width), F32),
            pltpu.HBM((n, LANES), F32),
            pltpu.HBM((n, width), BF16),
            pltpu.HBM((n, width), BF16),
            pltpu.HBM((n, 2 * width), F32),
            pltpu.HBM((n, 2 * width), F32),
            pltpu.HBM((3 * n, width), BF16),
            pltpu.HBM((3 * n, width), BF16),
        ],
        [SMEM, SMEM, VMEM, VMEM] + [None] * 4,
        (place, sessions, far, near, own, gain, w_in, w_out),
        2 * n * width * width * 12,
        mib=40,
    )

    send, user_grad = call(
        softmax_kernel,
        [shaped((big, LANES), BF16), pltpu.HBM((n, width), F32)],
        [VMEM] + [None] * 5,
        (fetched, neg_row, slot_row, slot_col, unit, length),
        2 * n * width * owners * 7,
        staging + [pltpu.VMEM((n, width), F32), pltpu.SemaphoreType.DMA(())],
        mib=40,
        out_specs=(HBM, HBM),
    )
    returned = exchange(send, (SLOTS, CHUNKS, LANES))

    own_grad, near_grad, far_grad, in_part = call(
        heads_back_kernel,
        [
            shaped((n, 2 * width), F32),
            shaped((n, 2 * width), BF16),
            shaped((n, 2 * width), BF16),
            shaped((n, width), F32),
        ],
        [SMEM, SMEM] + [None] * 10,
        (
            place,
            sessions,
            user_grad,
            w_out,
            gate,
            query,
            attn_hat,
            scale_a,
            keys,
            values,
            slope_gq,
            w_in,
        ),
        2 * n * width * width * 12,
    )
    near_back = passed_along(near_grad, "hist", -1)
    far_back = passed_along(far_grad, "hist", -2)
    table_grad, history_grad = call(
        last_kernel,
        [shaped((rows, width), BF16), shaped((n, width), BF16)],
        [VMEM] * 3 + [None] * 8,
        (
            returned,
            near_back,
            far_back,
            asks,
            own_grad,
            slope_vk,
            in_part,
            w_in,
            gain,
            own,
            user_grad,
        ),
        2 * SLOTS * owners * rows * width,
        [staging[1], pltpu.VMEM((rows, width), BF16), pltpu.SemaphoreType.DMA(())],
        mib=40,
        out_specs=(HBM, VMEM),
    )
    return history_grad[None], table_grad


def solution(mesh):
    return jax.shard_map(
        on_device,
        mesh=mesh,
        in_specs=(
            P("items", "hist", None),
            P(),
            P(),
            P(),
            P(("hist", "items"), None),
            P("items", None),
            P("items", "hist", None),
            P("items", "hist"),
            P("items", None, None),
        ),
        out_specs=(P("items", "hist", None), P(("hist", "items"), None)),
        check_vma=False,
    )
```

```python
import functools
import math

import jax
import jax.numpy as jnp
from jax import lax
from jax.experimental import pallas as pl
from jax.experimental.pallas import tpu as pltpu
from jax.sharding import PartitionSpec as P

HEADS = 8
TAU = 0.05
CAP = 2
CHUNKS = 4
LANES = 128
SLOTS = CAP + 1
PIECES = 4
NBANK = SLOTS * CHUNKS
F32 = jnp.float32
BF16 = jnp.bfloat16
VMEM = pl.BlockSpec(memory_space=pltpu.VMEM)
HBM = pl.BlockSpec(memory_space=pltpu.HBM)
SMEM = pl.BlockSpec(memory_space=pltpu.SMEM)


def call(kernel, outs, in_specs, args, flops, scratch=(), mib=60, out_specs=None):
    moved = sum(a.size * a.dtype.itemsize for a in args) + sum(
        math.prod(o.shape) * o.dtype.itemsize for o in outs
    )
    pinned = [i for i, spec in enumerate(in_specs) if spec is None]
    scratch = list(scratch)

    def body(*refs):
        refs = list(refs)
        count = len(pinned)
        if not count:
            return kernel(*refs)
        held, sems = refs[-count - 1 : -1], refs[-1]
        refs = refs[: -count - 1]
        copies = []
        for j, i in enumerate(pinned):
            copies.append(pltpu.make_async_copy(refs[i], held[j], sems.at[j]))
            copies[-1].start()
            refs[i] = held[j]

        waiting = list(copies)

        def loaded(count=len(copies)):
            for copy in waiting[:count]:
                copy.wait()
            del waiting[:count]

        return kernel(loaded, *refs)

    if pinned:
        scratch += [pltpu.VMEM(args[i].shape, args[i].dtype) for i in pinned]
        scratch.append(pltpu.SemaphoreType.DMA((len(pinned),)))
    return pl.pallas_call(
        body,
        out_shape=tuple(outs),
        in_specs=[HBM if spec is None else spec for spec in in_specs],
        out_specs=out_specs or tuple(VMEM for _ in outs),
        scratch_shapes=scratch,
        compiler_params=pltpu.CompilerParams(vmem_limit_bytes=mib * 2**20),
        cost_estimate=pl.CostEstimate(flops=flops, bytes_accessed=moved, transcendentals=0),
    )(
        *[
            pltpu.with_memory_space_constraint(a, pltpu.HBM) if spec is None else a
            for a, spec in zip(args, in_specs)
        ]
    )


def shaped(shape, dtype):
    return jax.ShapeDtypeStruct(shape, dtype)


def dot(a, b, contract=(1, 0)):
    return lax.dot_general(
        a, b, (((contract[0],), (contract[1],)), ((), ())), preferred_element_type=F32
    )


def layer_stats(values):
    center = values - jnp.mean(values, axis=-1, keepdims=True)
    scale_inv = lax.rsqrt(jnp.mean(center * center, axis=-1, keepdims=True) + 1e-05)
    return center * scale_inv, scale_inv


def norm_back(upstream, normed, scale_inv):
    return scale_inv * (
        upstream
        - jnp.mean(upstream, axis=-1, keepdims=True)
        - normed * jnp.mean(upstream * normed, axis=-1, keepdims=True)
    )


def item_norm(rows_in):
    values = rows_in.astype(F32)
    lengths = jnp.sqrt(jnp.sum(values * values, axis=-1, keepdims=True) + 1e-06)
    return values / lengths, lengths


def sigmoid(value):
    return 1.0 / (1.0 + jnp.exp(-value))


def ask_kernel(
    items, hists, owner_ref, row_ref, neg_ref, ask_ref, slot_row_ref, slot_col_ref, neg_row_ref
):
    n = owner_ref.shape[1]
    owners = ask_ref.shape[0]
    item_bits, hist_bits = items.bit_length() - 1, hists.bit_length() - 1
    lead = lax.broadcasted_iota(jnp.int32, (n, n), 0)
    lane = lax.broadcasted_iota(jnp.int32, (n, n), 1)

    def column(row):
        spread = jnp.broadcast_to(row.astype(F32), (n, n))
        return jnp.sum(jnp.where(lead == lane, spread, 0.0), axis=1, keepdims=True)

    place = ((owner_ref[...] & (items - 1)) << hist_bits) + (owner_ref[...] >> item_bits)
    place_r = jnp.broadcast_to(place.astype(F32), (n, n))
    place_c = column(place)
    same = place_r == place_c
    rank_r = jnp.sum(jnp.where(same & (lead < lane), 1.0, 0.0), axis=0, keepdims=True)
    rank_c = jnp.sum(jnp.where(same & (lane < lead), 1.0, 0.0), axis=1, keepdims=True)
    slot_r = place * CAP + rank_r.astype(jnp.int32)
    slot_row_ref[...] = slot_r
    slot_col_ref[...] = (place_c * CAP + rank_c).astype(jnp.int32)
    rows = jnp.broadcast_to(column(row_ref[...]), (n, LANES))
    by_owner = lax.broadcasted_iota(jnp.int32, (owners, n), 0) * CAP
    asked = None
    for k in range(CAP):
        hot = jnp.where(slot_r == by_owner + k, 1.0, 0.0).astype(BF16)
        part = dot(hot, jnp.where(lane == k, rows, 0.0).astype(BF16))
        asked = part if asked is None else asked + part
    neg_all = jnp.broadcast_to(neg_ref[...].astype(F32), (n, owners))
    at = lax.broadcasted_iota(jnp.int32, (n, owners), 0)
    named = lax.broadcasted_iota(jnp.int32, (n, owners), 1)
    for c in range(owners // n):
        own = slice(c * n, (c + 1) * n)
        owner = (((at + c * n) & (hists - 1)) << item_bits) + ((at + c * n) >> hist_bits)
        negative = jnp.sum(jnp.where(owner == named, neg_all, 0.0), axis=1, keepdims=True)
        ask_ref[own, :] = jnp.where(lane == CAP, negative, asked[own]).astype(jnp.int32)
        neg_row_ref[:, own] = jnp.sum(
            jnp.where(lead == lane, negative, 0.0), axis=0, keepdims=True
        ).astype(jnp.int32)


def spread_slot(wide, base, k, rows):
    for c in range(CHUNKS):
        wide[pl.ds(base + k * CHUNKS + c, rows.shape[0], stride=NBANK), :] = rows[
            :, c * LANES : (c + 1) * LANES
        ]


def slot_rows(wide, base, k, count):
    return jnp.concatenate(
        [wide[pl.ds(base + k * CHUNKS + c, count, stride=NBANK), :] for c in range(CHUNKS)], axis=1
    ).astype(BF16)


def piece(ref, i):
    size = ref.shape[0] // PIECES
    return ref.at[pl.ds(i * size, size), :]


def serve_kernel(loaded, asks_ref, table_ref, out_ref, wide, narrow, sems):
    owners = asks_ref.shape[0] // PIECES
    rows = table_ref.shape[0]
    loaded()
    table = table_ref[...]
    row_id = lax.broadcasted_iota(jnp.int32, (owners, rows), 1)
    copies = []
    for i in range(PIECES):
        base = i * owners * NBANK
        for k in range(SLOTS):
            asked = asks_ref[i * owners : (i + 1) * owners, k : k + 1]
            hot = jnp.where(asked == row_id, 1.0, 0.0).astype(BF16)
            spread_slot(wide, base, k, dot(hot, table))
        narrow[base : base + owners * NBANK, :] = wide[base : base + owners * NBANK, :].astype(BF16)
        copies.append(pltpu.make_async_copy(piece(narrow, i), piece(out_ref, i), sems.at[i]))
        copies[-1].start()
    for copy in copies:
        copy.wait()


def pair_masks(n):
    lane = lax.broadcasted_iota(jnp.int32, (n, LANES), 1)
    return lane < (LANES // 2)


def both_heads(part, low):
    zero = jnp.zeros_like(part)
    return jnp.concatenate([jnp.where(low, part, zero), jnp.where(low, zero, part)], axis=0)


def same_before(place_ref, sess_ref, ahead):
    block = place_ref[0] + ahead
    inside = block < sess_ref.shape[1]
    block = jnp.minimum(block, sess_ref.shape[1] - 1)
    here = sess_ref[0, block]
    near = inside & (block >= 1) & (sess_ref[0, jnp.maximum(block - 1, 0)] == here)
    far = inside & (block >= 2) & (sess_ref[0, jnp.maximum(block - 2, 0)] == here)
    return jnp.where(near, 1, 0), jnp.where(far, 1, 0)


def window_scale(place_ref, sess_ref, n):
    near, far = same_before(place_ref, sess_ref, 0)
    place = lax.broadcasted_iota(jnp.int32, (n, 3 * n), 0)
    lane = lax.broadcasted_iota(jnp.int32, (n, 3 * n), 1)
    count = place + 1 + n * (near + far)
    allowed = jnp.where(
        lane < n, far, jnp.where(lane < 2 * n, near, jnp.where(lane - 2 * n <= place, 1, 0))
    )
    scale = allowed.astype(F32) * (1.0 / count.astype(F32))
    return jnp.concatenate([scale, scale], axis=0)


def forward_kernel(
    loaded,
    place_ref,
    sess_ref,
    far_ref,
    near_ref,
    own_ref,
    gain_ref,
    w_in_ref,
    w_out_ref,
    unit_ref,
    length_ref,
    hat_ref,
    scale_ref,
    gate_ref,
    query_ref,
    slope_gq_ref,
    slope_vk_ref,
    keys_ref,
    values_ref,
):
    n, width = own_ref.shape
    loaded()
    gain = gain_ref[...]
    hist_f = own_ref[...].astype(F32)

    def normed_in(values):
        return (layer_stats(values)[0] * gain).astype(BF16)

    projected = dot(normed_in(hist_f), w_in_ref[...])
    sigma = sigmoid(projected)
    slope = sigma * (1.0 + projected * (1.0 - sigma))
    slope_gq_ref[:, :width] = slope[:, :width]
    slope_vk_ref[:, :width] = slope[:, width : 2 * width]
    slope_gq_ref[:, width:] = slope[:, 2 * width : 3 * width]
    slope_vk_ref[:, width:] = slope[:, 3 * width :]
    act = (projected * sigma).astype(BF16)
    gate_ref[...] = act[:, :width]
    query_ref[...] = act[:, 2 * width : 3 * width]
    before = jnp.concatenate(
        [normed_in(far_ref[...].astype(F32)), normed_in(near_ref[...].astype(F32))], axis=0
    )
    values_before = dot(before, w_in_ref[:, width : 2 * width])
    keys_before = dot(before, w_in_ref[:, 3 * width :])
    values_ref[: 2 * n, :] = (values_before * sigmoid(values_before)).astype(BF16)
    keys_ref[: 2 * n, :] = (keys_before * sigmoid(keys_before)).astype(BF16)
    values_ref[2 * n :, :] = act[:, width : 2 * width]
    keys_ref[2 * n :, :] = act[:, 3 * width :]
    scale = window_scale(place_ref, sess_ref, n)
    low = pair_masks(n)
    score_scale = 1.0 / math.sqrt(width // HEADS)
    attended = []
    for pair in range(HEADS // 2):
        lanes = slice(pair * LANES, (pair + 1) * LANES)
        queries = both_heads(act[:, 2 * width + pair * LANES : 2 * width + (pair + 1) * LANES], low)
        scores = dot(queries, keys_ref[:, lanes], (1, 1)) * score_scale
        weights = (scores * sigmoid(scores) * scale).astype(BF16)
        both = dot(weights, values_ref[:, lanes])
        attended.append(jnp.where(low, both[:n], both[n:]))
    attn_hat, scale_a = layer_stats(jnp.concatenate(attended, axis=1))
    hat_ref[...] = attn_hat
    scale_ref[...] = jnp.broadcast_to(scale_a, scale_ref.shape)
    gated = (attn_hat * act[:, :width].astype(F32)).astype(BF16)
    user_out = dot(gated, w_out_ref[...]) + hist_f
    user_len = jnp.sqrt(jnp.sum(user_out * user_out, axis=-1, keepdims=True) + 1e-06)
    unit_ref[...] = user_out / user_len
    length_ref[...] = jnp.broadcast_to(user_len, length_ref.shape)


def softmax_kernel(
    loaded,
    fetched_ref,
    neg_row_ref,
    slot_row_ref,
    slot_col_ref,
    unit_ref,
    length_ref,
    send_ref,
    user_grad_ref,
    narrow,
    wide,
    sems,
    held,
    held_sem,
):
    n = unit_ref.shape[0]
    owners = neg_row_ref.shape[1]
    wide[...] = fetched_ref[...].astype(F32)
    neg_unit, neg_len = item_norm(slot_rows(wide, 0, CAP, owners))
    neg_bf = neg_unit.astype(BF16)
    loaded()
    user_unit = unit_ref[...]
    user_bf = user_unit.astype(BF16)
    user_f = user_bf.astype(F32)
    neg_row = neg_row_ref[...] + 1
    exponent = jnp.zeros(neg_row.shape, F32)
    for level in range(1, 8):
        exponent = exponent + jnp.where(neg_row >= (1 << level), 1.0, 0.0)
    shift = math.log(8) + exponent * math.log(2.0)
    neg_exp = jnp.exp(dot(user_bf, neg_bf, (1, 1)) / TAU + shift)
    slot_col = slot_col_ref[...]
    lane = lax.broadcasted_iota(jnp.int32, (n, owners), 1) * CAP
    hots, rows = [], []
    for k in range(CAP):
        hots.append(jnp.where(slot_col == lane + k, 1.0, 0.0).astype(BF16))
        rows.append(slot_rows(wide, 0, k, owners))
    pos_rows = dot(jnp.concatenate(hots, axis=1), jnp.concatenate(rows, axis=0))
    pos_unit, pos_len = item_norm(pos_rows)
    pos_bf = pos_unit.astype(BF16).astype(F32)
    pos_exp = jnp.exp(jnp.sum(user_f * pos_bf, axis=-1, keepdims=True) / TAU)
    denominator = pos_exp + jnp.sum(neg_exp, axis=-1, keepdims=True)
    pos_delta = pos_exp / denominator - 1.0
    neg_prob = (neg_exp / denominator).astype(BF16)
    unit_grad = (pos_delta * pos_bf + dot(neg_prob, neg_bf)) / TAU
    held[...] = (
        unit_grad - user_unit * jnp.sum(user_unit * unit_grad, axis=-1, keepdims=True)
    ) / length_ref[:, 0:1]
    copies = [pltpu.make_async_copy(held, user_grad_ref, held_sem)]
    copies[0].start()
    raw_pos = pos_delta * user_f / TAU
    pos_grad = (raw_pos - pos_unit * jnp.sum(pos_unit * raw_pos, axis=-1, keepdims=True)) / pos_len
    pos_grad = pos_grad.astype(BF16)
    slot_row = slot_row_ref[...]
    owners = owners // PIECES
    lead = lax.broadcasted_iota(jnp.int32, (owners, n), 0) * CAP
    for i in range(PIECES):
        base = i * owners * NBANK
        for k in range(CAP):
            hot = jnp.where(slot_row == lead + (i * owners * CAP + k), 1.0, 0.0).astype(BF16)
            spread_slot(wide, base, k, dot(hot, pos_grad))
        own = slice(i * owners, (i + 1) * owners)
        raw_neg = dot(neg_prob[:, own], user_bf, (0, 0)) / TAU
        along = jnp.sum(neg_unit[own] * raw_neg, axis=-1, keepdims=True)
        spread_slot(wide, base, CAP, (raw_neg - neg_unit[own] * along) / neg_len[own])
        narrow[base : base + owners * NBANK, :] = wide[base : base + owners * NBANK, :].astype(BF16)
        copies.append(pltpu.make_async_copy(piece(narrow, i), piece(send_ref, i), sems.at[i]))
        copies[-1].start()
    for copy in copies:
        copy.wait()


def heads_back_kernel(
    loaded,
    place_ref,
    sess_ref,
    user_grad_ref,
    w_out_ref,
    gate_ref,
    query_ref,
    hat_ref,
    scale_ref,
    keys_ref,
    values_ref,
    slope_ref,
    w_in_ref,
    own_ref,
    near_ref,
    far_ref,
    in_part_ref,
):
    n, width = hat_ref.shape
    loaded()
    attn_hat = hat_ref[...]
    gated_grad = dot(user_grad_ref[...].astype(BF16), w_out_ref[...], (1, 1))
    hat_grad = gated_grad * gate_ref[...].astype(F32)
    upstream = norm_back(hat_grad, attn_hat, scale_ref[:, 0:1]).astype(BF16)
    scale = window_scale(place_ref, sess_ref, n)
    low = pair_masks(n)
    score_scale = 1.0 / math.sqrt(width // HEADS)
    query_grads = []
    for pair in range(HEADS // 2):
        first = pair * LANES
        lanes = slice(first, first + LANES)
        later = slice(width + first, width + first + LANES)
        queries = both_heads(query_ref[:, lanes], low)
        grads = both_heads(upstream[:, lanes], low)
        keys = keys_ref[:, lanes]
        scores = dot(queries, keys, (1, 1)) * score_scale
        weight_grad = dot(grads, values_ref[:, lanes], (1, 1))
        sigma = sigmoid(scores)
        weights = (scores * sigma * scale).astype(BF16)
        slope = sigma * (1.0 + scores * (1.0 - sigma))
        score_grad = (weight_grad * slope * (scale * score_scale)).astype(BF16)
        both = dot(score_grad, keys)
        query_grads.append(jnp.where(low, both[:n], both[n:]))
        key_grad = dot(score_grad, queries, (0, 0))
        value_grad = dot(weights, grads, (0, 0))
        far_ref[:, lanes] = value_grad[:n].astype(BF16)
        near_ref[:, lanes] = value_grad[n : 2 * n].astype(BF16)
        own_ref[:, lanes] = value_grad[2 * n :]
        far_ref[:, later] = key_grad[:n].astype(BF16)
        near_ref[:, later] = key_grad[n : 2 * n].astype(BF16)
        own_ref[:, later] = key_grad[2 * n :]
    gate_part = (gated_grad * attn_hat * slope_ref[:, :width]).astype(BF16)
    query_part = (jnp.concatenate(query_grads, axis=1) * slope_ref[:, width:]).astype(BF16)
    in_part_ref[...] = dot(gate_part, w_in_ref[:, :width], (1, 1)) + dot(
        query_part, w_in_ref[:, 2 * width : 3 * width], (1, 1)
    )


def last_kernel(
    loaded,
    returned_ref,
    near_ref,
    far_ref,
    asks_ref,
    own_grad_ref,
    slope_ref,
    in_part_ref,
    w_in_ref,
    gain_ref,
    hist_ref,
    user_grad_ref,
    table_grad_ref,
    history_grad_ref,
    wide,
    held,
    held_sem,
):
    width = hist_ref.shape[1]
    owners = asks_ref.shape[0] // 2
    rows = table_grad_ref.shape[0]
    wide[...] = returned_ref[...].astype(F32)
    loaded(1)
    asks = jnp.transpose(asks_ref[...].astype(F32))
    row_id = lax.broadcasted_iota(jnp.int32, (rows, owners), 0).astype(F32)
    total = None
    for i in range(2):
        hots, parts = [], []
        for k in range(SLOTS):
            asked = asks[k : k + 1, i * owners : (i + 1) * owners]
            hots.append(jnp.where(asked == row_id, 1.0, 0.0).astype(BF16))
            parts.append(slot_rows(wide, i * owners * NBANK, k, owners))
        part = dot(jnp.concatenate(hots, axis=1), jnp.concatenate(parts, axis=0))
        total = part if total is None else total + part
    held[...] = total.astype(BF16)
    copy = pltpu.make_async_copy(held, table_grad_ref, held_sem)
    copy.start()
    loaded()
    come = near_ref[...].astype(F32) + far_ref[...].astype(F32)
    proj_grad = ((own_grad_ref[...] + come) * slope_ref[...]).astype(BF16)
    in_grad = (
        in_part_ref[...]
        + dot(proj_grad[:, :width], w_in_ref[:, width : 2 * width], (1, 1))
        + dot(proj_grad[:, width:], w_in_ref[:, 3 * width :], (1, 1))
    )
    normed_x, scale_x = layer_stats(hist_ref[...].astype(F32))
    back = norm_back(in_grad * gain_ref[...], normed_x, scale_x)
    history_grad_ref[...] = (back + user_grad_ref[...]).astype(BF16)
    copy.wait()


def passed_along(shard, axis, by):
    count = lax.axis_size(axis)
    pairs = [(i, i + by) for i in range(count) if 0 <= i + by < count]
    return lax.ppermute(shard, axis, pairs)


def on_device(history, ln_gain, w_in, w_out, item_table, sessions, pos_owner, pos_row, neg_rows):
    n, width = history.shape[1:]
    items = lax.axis_size("items")
    hists = lax.axis_size("hist")
    owners = hists * items
    rows = item_table.shape[0]
    axes = ("items", "hist")
    place = jnp.stack([lax.axis_index("hist"), lax.axis_index("items")]).astype(jnp.int32)
    own = history[0]
    gain = ln_gain.reshape(1, width)
    neg_row = neg_rows.reshape(1, owners)

    def exchange(shard, chunk):
        shape = shard.shape
        split = shard.reshape((owners,) + chunk)
        return lax.all_to_all(split, axes, split_axis=0, concat_axis=0, tiled=True).reshape(shape)

    ask, slot_row, slot_col, neg_row = call(
        functools.partial(ask_kernel, items, hists),
        [
            shaped((owners, LANES), jnp.int32),
            shaped((1, n), jnp.int32),
            shaped((n, 1), jnp.int32),
            shaped((1, owners), jnp.int32),
        ],
        [VMEM, VMEM, VMEM],
        (pos_owner.reshape(1, n), pos_row, neg_row),
        2 * CAP * owners * n * LANES,
    )
    asks = exchange(ask, (1, LANES))
    near = passed_along(own, "hist", 1)
    far = passed_along(own, "hist", 2)

    big = owners * NBANK
    staging = [
        pltpu.VMEM((big, LANES), BF16),
        pltpu.VMEM((big, LANES), F32),
        pltpu.SemaphoreType.DMA((PIECES,)),
    ]
    outward = [staging[1], staging[0], staging[2]]
    (served,) = call(
        serve_kernel,
        [shaped((big, LANES), BF16)],
        [VMEM, None],
        (asks, item_table),
        2 * SLOTS * owners * rows * width,
        outward,
        mib=40,
        out_specs=(HBM,),
    )
    served, near, far = lax.optimization_barrier((served, near, far))
    fetched = exchange(served, (SLOTS, CHUNKS, LANES))

    unit, length, attn_hat, scale_a, gate, query, slope_gq, slope_vk, keys, values = call(
        forward_kernel,
        [
            pltpu.HBM((n, width), F32),
            pltpu.HBM((n, LANES), F32),
            pltpu.HBM((n, width), F32),
            pltpu.HBM((n, LANES), F32),
            pltpu.HBM((n, width), BF16),
            pltpu.HBM((n, width), BF16),
            pltpu.HBM((n, 2 * width), F32),
            pltpu.HBM((n, 2 * width), F32),
            pltpu.HBM((3 * n, width), BF16),
            pltpu.HBM((3 * n, width), BF16),
        ],
        [SMEM, SMEM, VMEM, VMEM] + [None] * 4,
        (place, sessions, far, near, own, gain, w_in, w_out),
        2 * n * width * width * 12,
        mib=40,
    )

    send, user_grad = call(
        softmax_kernel,
        [shaped((big, LANES), BF16), pltpu.HBM((n, width), F32)],
        [VMEM] + [None] * 5,
        (fetched, neg_row, slot_row, slot_col, unit, length),
        2 * n * width * owners * 7,
        staging + [pltpu.VMEM((n, width), F32), pltpu.SemaphoreType.DMA(())],
        mib=40,
        out_specs=(HBM, HBM),
    )
    returned = exchange(send, (SLOTS, CHUNKS, LANES))

    own_grad, near_grad, far_grad, in_part = call(
        heads_back_kernel,
        [
            shaped((n, 2 * width), F32),
            shaped((n, 2 * width), BF16),
            shaped((n, 2 * width), BF16),
            shaped((n, width), F32),
        ],
        [SMEM, SMEM] + [None] * 10,
        (
            place,
            sessions,
            user_grad,
            w_out,
            gate,
            query,
            attn_hat,
            scale_a,
            keys,
            values,
            slope_gq,
            w_in,
        ),
        2 * n * width * width * 12,
    )
    near_back = passed_along(near_grad, "hist", -1)
    far_back = passed_along(far_grad, "hist", -2)
    table_grad, history_grad = call(
        last_kernel,
        [shaped((rows, width), BF16), shaped((n, width), BF16)],
        [VMEM] * 3 + [None] * 8,
        (
            returned,
            near_back,
            far_back,
            asks,
            own_grad,
            slope_vk,
            in_part,
            w_in,
            gain,
            own,
            user_grad,
        ),
        2 * SLOTS * owners * rows * width,
        [staging[1], pltpu.VMEM((rows, width), BF16), pltpu.SemaphoreType.DMA(())],
        mib=40,
        out_specs=(HBM, VMEM),
    )
    return history_grad[None], table_grad


def solution(mesh):
    return jax.shard_map(
        on_device,
        mesh=mesh,
        in_specs=(
            P("items", "hist", None),
            P(),
            P(),
            P(),
            P(("hist", "items"), None),
            P("items", None),
            P("items", "hist", None),
            P("items", "hist"),
            P("items", None, None),
        ),
        out_specs=(P("items", "hist", None), P(("hist", "items"), None)),
        check_vma=False,
    )
```

```python
import functools
import math

import jax
import jax.numpy as jnp
from jax import lax
from jax.experimental import pallas as pl
from jax.experimental.pallas import tpu as pltpu
from jax.sharding import PartitionSpec as P

HEADS = 8
TAU = 0.05
CAP = 2
CHUNKS = 4
LANES = 128
SLOTS = CAP + 1
SEATS = 2 * CAP + 1
PIECES = 2
NBANK = SEATS * CHUNKS
F32 = jnp.float32
BF16 = jnp.bfloat16
VMEM = pl.BlockSpec(memory_space=pltpu.VMEM)
HBM = pl.BlockSpec(memory_space=pltpu.HBM)
SMEM = pl.BlockSpec(memory_space=pltpu.SMEM)


def call(kernel, outs, in_specs, args, flops, scratch=(), mib=60, out_specs=None):
    moved = sum(a.size * a.dtype.itemsize for a in args) + sum(
        math.prod(o.shape) * o.dtype.itemsize for o in outs
    )
    pinned = [i for i, spec in enumerate(in_specs) if spec is None]
    scratch = list(scratch)

    def body(*refs):
        refs = list(refs)
        count = len(pinned)
        if not count:
            return kernel(*refs)
        held, sems = refs[-count - 1 : -1], refs[-1]
        refs = refs[: -count - 1]
        copies = []
        for j, i in enumerate(pinned):
            copies.append(pltpu.make_async_copy(refs[i], held[j], sems.at[j]))
            copies[-1].start()
            refs[i] = held[j]

        waiting = list(copies)

        def loaded(count=len(copies)):
            for copy in waiting[:count]:
                copy.wait()
            del waiting[:count]

        return kernel(loaded, *refs)

    if pinned:
        scratch += [pltpu.VMEM(args[i].shape, args[i].dtype) for i in pinned]
        scratch.append(pltpu.SemaphoreType.DMA((len(pinned),)))
    return pl.pallas_call(
        body,
        out_shape=tuple(outs),
        in_specs=[HBM if spec is None else spec for spec in in_specs],
        out_specs=out_specs or tuple(VMEM for _ in outs),
        scratch_shapes=scratch,
        compiler_params=pltpu.CompilerParams(vmem_limit_bytes=mib * 2**20),
        cost_estimate=pl.CostEstimate(flops=flops, bytes_accessed=moved, transcendentals=0),
    )(
        *[
            pltpu.with_memory_space_constraint(a, pltpu.HBM) if spec is None else a
            for a, spec in zip(args, in_specs)
        ]
    )


def shaped(shape, dtype):
    return jax.ShapeDtypeStruct(shape, dtype)


def dot(a, b, contract=(1, 0)):
    return lax.dot_general(
        a, b, (((contract[0],), (contract[1],)), ((), ())), preferred_element_type=F32
    )


def layer_stats(values):
    center = values - jnp.mean(values, axis=-1, keepdims=True)
    scale_inv = lax.rsqrt(jnp.mean(center * center, axis=-1, keepdims=True) + 1e-05)
    return center * scale_inv, scale_inv


def norm_back(upstream, normed, scale_inv):
    return scale_inv * (
        upstream
        - jnp.mean(upstream, axis=-1, keepdims=True)
        - normed * jnp.mean(upstream * normed, axis=-1, keepdims=True)
    )


def item_norm(rows_in):
    values = rows_in.astype(F32)
    lengths = jnp.sqrt(jnp.sum(values * values, axis=-1, keepdims=True) + 1e-06)
    return values / lengths, lengths


def sigmoid(value):
    return 1.0 / (1.0 + jnp.exp(-value))


def ask_kernel(owner_ref, row_ref, neg_ref, ask_ref, slot_row_ref, slot_col_ref):
    n = owner_ref.shape[1]
    owners = ask_ref.shape[0]
    lead = lax.broadcasted_iota(jnp.int32, (n, n), 0)
    lane = lax.broadcasted_iota(jnp.int32, (n, n), 1)

    def column(row):
        spread = jnp.broadcast_to(row.astype(F32), (n, n))
        return jnp.sum(jnp.where(lead == lane, spread, 0.0), axis=1, keepdims=True)

    owner_r = jnp.broadcast_to(owner_ref[...].astype(F32), (n, n))
    owner_c = column(owner_ref[...])
    same = owner_r == owner_c
    rank_r = jnp.sum(jnp.where(same & (lead < lane), 1.0, 0.0), axis=0, keepdims=True)
    rank_c = jnp.sum(jnp.where(same & (lane < lead), 1.0, 0.0), axis=1, keepdims=True)
    slot_r = owner_ref[...] * CAP + rank_r.astype(jnp.int32)
    slot_row_ref[...] = slot_r
    slot_col_ref[...] = (owner_c * CAP + rank_c).astype(jnp.int32)
    rows = jnp.broadcast_to(column(row_ref[...]), (n, LANES))
    by_owner = lax.broadcasted_iota(jnp.int32, (owners, n), 0) * CAP
    asked = None
    for k in range(CAP):
        hot = jnp.where(slot_r == by_owner + k, 1.0, 0.0).astype(BF16)
        part = dot(hot, jnp.where(lane == k, rows, 0.0).astype(BF16))
        asked = part if asked is None else asked + part
    for c in range(owners // n):
        negative = column(neg_ref[:, c * n : (c + 1) * n])
        ask_ref[c * n : (c + 1) * n, :] = jnp.where(
            lane == CAP, negative, asked[c * n : (c + 1) * n]
        ).astype(jnp.int32)


def spread_slot(wide, base, k, rows):
    for c in range(CHUNKS):
        wide[pl.ds(base + k * CHUNKS + c, rows.shape[0], stride=NBANK), :] = rows[
            :, c * LANES : (c + 1) * LANES
        ]


def slot_rows(wide, base, k, count):
    return jnp.concatenate(
        [wide[pl.ds(base + k * CHUNKS + c, count, stride=NBANK), :] for c in range(CHUNKS)], axis=1
    ).astype(BF16)


def piece(ref, i):
    size = ref.shape[0] // PIECES
    return ref.at[pl.ds(i * size, size), :]


def by_chip(asks_ref, core, items):
    count = asks_ref.shape[0] // (2 * items)
    return jnp.concatenate(
        [
            asks_ref[(2 * z + core) * items : (2 * z + core + 1) * items, :]
            for z in range(count)
        ],
        axis=0,
    )


def serve_kernel(items, loaded, asks_ref, table_ref, out_ref, wide, narrow, sems):
    chips = asks_ref.shape[0] // 2
    part = chips // PIECES
    rows = table_ref.shape[0]
    asks = [by_chip(asks_ref, core, items) for core in range(2)]
    loaded()
    table = table_ref[...]
    row_id = lax.broadcasted_iota(jnp.int32, (part, rows), 1)
    copies = []
    for i in range(PIECES):
        base = i * part * NBANK
        for seat in range(SEATS):
            core, k = (0, CAP) if seat == 2 * CAP else divmod(seat, CAP)
            asked = asks[core][i * part : (i + 1) * part, k : k + 1]
            hot = jnp.where(asked == row_id, 1.0, 0.0).astype(BF16)
            spread_slot(wide, base, seat, dot(hot, table))
        narrow[base : base + part * NBANK, :] = wide[base : base + part * NBANK, :].astype(BF16)
        copies.append(pltpu.make_async_copy(piece(narrow, i), piece(out_ref, i), sems.at[i]))
        copies[-1].start()
    for copy in copies:
        copy.wait()


def pair_masks(n):
    lane = lax.broadcasted_iota(jnp.int32, (n, LANES), 1)
    return lane < (LANES // 2)


def both_heads(part, low):
    zero = jnp.zeros_like(part)
    return jnp.concatenate([jnp.where(low, part, zero), jnp.where(low, zero, part)], axis=0)


def same_before(place_ref, sess_ref, ahead):
    block = place_ref[0] + ahead
    inside = block < sess_ref.shape[1]
    block = jnp.minimum(block, sess_ref.shape[1] - 1)
    here = sess_ref[0, block]
    near = inside & (block >= 1) & (sess_ref[0, jnp.maximum(block - 1, 0)] == here)
    far = inside & (block >= 2) & (sess_ref[0, jnp.maximum(block - 2, 0)] == here)
    return jnp.where(near, 1, 0), jnp.where(far, 1, 0)


def window_scale(place_ref, sess_ref, n):
    near, far = same_before(place_ref, sess_ref, 0)
    place = lax.broadcasted_iota(jnp.int32, (n, 3 * n), 0)
    lane = lax.broadcasted_iota(jnp.int32, (n, 3 * n), 1)
    count = place + 1 + n * (near + far)
    allowed = jnp.where(
        lane < n, far, jnp.where(lane < 2 * n, near, jnp.where(lane - 2 * n <= place, 1, 0))
    )
    scale = allowed.astype(F32) * (1.0 / count.astype(F32))
    return jnp.concatenate([scale, scale], axis=0)


def forward_kernel(
    loaded,
    place_ref,
    sess_ref,
    far_ref,
    near_ref,
    own_ref,
    gain_ref,
    w_in_ref,
    w_out_ref,
    unit_ref,
    length_ref,
    hat_ref,
    scale_ref,
    gate_ref,
    query_ref,
    slope_gq_ref,
    slope_vk_ref,
    keys_ref,
    values_ref,
    user_ref,
):
    n, width = own_ref.shape
    loaded()
    gain = gain_ref[...]
    hist_f = own_ref[...].astype(F32)

    def normed_in(values):
        return (layer_stats(values)[0] * gain).astype(BF16)

    projected = dot(normed_in(hist_f), w_in_ref[...])
    sigma = sigmoid(projected)
    slope = sigma * (1.0 + projected * (1.0 - sigma))
    slope_gq_ref[:, :width] = slope[:, :width]
    slope_vk_ref[:, :width] = slope[:, width : 2 * width]
    slope_gq_ref[:, width:] = slope[:, 2 * width : 3 * width]
    slope_vk_ref[:, width:] = slope[:, 3 * width :]
    act = (projected * sigma).astype(BF16)
    gate_ref[...] = act[:, :width]
    query_ref[...] = act[:, 2 * width : 3 * width]
    before = jnp.concatenate(
        [normed_in(far_ref[...].astype(F32)), normed_in(near_ref[...].astype(F32))], axis=0
    )
    values_before = dot(before, w_in_ref[:, width : 2 * width])
    keys_before = dot(before, w_in_ref[:, 3 * width :])
    values_ref[: 2 * n, :] = (values_before * sigmoid(values_before)).astype(BF16)
    keys_ref[: 2 * n, :] = (keys_before * sigmoid(keys_before)).astype(BF16)
    values_ref[2 * n :, :] = act[:, width : 2 * width]
    keys_ref[2 * n :, :] = act[:, 3 * width :]
    scale = window_scale(place_ref, sess_ref, n)
    low = pair_masks(n)
    score_scale = 1.0 / math.sqrt(width // HEADS)
    attended = []
    for pair in range(HEADS // 2):
        lanes = slice(pair * LANES, (pair + 1) * LANES)
        queries = both_heads(act[:, 2 * width + pair * LANES : 2 * width + (pair + 1) * LANES], low)
        scores = dot(queries, keys_ref[:, lanes], (1, 1)) * score_scale
        weights = (scores * sigmoid(scores) * scale).astype(BF16)
        both = dot(weights, values_ref[:, lanes])
        attended.append(jnp.where(low, both[:n], both[n:]))
    attn_hat, scale_a = layer_stats(jnp.concatenate(attended, axis=1))
    hat_ref[...] = attn_hat
    scale_ref[...] = jnp.broadcast_to(scale_a, scale_ref.shape)
    gated = (attn_hat * act[:, :width].astype(F32)).astype(BF16)
    user_out = dot(gated, w_out_ref[...]) + hist_f
    user_len = jnp.sqrt(jnp.sum(user_out * user_out, axis=-1, keepdims=True) + 1e-06)
    user_unit = user_out / user_len
    unit_ref[...] = user_unit
    user_ref[...] = user_unit.astype(BF16)
    length_ref[...] = jnp.broadcast_to(user_len, length_ref.shape)


def local_slots(slots, core, items):
    bits = items.bit_length() - 1
    owner = slots >> 1
    local = ((owner >> (bits + 1)) << bits) + (owner & (items - 1))
    return jnp.where(((owner >> bits) & 1) == core, local * CAP + (slots & 1), -1)


def as_column(row):
    n = row.shape[1]
    lead = lax.broadcasted_iota(jnp.int32, (n, n), 0)
    lane = lax.broadcasted_iota(jnp.int32, (n, n), 1)
    spread = jnp.broadcast_to(row.astype(F32), (n, n))
    return jnp.sum(jnp.where(lead == lane, spread, 0.0), axis=1, keepdims=True).astype(jnp.int32)


def softmax_kernel(
    items,
    loaded,
    place_ref,
    fetched_ref,
    neg_row_ref,
    slots_ref,
    users_ref,
    den_ref,
    pos_exp_ref,
    neg_exp_ref,
    neg_rows_ref,
    pos_rows_ref,
    wide,
):
    chips = neg_row_ref.shape[1]
    n = users_ref.shape[0] // 2
    wide[...] = fetched_ref[...].astype(F32)
    neg_rows = slot_rows(wide, 0, 2 * CAP, chips)
    neg_rows_ref[...] = neg_rows
    neg_bf = item_norm(neg_rows)[0].astype(BF16)
    loaded()
    users = users_ref[...]
    neg_row = neg_row_ref[...] + 1
    exponent = jnp.zeros(neg_row.shape, F32)
    for level in range(1, 8):
        exponent = exponent + jnp.where(neg_row >= (1 << level), 1.0, 0.0)
    shift = math.log(8) + exponent * math.log(2.0)
    neg_exp = jnp.exp(dot(users, neg_bf, (1, 1)) / TAU + shift)
    neg_exp_ref[...] = neg_exp
    slots = local_slots(slots_ref[...], place_ref[1], items)
    lane = lax.broadcasted_iota(jnp.int32, (n, chips), 1) * CAP
    pos_rows, here = [], []
    for core in range(2):
        column = as_column(slots[:, core * n : (core + 1) * n])
        here.append(jnp.where(column >= 0, 1.0, 0.0))
        hots = [jnp.where(column == lane + k, 1.0, 0.0).astype(BF16) for k in range(CAP)]
        rows = [slot_rows(wide, 0, core * CAP + k, chips) for k in range(CAP)]
        pos_rows.append(dot(jnp.concatenate(hots, axis=1), jnp.concatenate(rows, axis=0)))
    pos_rows = jnp.concatenate(pos_rows, axis=0)
    pos_rows_ref[...] = pos_rows.astype(BF16)
    pos_bf = item_norm(pos_rows)[0].astype(BF16).astype(F32)
    along = jnp.sum(users.astype(F32) * pos_bf, axis=-1, keepdims=True)
    pos_exp = jnp.concatenate(here, axis=0) * jnp.exp(along / TAU)
    pos_exp_ref[...] = jnp.broadcast_to(pos_exp, pos_exp_ref.shape)
    den_ref[...] = jnp.broadcast_to(
        pos_exp + jnp.sum(neg_exp, axis=-1, keepdims=True), den_ref.shape
    )


def send_kernel(
    items,
    loaded,
    place_ref,
    den_ref,
    den_other_ref,
    pos_exp_ref,
    neg_exp_ref,
    neg_rows_ref,
    pos_rows_ref,
    users_ref,
    slots_ref,
    send_ref,
    own_part_ref,
    other_part_ref,
    wide,
    narrow,
    sems,
    held,
    held_sems,
):
    chips = neg_rows_ref.shape[0]
    n = users_ref.shape[0] // 2
    core_here = place_ref[1]
    loaded()
    users = users_ref[...]
    user_f = users.astype(F32)
    neg_unit, neg_len = item_norm(neg_rows_ref[...])
    neg_bf = neg_unit.astype(BF16)
    pos_unit, pos_len = item_norm(pos_rows_ref[...])
    pos_bf = pos_unit.astype(BF16).astype(F32)
    slots = local_slots(slots_ref[...], core_here, items)
    here = jnp.concatenate(
        [jnp.where(as_column(slots[:, c * n : (c + 1) * n]) >= 0, 1.0, 0.0) for c in range(2)],
        axis=0,
    )
    denominator = den_ref[:, 0:1] + den_other_ref[:, 0:1]
    pos_delta = here * (pos_exp_ref[:, 0:1] / denominator - 1.0)
    neg_prob = (neg_exp_ref[...] / denominator).astype(BF16)
    raw_pos = pos_delta * user_f / TAU
    pos_grad = (raw_pos - pos_unit * jnp.sum(pos_unit * raw_pos, axis=-1, keepdims=True)) / pos_len
    pos_grad = pos_grad.astype(BF16)
    unit_part = (pos_delta * pos_bf + dot(neg_prob, neg_bf)) / TAU
    first = core_here == 0
    held[:n, :] = jnp.where(first, unit_part[:n], unit_part[n:])
    held[n:, :] = jnp.where(first, unit_part[n:], unit_part[:n])
    copies = [
        pltpu.make_async_copy(held.at[pl.ds(n, n), :], other_part_ref, held_sems.at[0]),
        pltpu.make_async_copy(held.at[pl.ds(0, n), :], own_part_ref, held_sems.at[1]),
    ]
    for copy in copies:
        copy.start()
    part = chips // PIECES
    lead = lax.broadcasted_iota(jnp.int32, (part, n), 0) * CAP
    for i in range(PIECES):
        base = i * part * NBANK
        for core in range(2):
            row = slots[:, core * n : (core + 1) * n]
            for k in range(CAP):
                hot = jnp.where(row == lead + (i * part * CAP + k), 1.0, 0.0).astype(BF16)
                placed = dot(hot, pos_grad[core * n : (core + 1) * n])
                spread_slot(wide, base, core * CAP + k, placed)
        own = slice(i * part, (i + 1) * part)
        raw_neg = dot(neg_prob[:, own], users, (0, 0)) / TAU
        along = jnp.sum(neg_unit[own] * raw_neg, axis=-1, keepdims=True)
        spread_slot(wide, base, 2 * CAP, (raw_neg - neg_unit[own] * along) / neg_len[own])
        narrow[base : base + part * NBANK, :] = wide[base : base + part * NBANK, :].astype(BF16)
        copies.append(pltpu.make_async_copy(piece(narrow, i), piece(send_ref, i), sems.at[i]))
        copies[-1].start()
    for copy in copies:
        copy.wait()


def heads_back_kernel(
    loaded,
    place_ref,
    sess_ref,
    own_part_ref,
    other_part_ref,
    unit_ref,
    length_ref,
    w_out_ref,
    gate_ref,
    query_ref,
    hat_ref,
    scale_ref,
    keys_ref,
    values_ref,
    slope_ref,
    w_in_ref,
    own_ref,
    near_ref,
    far_ref,
    in_part_ref,
    user_grad_ref,
):
    n, width = hat_ref.shape
    loaded()
    attn_hat = hat_ref[...]
    user_unit = unit_ref[...]
    unit_grad = own_part_ref[...] + other_part_ref[...]
    user_grad = (
        unit_grad - user_unit * jnp.sum(user_unit * unit_grad, axis=-1, keepdims=True)
    ) / length_ref[:, 0:1]
    user_grad_ref[...] = user_grad
    gated_grad = dot(user_grad.astype(BF16), w_out_ref[...], (1, 1))
    hat_grad = gated_grad * gate_ref[...].astype(F32)
    upstream = norm_back(hat_grad, attn_hat, scale_ref[:, 0:1]).astype(BF16)
    scale = window_scale(place_ref, sess_ref, n)
    low = pair_masks(n)
    score_scale = 1.0 / math.sqrt(width // HEADS)
    query_grads = []
    for pair in range(HEADS // 2):
        first = pair * LANES
        lanes = slice(first, first + LANES)
        later = slice(width + first, width + first + LANES)
        queries = both_heads(query_ref[:, lanes], low)
        grads = both_heads(upstream[:, lanes], low)
        keys = keys_ref[:, lanes]
        scores = dot(queries, keys, (1, 1)) * score_scale
        weight_grad = dot(grads, values_ref[:, lanes], (1, 1))
        sigma = sigmoid(scores)
        weights = (scores * sigma * scale).astype(BF16)
        slope = sigma * (1.0 + scores * (1.0 - sigma))
        score_grad = (weight_grad * slope * (scale * score_scale)).astype(BF16)
        both = dot(score_grad, keys)
        query_grads.append(jnp.where(low, both[:n], both[n:]))
        key_grad = dot(score_grad, queries, (0, 0))
        value_grad = dot(weights, grads, (0, 0))
        far_ref[:, lanes] = value_grad[:n].astype(BF16)
        near_ref[:, lanes] = value_grad[n : 2 * n].astype(BF16)
        own_ref[:, lanes] = value_grad[2 * n :]
        far_ref[:, later] = key_grad[:n].astype(BF16)
        near_ref[:, later] = key_grad[n : 2 * n].astype(BF16)
        own_ref[:, later] = key_grad[2 * n :]
    gate_part = (gated_grad * attn_hat * slope_ref[:, :width]).astype(BF16)
    query_part = (jnp.concatenate(query_grads, axis=1) * slope_ref[:, width:]).astype(BF16)
    in_part_ref[...] = dot(gate_part, w_in_ref[:, :width], (1, 1)) + dot(
        query_part, w_in_ref[:, 2 * width : 3 * width], (1, 1)
    )


def last_kernel(
    items,
    loaded,
    returned_ref,
    near_ref,
    far_ref,
    asks_ref,
    own_grad_ref,
    slope_ref,
    in_part_ref,
    w_in_ref,
    gain_ref,
    hist_ref,
    user_grad_ref,
    table_grad_ref,
    history_grad_ref,
    wide,
    held,
    held_sem,
):
    width = hist_ref.shape[1]
    chips = asks_ref.shape[0] // 2
    rows = table_grad_ref.shape[0]
    wide[...] = returned_ref[...].astype(F32)
    loaded(1)
    asks = [jnp.transpose(by_chip(asks_ref, core, items).astype(F32)) for core in range(2)]
    row_id = lax.broadcasted_iota(jnp.int32, (rows, chips), 0).astype(F32)
    hots, parts = [], []
    for seat in range(SEATS):
        core, k = (0, CAP) if seat == 2 * CAP else divmod(seat, CAP)
        hots.append(jnp.where(asks[core][k : k + 1] == row_id, 1.0, 0.0).astype(BF16))
        parts.append(slot_rows(wide, 0, seat, chips))
    total = dot(jnp.concatenate(hots, axis=1), jnp.concatenate(parts, axis=0))
    held[...] = total.astype(BF16)
    copy = pltpu.make_async_copy(held, table_grad_ref, held_sem)
    copy.start()
    loaded()
    come = near_ref[...].astype(F32) + far_ref[...].astype(F32)
    proj_grad = ((own_grad_ref[...] + come) * slope_ref[...]).astype(BF16)
    in_grad = (
        in_part_ref[...]
        + dot(proj_grad[:, :width], w_in_ref[:, width : 2 * width], (1, 1))
        + dot(proj_grad[:, width:], w_in_ref[:, 3 * width :], (1, 1))
    )
    normed_x, scale_x = layer_stats(hist_ref[...].astype(F32))
    back = norm_back(in_grad * gain_ref[...], normed_x, scale_x)
    history_grad_ref[...] = (back + user_grad_ref[...]).astype(BF16)
    copy.wait()


def passed_along(shard, by):
    axes = ("z", "core")
    count = lax.axis_size(axes)
    pairs = [(i, i + by) for i in range(count) if 0 <= i + by < count]
    return lax.ppermute(shard, axes, pairs)


def swapped(shard):
    return lax.ppermute(shard, "core", [(0, 1), (1, 0)])


def on_device(history, ln_gain, w_in, w_out, item_table, sessions, pos_owner, pos_row, neg_rows):
    n, width = history.shape[1:]
    items = lax.axis_size("items")
    chips = lax.axis_size("z") * items
    owners = 2 * chips
    rows = item_table.shape[0]
    core = lax.axis_index("core")
    place = jnp.stack([2 * lax.axis_index("z") + core, core]).astype(jnp.int32)
    own = history[0]
    gain = ln_gain.reshape(1, width)
    neg_row = neg_rows.reshape(1, owners)

    def exchange(shard, axes, chunk):
        shape = shard.shape
        split = shard.reshape((-1,) + chunk)
        return lax.all_to_all(split, axes, split_axis=0, concat_axis=0, tiled=True).reshape(shape)

    def by_core(mine, other, axis):
        return jnp.where(
            core == 0,
            jnp.concatenate([mine, other], axis=axis),
            jnp.concatenate([other, mine], axis=axis),
        )

    ask, slot_row, slot_col = call(
        ask_kernel,
        [shaped((owners, LANES), jnp.int32), shaped((1, n), jnp.int32), shaped((n, 1), jnp.int32)],
        [VMEM, VMEM, VMEM],
        (pos_owner.reshape(1, n), pos_row, neg_row),
        2 * CAP * owners * n * LANES,
    )
    asks = exchange(ask, ("z", "core", "items"), (1, LANES))
    near = passed_along(own, 1)
    far = passed_along(own, 2)

    big = chips * NBANK
    staging = [
        pltpu.VMEM((big, LANES), BF16),
        pltpu.VMEM((big, LANES), F32),
        pltpu.SemaphoreType.DMA((PIECES,)),
    ]
    outward = [staging[1], staging[0], staging[2]]
    (served,) = call(
        functools.partial(serve_kernel, items),
        [shaped((big, LANES), BF16)],
        [VMEM, None],
        (asks, item_table),
        2 * SEATS * chips * rows * width,
        outward,
        mib=40,
        out_specs=(HBM,),
    )
    served, near, far = lax.optimization_barrier((served, near, far))
    fetched = exchange(served, ("z", "items"), (SEATS, CHUNKS, LANES))

    unit, length, attn_hat, scale_a, gate, query, slope_gq, slope_vk, keys, values, user = call(
        forward_kernel,
        [
            pltpu.HBM((n, width), F32),
            pltpu.HBM((n, LANES), F32),
            pltpu.HBM((n, width), F32),
            pltpu.HBM((n, LANES), F32),
            pltpu.HBM((n, width), BF16),
            pltpu.HBM((n, width), BF16),
            pltpu.HBM((n, 2 * width), F32),
            pltpu.HBM((n, 2 * width), F32),
            pltpu.HBM((3 * n, width), BF16),
            pltpu.HBM((3 * n, width), BF16),
            pltpu.HBM((n, width), BF16),
        ],
        [SMEM, SMEM, VMEM, VMEM] + [None] * 4,
        (place, sessions, far, near, own, gain, w_in, w_out),
        2 * n * width * width * 12,
        mib=40,
    )

    users = by_core(user, swapped(user), 0)
    slots = by_core(slot_row, swapped(slot_row), 1)
    neg_here = lax.dynamic_index_in_dim(
        neg_rows.reshape(chips // items, 2, items), core, axis=1, keepdims=False
    ).reshape(1, chips)
    den, pos_exp, neg_exp, neg_kept, pos_kept = call(
        functools.partial(softmax_kernel, items),
        [
            pltpu.HBM((2 * n, LANES), F32),
            pltpu.HBM((2 * n, LANES), F32),
            pltpu.HBM((2 * n, chips), F32),
            pltpu.HBM((chips, width), BF16),
            pltpu.HBM((2 * n, width), BF16),
        ],
        [SMEM, VMEM] + [None] * 3,
        (place, fetched, neg_here, slots, users),
        2 * n * width * owners * 3,
        [staging[1]],
        mib=40,
    )
    send, own_part, other_part = call(
        functools.partial(send_kernel, items),
        [shaped((big, LANES), BF16), pltpu.HBM((n, width), F32), pltpu.HBM((n, width), F32)],
        [SMEM, None, VMEM] + [None] * 6,
        (place, den, swapped(den), pos_exp, neg_exp, neg_kept, pos_kept, users, slots),
        2 * n * width * owners * 4,
        outward + [pltpu.VMEM((2 * n, width), F32), pltpu.SemaphoreType.DMA((2,))],
        mib=40,
        out_specs=(HBM, HBM, HBM),
    )
    returned = exchange(send, ("z", "items"), (SEATS, CHUNKS, LANES))

    own_grad, near_grad, far_grad, in_part, user_grad = call(
        heads_back_kernel,
        [
            shaped((n, 2 * width), F32),
            shaped((n, 2 * width), BF16),
            shaped((n, 2 * width), BF16),
            shaped((n, width), F32),
            shaped((n, width), F32),
        ],
        [SMEM, SMEM] + [None] * 13,
        (
            place,
            sessions,
            own_part,
            swapped(other_part),
            unit,
            length,
            w_out,
            gate,
            query,
            attn_hat,
            scale_a,
            keys,
            values,
            slope_gq,
            w_in,
        ),
        2 * n * width * width * 12,
    )
    near_back = passed_along(near_grad, -1)
    far_back = passed_along(far_grad, -2)
    table_grad, history_grad = call(
        functools.partial(last_kernel, items),
        [shaped((rows, width), BF16), shaped((n, width), BF16)],
        [VMEM] * 3 + [None] * 8,
        (
            returned,
            near_back,
            far_back,
            asks,
            own_grad,
            slope_vk,
            in_part,
            w_in,
            gain,
            own,
            user_grad,
        ),
        2 * SEATS * chips * rows * width,
        [staging[1], pltpu.VMEM((rows, width), BF16), pltpu.SemaphoreType.DMA(())],
        mib=40,
        out_specs=(HBM, VMEM),
    )
    return history_grad[None], table_grad


def solution(mesh):
    hist, items = mesh.shape["hist"], mesh.shape["items"]
    split = jax.sharding.Mesh(
        mesh.devices.reshape(hist // 2, 2, items), ("z", "core", "items")
    )
    return jax.shard_map(
        on_device,
        mesh=split,
        in_specs=(
            P("items", ("z", "core"), None),
            P(),
            P(),
            P(),
            P(("z", "core", "items"), None),
            P("items", None),
            P("items", ("z", "core"), None),
            P("items", ("z", "core")),
            P("items", None, None),
        ),
        out_specs=(P("items", ("z", "core"), None), P(("z", "core", "items"), None)),
        check_vma=False,
    )
```

```python
import functools
import math

import jax
import jax.numpy as jnp
from jax import lax
from jax.experimental import pallas as pl
from jax.experimental.pallas import tpu as pltpu
from jax.sharding import PartitionSpec as P

HEADS = 8
TAU = 0.05
CAP = 2
CHUNKS = 4
LANES = 128
SLOTS = CAP + 1
SEATS = 2 * CAP + 1
PIECES = 2
NBANK = SEATS * CHUNKS
F32 = jnp.float32
BF16 = jnp.bfloat16
VMEM = pl.BlockSpec(memory_space=pltpu.VMEM)
HBM = pl.BlockSpec(memory_space=pltpu.HBM)
SMEM = pl.BlockSpec(memory_space=pltpu.SMEM)


def call(kernel, outs, in_specs, args, flops, scratch=(), mib=60, out_specs=None):
    moved = sum(a.size * a.dtype.itemsize for a in args) + sum(
        math.prod(o.shape) * o.dtype.itemsize for o in outs
    )
    pinned = [i for i, spec in enumerate(in_specs) if spec is None]
    scratch = list(scratch)

    def body(*refs):
        refs = list(refs)
        count = len(pinned)
        if not count:
            return kernel(*refs)
        held, sems = refs[-count - 1 : -1], refs[-1]
        refs = refs[: -count - 1]
        copies = []
        for j, i in enumerate(pinned):
            copies.append(pltpu.make_async_copy(refs[i], held[j], sems.at[j]))
            copies[-1].start()
            refs[i] = held[j]

        waiting = list(copies)

        def loaded(count=len(copies)):
            for copy in waiting[:count]:
                copy.wait()
            del waiting[:count]

        return kernel(loaded, *refs)

    if pinned:
        scratch += [pltpu.VMEM(args[i].shape, args[i].dtype) for i in pinned]
        scratch.append(pltpu.SemaphoreType.DMA((len(pinned),)))
    return pl.pallas_call(
        body,
        out_shape=tuple(outs),
        in_specs=[HBM if spec is None else spec for spec in in_specs],
        out_specs=out_specs or tuple(VMEM for _ in outs),
        scratch_shapes=scratch,
        compiler_params=pltpu.CompilerParams(vmem_limit_bytes=mib * 2**20),
        cost_estimate=pl.CostEstimate(flops=flops, bytes_accessed=moved, transcendentals=0),
    )(
        *[
            pltpu.with_memory_space_constraint(a, pltpu.HBM) if spec is None else a
            for a, spec in zip(args, in_specs)
        ]
    )


def shaped(shape, dtype):
    return jax.ShapeDtypeStruct(shape, dtype)


def dot(a, b, contract=(1, 0)):
    return lax.dot_general(
        a, b, (((contract[0],), (contract[1],)), ((), ())), preferred_element_type=F32
    )


def layer_stats(values):
    center = values - jnp.mean(values, axis=-1, keepdims=True)
    scale_inv = lax.rsqrt(jnp.mean(center * center, axis=-1, keepdims=True) + 1e-05)
    return center * scale_inv, scale_inv


def norm_back(upstream, normed, scale_inv):
    return scale_inv * (
        upstream
        - jnp.mean(upstream, axis=-1, keepdims=True)
        - normed * jnp.mean(upstream * normed, axis=-1, keepdims=True)
    )


def item_norm(rows_in):
    values = rows_in.astype(F32)
    lengths = jnp.sqrt(jnp.sum(values * values, axis=-1, keepdims=True) + 1e-06)
    return values / lengths, lengths


def sigmoid(value):
    return 1.0 / (1.0 + jnp.exp(-value))


def ask_kernel(owner_ref, row_ref, neg_ref, ask_ref, slot_row_ref, slot_col_ref):
    n = owner_ref.shape[1]
    owners = ask_ref.shape[0]
    lead = lax.broadcasted_iota(jnp.int32, (n, n), 0)
    lane = lax.broadcasted_iota(jnp.int32, (n, n), 1)

    def column(row):
        spread = jnp.broadcast_to(row.astype(F32), (n, n))
        return jnp.sum(jnp.where(lead == lane, spread, 0.0), axis=1, keepdims=True)

    owner_r = jnp.broadcast_to(owner_ref[...].astype(F32), (n, n))
    owner_c = column(owner_ref[...])
    same = owner_r == owner_c
    rank_r = jnp.sum(jnp.where(same & (lead < lane), 1.0, 0.0), axis=0, keepdims=True)
    rank_c = jnp.sum(jnp.where(same & (lane < lead), 1.0, 0.0), axis=1, keepdims=True)
    slot_r = owner_ref[...] * CAP + rank_r.astype(jnp.int32)
    slot_row_ref[...] = slot_r
    slot_col_ref[...] = (owner_c * CAP + rank_c).astype(jnp.int32)
    rows = jnp.broadcast_to(column(row_ref[...]), (n, LANES))
    by_owner = lax.broadcasted_iota(jnp.int32, (owners, n), 0) * CAP
    asked = None
    for k in range(CAP):
        hot = jnp.where(slot_r == by_owner + k, 1.0, 0.0).astype(BF16)
        part = dot(hot, jnp.where(lane == k, rows, 0.0).astype(BF16))
        asked = part if asked is None else asked + part
    for c in range(owners // n):
        negative = column(neg_ref[:, c * n : (c + 1) * n])
        ask_ref[c * n : (c + 1) * n, :] = jnp.where(
            lane == CAP, negative, asked[c * n : (c + 1) * n]
        ).astype(jnp.int32)


def spread_slot(wide, base, k, rows):
    for c in range(CHUNKS):
        wide[pl.ds(base + k * CHUNKS + c, rows.shape[0], stride=NBANK), :] = rows[
            :, c * LANES : (c + 1) * LANES
        ]


def slot_rows(wide, base, k, count):
    return jnp.concatenate(
        [wide[pl.ds(base + k * CHUNKS + c, count, stride=NBANK), :] for c in range(CHUNKS)], axis=1
    ).astype(BF16)


def piece(ref, i):
    size = ref.shape[0] // PIECES
    return ref.at[pl.ds(i * size, size), :]


def by_chip(asks_ref, core, items):
    count = asks_ref.shape[0] // (2 * items)
    return jnp.concatenate(
        [
            asks_ref[(2 * z + core) * items : (2 * z + core + 1) * items, :]
            for z in range(count)
        ],
        axis=0,
    )


def serve_kernel(items, loaded, asks_ref, table_ref, out_ref, wide, narrow, sems):
    chips = asks_ref.shape[0] // 2
    part = chips // PIECES
    rows = table_ref.shape[0]
    asks = [by_chip(asks_ref, core, items) for core in range(2)]
    loaded()
    table = table_ref[...]
    row_id = lax.broadcasted_iota(jnp.int32, (part, rows), 1)
    copies = []
    for i in range(PIECES):
        base = i * part * NBANK
        for seat in range(SEATS):
            core, k = (0, CAP) if seat == 2 * CAP else divmod(seat, CAP)
            asked = asks[core][i * part : (i + 1) * part, k : k + 1]
            hot = jnp.where(asked == row_id, 1.0, 0.0).astype(BF16)
            spread_slot(wide, base, seat, dot(hot, table))
        narrow[base : base + part * NBANK, :] = wide[base : base + part * NBANK, :].astype(BF16)
        copies.append(pltpu.make_async_copy(piece(narrow, i), piece(out_ref, i), sems.at[i]))
        copies[-1].start()
    for copy in copies:
        copy.wait()


def pair_masks(n):
    lane = lax.broadcasted_iota(jnp.int32, (n, LANES), 1)
    return lane < (LANES // 2)


def both_heads(part, low):
    zero = jnp.zeros_like(part)
    return jnp.concatenate([jnp.where(low, part, zero), jnp.where(low, zero, part)], axis=0)


def same_before(place_ref, sess_ref, ahead):
    block = place_ref[0] + ahead
    inside = block < sess_ref.shape[1]
    block = jnp.minimum(block, sess_ref.shape[1] - 1)
    here = sess_ref[0, block]
    near = inside & (block >= 1) & (sess_ref[0, jnp.maximum(block - 1, 0)] == here)
    far = inside & (block >= 2) & (sess_ref[0, jnp.maximum(block - 2, 0)] == here)
    return jnp.where(near, 1, 0), jnp.where(far, 1, 0)


def window_scale(place_ref, sess_ref, n):
    near, far = same_before(place_ref, sess_ref, 0)
    place = lax.broadcasted_iota(jnp.int32, (n, 3 * n), 0)
    lane = lax.broadcasted_iota(jnp.int32, (n, 3 * n), 1)
    count = place + 1 + n * (near + far)
    allowed = jnp.where(
        lane < n, far, jnp.where(lane < 2 * n, near, jnp.where(lane - 2 * n <= place, 1, 0))
    )
    scale = allowed.astype(F32) * (1.0 / count.astype(F32))
    return jnp.concatenate([scale, scale], axis=0)


def forward_kernel(
    loaded,
    place_ref,
    sess_ref,
    far_ref,
    near_ref,
    own_ref,
    gain_ref,
    w_in_ref,
    w_out_ref,
    unit_ref,
    length_ref,
    hat_ref,
    scale_ref,
    gate_ref,
    query_ref,
    slope_gq_ref,
    slope_vk_ref,
    keys_ref,
    values_ref,
    user_ref,
):
    n, width = own_ref.shape
    loaded()
    gain = gain_ref[...]
    hist_f = own_ref[...].astype(F32)

    def normed_in(values):
        return (layer_stats(values)[0] * gain).astype(BF16)

    projected = dot(normed_in(hist_f), w_in_ref[...])
    sigma = sigmoid(projected)
    slope = sigma * (1.0 + projected * (1.0 - sigma))
    slope_gq_ref[:, :width] = slope[:, :width]
    slope_vk_ref[:, :width] = slope[:, width : 2 * width]
    slope_gq_ref[:, width:] = slope[:, 2 * width : 3 * width]
    slope_vk_ref[:, width:] = slope[:, 3 * width :]
    act = (projected * sigma).astype(BF16)
    gate_ref[...] = act[:, :width]
    query_ref[...] = act[:, 2 * width : 3 * width]
    before = jnp.concatenate(
        [normed_in(far_ref[...].astype(F32)), normed_in(near_ref[...].astype(F32))], axis=0
    )
    values_before = dot(before, w_in_ref[:, width : 2 * width])
    keys_before = dot(before, w_in_ref[:, 3 * width :])
    values_ref[: 2 * n, :] = (values_before * sigmoid(values_before)).astype(BF16)
    keys_ref[: 2 * n, :] = (keys_before * sigmoid(keys_before)).astype(BF16)
    values_ref[2 * n :, :] = act[:, width : 2 * width]
    keys_ref[2 * n :, :] = act[:, 3 * width :]
    scale = window_scale(place_ref, sess_ref, n)
    low = pair_masks(n)
    score_scale = 1.0 / math.sqrt(width // HEADS)
    attended = []
    for pair in range(HEADS // 2):
        lanes = slice(pair * LANES, (pair + 1) * LANES)
        queries = both_heads(act[:, 2 * width + pair * LANES : 2 * width + (pair + 1) * LANES], low)
        scores = dot(queries, keys_ref[:, lanes], (1, 1)) * score_scale
        weights = (scores * sigmoid(scores) * scale).astype(BF16)
        both = dot(weights, values_ref[:, lanes])
        attended.append(jnp.where(low, both[:n], both[n:]))
    attn_hat, scale_a = layer_stats(jnp.concatenate(attended, axis=1))
    hat_ref[...] = attn_hat
    scale_ref[...] = jnp.broadcast_to(scale_a, scale_ref.shape)
    gated = (attn_hat * act[:, :width].astype(F32)).astype(BF16)
    user_out = dot(gated, w_out_ref[...]) + hist_f
    user_len = jnp.sqrt(jnp.sum(user_out * user_out, axis=-1, keepdims=True) + 1e-06)
    user_unit = user_out / user_len
    unit_ref[...] = user_unit
    user_ref[...] = user_unit.astype(BF16)
    length_ref[...] = jnp.broadcast_to(user_len, length_ref.shape)


def local_slots(slots, core, items):
    bits = items.bit_length() - 1
    owner = slots >> 1
    local = ((owner >> (bits + 1)) << bits) + (owner & (items - 1))
    return jnp.where(((owner >> bits) & 1) == core, local * CAP + (slots & 1), -1)


def as_column(row):
    n = row.shape[1]
    lead = lax.broadcasted_iota(jnp.int32, (n, n), 0)
    lane = lax.broadcasted_iota(jnp.int32, (n, n), 1)
    spread = jnp.broadcast_to(row, (n, n))
    return jnp.sum(jnp.where(lead == lane, spread, 0.0), axis=1, keepdims=True)


def as_row(column):
    n = column.shape[0]
    lead = lax.broadcasted_iota(jnp.int32, (n, n), 0)
    lane = lax.broadcasted_iota(jnp.int32, (n, n), 1)
    return jnp.sum(jnp.where(lead == lane, column, 0.0), axis=0, keepdims=True)


def halves(convert, values, axis):
    n = values.shape[axis] // 2
    first, second = (values[:, :n], values[:, n:]) if axis else (values[:n], values[n:])
    return jnp.concatenate([convert(first), convert(second)], axis=1 - axis)


def softmax_kernel(
    items,
    loaded,
    place_ref,
    fetched_ref,
    neg_row_ref,
    slots_ref,
    users_ref,
    stats_ref,
    neg_exp_ref,
    neg_rows_ref,
    pos_rows_ref,
    wide,
    held_rows,
    held_exp,
    held_sems,
):
    chips = neg_row_ref.shape[1]
    n = users_ref.shape[0] // 2
    wide[...] = fetched_ref[...].astype(F32)
    neg_rows = slot_rows(wide, 0, 2 * CAP, chips)
    held_rows[:chips, :] = neg_rows
    copies = [
        pltpu.make_async_copy(held_rows.at[pl.ds(0, chips), :], neg_rows_ref, held_sems.at[0]),
        pltpu.make_async_copy(held_exp, neg_exp_ref, held_sems.at[1]),
        pltpu.make_async_copy(
            held_rows.at[pl.ds(chips, 2 * n), :], pos_rows_ref, held_sems.at[2]
        ),
    ]
    copies[0].start()
    neg_bf = item_norm(neg_rows)[0].astype(BF16)
    loaded()
    users = users_ref[...]
    neg_row = neg_row_ref[...] + 1
    exponent = jnp.zeros(neg_row.shape, F32)
    for level in range(1, 8):
        exponent = exponent + jnp.where(neg_row >= (1 << level), 1.0, 0.0)
    shift = math.log(8) + exponent * math.log(2.0)
    neg_exp = jnp.exp(dot(users, neg_bf, (1, 1)) / TAU + shift)
    held_exp[...] = neg_exp
    copies[1].start()
    slots = local_slots(slots_ref[...], place_ref[1], items)
    lane = lax.broadcasted_iota(jnp.int32, (n, chips), 1) * CAP
    pos_rows, here = [], []
    for core in range(2):
        column = as_column(slots[:, core * n : (core + 1) * n].astype(F32)).astype(jnp.int32)
        here.append(jnp.where(column >= 0, 1.0, 0.0))
        hots = [jnp.where(column == lane + k, 1.0, 0.0).astype(BF16) for k in range(CAP)]
        rows = [slot_rows(wide, 0, core * CAP + k, chips) for k in range(CAP)]
        pos_rows.append(dot(jnp.concatenate(hots, axis=1), jnp.concatenate(rows, axis=0)))
    pos_rows = jnp.concatenate(pos_rows, axis=0)
    held_rows[chips:, :] = pos_rows.astype(BF16)
    copies[2].start()
    pos_bf = item_norm(pos_rows)[0].astype(BF16).astype(F32)
    along = jnp.sum(users.astype(F32) * pos_bf, axis=-1, keepdims=True)
    pos_exp = jnp.concatenate(here, axis=0) * jnp.exp(along / TAU)
    total = pos_exp + jnp.sum(neg_exp, axis=-1, keepdims=True)
    stats_ref[0:1, :] = halves(as_row, total, 0)
    stats_ref[1:2, :] = halves(as_row, pos_exp, 0)
    for copy in copies:
        copy.wait()


def send_kernel(
    items,
    loaded,
    place_ref,
    stats_ref,
    stats_other_ref,
    neg_rows_ref,
    pos_rows_ref,
    users_ref,
    slots_ref,
    neg_exp_ref,
    send_ref,
    own_part_ref,
    other_part_ref,
    wide,
    narrow,
    sems,
    held,
    held_sems,
):
    chips = neg_rows_ref.shape[0]
    n = users_ref.shape[0] // 2
    core_here = place_ref[1]
    loaded(2)
    neg_unit, neg_len = item_norm(neg_rows_ref[...])
    neg_bf = neg_unit.astype(BF16)
    pos_unit, pos_len = item_norm(pos_rows_ref[...])
    pos_bf = pos_unit.astype(BF16).astype(F32)
    loaded()
    users = users_ref[...]
    user_f = users.astype(F32)
    slots = local_slots(slots_ref[...], core_here, items)
    total = stats_ref[0:1, :] + stats_other_ref[0:1, :]
    denominator = halves(as_column, total, 1)
    delta = jnp.where(slots >= 0, stats_ref[1:2, :] / total - 1.0, 0.0)
    pos_delta = halves(as_column, delta, 1)
    neg_prob = (neg_exp_ref[...] / denominator).astype(BF16)
    raw_pos = pos_delta * user_f / TAU
    pos_grad = (raw_pos - pos_unit * jnp.sum(pos_unit * raw_pos, axis=-1, keepdims=True)) / pos_len
    pos_grad = pos_grad.astype(BF16)
    unit_part = (pos_delta * pos_bf + dot(neg_prob, neg_bf)) / TAU
    first = core_here == 0
    held[:n, :] = jnp.where(first, unit_part[:n], unit_part[n:])
    held[n:, :] = jnp.where(first, unit_part[n:], unit_part[:n])
    copies = [
        pltpu.make_async_copy(held.at[pl.ds(n, n), :], other_part_ref, held_sems.at[0]),
        pltpu.make_async_copy(held.at[pl.ds(0, n), :], own_part_ref, held_sems.at[1]),
    ]
    for copy in copies:
        copy.start()
    part = chips // PIECES
    lead = lax.broadcasted_iota(jnp.int32, (part, n), 0) * CAP
    for i in range(PIECES):
        base = i * part * NBANK
        for core in range(2):
            row = slots[:, core * n : (core + 1) * n]
            for k in range(CAP):
                hot = jnp.where(row == lead + (i * part * CAP + k), 1.0, 0.0).astype(BF16)
                placed = dot(hot, pos_grad[core * n : (core + 1) * n])
                spread_slot(wide, base, core * CAP + k, placed)
        own = slice(i * part, (i + 1) * part)
        raw_neg = dot(neg_prob[:, own], users, (0, 0)) / TAU
        along = jnp.sum(neg_unit[own] * raw_neg, axis=-1, keepdims=True)
        spread_slot(wide, base, 2 * CAP, (raw_neg - neg_unit[own] * along) / neg_len[own])
        narrow[base : base + part * NBANK, :] = wide[base : base + part * NBANK, :].astype(BF16)
        copies.append(pltpu.make_async_copy(piece(narrow, i), piece(send_ref, i), sems.at[i]))
        copies[-1].start()
    for copy in copies:
        copy.wait()


def heads_back_kernel(
    loaded,
    place_ref,
    sess_ref,
    own_part_ref,
    other_part_ref,
    unit_ref,
    length_ref,
    w_out_ref,
    gate_ref,
    query_ref,
    hat_ref,
    scale_ref,
    keys_ref,
    values_ref,
    slope_ref,
    w_in_ref,
    own_ref,
    near_ref,
    far_ref,
    in_part_ref,
    user_grad_ref,
):
    n, width = hat_ref.shape
    loaded()
    attn_hat = hat_ref[...]
    user_unit = unit_ref[...]
    unit_grad = own_part_ref[...] + other_part_ref[...]
    user_grad = (
        unit_grad - user_unit * jnp.sum(user_unit * unit_grad, axis=-1, keepdims=True)
    ) / length_ref[:, 0:1]
    user_grad_ref[...] = user_grad
    gated_grad = dot(user_grad.astype(BF16), w_out_ref[...], (1, 1))
    hat_grad = gated_grad * gate_ref[...].astype(F32)
    upstream = norm_back(hat_grad, attn_hat, scale_ref[:, 0:1]).astype(BF16)
    scale = window_scale(place_ref, sess_ref, n)
    low = pair_masks(n)
    score_scale = 1.0 / math.sqrt(width // HEADS)
    query_grads = []
    for pair in range(HEADS // 2):
        first = pair * LANES
        lanes = slice(first, first + LANES)
        later = slice(width + first, width + first + LANES)
        queries = both_heads(query_ref[:, lanes], low)
        grads = both_heads(upstream[:, lanes], low)
        keys = keys_ref[:, lanes]
        scores = dot(queries, keys, (1, 1)) * score_scale
        weight_grad = dot(grads, values_ref[:, lanes], (1, 1))
        sigma = sigmoid(scores)
        weights = (scores * sigma * scale).astype(BF16)
        slope = sigma * (1.0 + scores * (1.0 - sigma))
        score_grad = (weight_grad * slope * (scale * score_scale)).astype(BF16)
        both = dot(score_grad, keys)
        query_grads.append(jnp.where(low, both[:n], both[n:]))
        key_grad = dot(score_grad, queries, (0, 0))
        value_grad = dot(weights, grads, (0, 0))
        far_ref[:, lanes] = value_grad[:n].astype(BF16)
        near_ref[:, lanes] = value_grad[n : 2 * n].astype(BF16)
        own_ref[:, lanes] = value_grad[2 * n :]
        far_ref[:, later] = key_grad[:n].astype(BF16)
        near_ref[:, later] = key_grad[n : 2 * n].astype(BF16)
        own_ref[:, later] = key_grad[2 * n :]
    gate_part = (gated_grad * attn_hat * slope_ref[:, :width]).astype(BF16)
    query_part = (jnp.concatenate(query_grads, axis=1) * slope_ref[:, width:]).astype(BF16)
    in_part_ref[...] = dot(gate_part, w_in_ref[:, :width], (1, 1)) + dot(
        query_part, w_in_ref[:, 2 * width : 3 * width], (1, 1)
    )


def last_kernel(
    items,
    loaded,
    returned_ref,
    near_ref,
    far_ref,
    asks_ref,
    own_grad_ref,
    slope_ref,
    in_part_ref,
    w_in_ref,
    gain_ref,
    hist_ref,
    user_grad_ref,
    table_grad_ref,
    history_grad_ref,
    wide,
    held,
    held_sem,
):
    width = hist_ref.shape[1]
    chips = asks_ref.shape[0] // 2
    rows = table_grad_ref.shape[0]
    wide[...] = returned_ref[...].astype(F32)
    loaded(1)
    asks = [jnp.transpose(by_chip(asks_ref, core, items).astype(F32)) for core in range(2)]
    row_id = lax.broadcasted_iota(jnp.int32, (rows, chips), 0).astype(F32)
    hots, parts = [], []
    for seat in range(SEATS):
        core, k = (0, CAP) if seat == 2 * CAP else divmod(seat, CAP)
        hots.append(jnp.where(asks[core][k : k + 1] == row_id, 1.0, 0.0).astype(BF16))
        parts.append(slot_rows(wide, 0, seat, chips))
    total = dot(jnp.concatenate(hots, axis=1), jnp.concatenate(parts, axis=0))
    held[...] = total.astype(BF16)
    copy = pltpu.make_async_copy(held, table_grad_ref, held_sem)
    copy.start()
    loaded()
    come = near_ref[...].astype(F32) + far_ref[...].astype(F32)
    proj_grad = ((own_grad_ref[...] + come) * slope_ref[...]).astype(BF16)
    in_grad = (
        in_part_ref[...]
        + dot(proj_grad[:, :width], w_in_ref[:, width : 2 * width], (1, 1))
        + dot(proj_grad[:, width:], w_in_ref[:, 3 * width :], (1, 1))
    )
    normed_x, scale_x = layer_stats(hist_ref[...].astype(F32))
    back = norm_back(in_grad * gain_ref[...], normed_x, scale_x)
    history_grad_ref[...] = (back + user_grad_ref[...]).astype(BF16)
    copy.wait()


def passed_along(shard, by):
    axes = ("z", "core")
    count = lax.axis_size(axes)
    pairs = [(i, i + by) for i in range(count) if 0 <= i + by < count]
    return lax.ppermute(shard, axes, pairs)


def swapped(shard):
    return lax.ppermute(shard, "core", [(0, 1), (1, 0)])


def on_device(history, ln_gain, w_in, w_out, item_table, sessions, pos_owner, pos_row, neg_rows):
    n, width = history.shape[1:]
    items = lax.axis_size("items")
    chips = lax.axis_size("z") * items
    owners = 2 * chips
    rows = item_table.shape[0]
    core = lax.axis_index("core")
    place = jnp.stack([2 * lax.axis_index("z") + core, core]).astype(jnp.int32)
    own = history[0]
    gain = ln_gain.reshape(1, width)
    neg_row = neg_rows.reshape(1, owners)

    def exchange(shard, axes, chunk):
        shape = shard.shape
        split = shard.reshape((-1,) + chunk)
        return lax.all_to_all(split, axes, split_axis=0, concat_axis=0, tiled=True).reshape(shape)

    def by_core(mine, other, axis):
        return jnp.where(
            core == 0,
            jnp.concatenate([mine, other], axis=axis),
            jnp.concatenate([other, mine], axis=axis),
        )

    ask, slot_row, slot_col = call(
        ask_kernel,
        [shaped((owners, LANES), jnp.int32), shaped((1, n), jnp.int32), shaped((n, 1), jnp.int32)],
        [VMEM, VMEM, VMEM],
        (pos_owner.reshape(1, n), pos_row, neg_row),
        2 * CAP * owners * n * LANES,
    )
    asks = exchange(ask, ("z", "core", "items"), (1, LANES))
    near = passed_along(own, 1)
    far = passed_along(own, 2)

    big = chips * NBANK
    staging = [
        pltpu.VMEM((big, LANES), BF16),
        pltpu.VMEM((big, LANES), F32),
        pltpu.SemaphoreType.DMA((PIECES,)),
    ]
    outward = [staging[1], staging[0], staging[2]]
    (served,) = call(
        functools.partial(serve_kernel, items),
        [shaped((big, LANES), BF16)],
        [VMEM, None],
        (asks, item_table),
        2 * SEATS * chips * rows * width,
        outward,
        mib=40,
        out_specs=(HBM,),
    )
    served, near, far = lax.optimization_barrier((served, near, far))
    fetched = exchange(served, ("z", "items"), (SEATS, CHUNKS, LANES))

    unit, length, attn_hat, scale_a, gate, query, slope_gq, slope_vk, keys, values, user = call(
        forward_kernel,
        [
            pltpu.HBM((n, width), F32),
            pltpu.HBM((n, LANES), F32),
            pltpu.HBM((n, width), F32),
            pltpu.HBM((n, LANES), F32),
            pltpu.HBM((n, width), BF16),
            pltpu.HBM((n, width), BF16),
            pltpu.HBM((n, 2 * width), F32),
            pltpu.HBM((n, 2 * width), F32),
            pltpu.HBM((3 * n, width), BF16),
            pltpu.HBM((3 * n, width), BF16),
            pltpu.HBM((n, width), BF16),
        ],
        [SMEM, SMEM, VMEM, VMEM] + [None] * 4,
        (place, sessions, far, near, own, gain, w_in, w_out),
        2 * n * width * width * 12,
        mib=40,
    )

    users = by_core(user, swapped(user), 0)
    slots = by_core(slot_row, swapped(slot_row), 1)
    neg_here = lax.dynamic_index_in_dim(
        neg_rows.reshape(chips // items, 2, items), core, axis=1, keepdims=False
    ).reshape(1, chips)
    stats, neg_exp, neg_kept, pos_kept = call(
        functools.partial(softmax_kernel, items),
        [
            shaped((2, 2 * n), F32),
            pltpu.HBM((2 * n, chips), F32),
            pltpu.HBM((chips, width), BF16),
            pltpu.HBM((2 * n, width), BF16),
        ],
        [SMEM, VMEM] + [None] * 3,
        (place, fetched, neg_here, slots, users),
        2 * n * width * owners * 3,
        [
            staging[1],
            pltpu.VMEM((chips + 2 * n, width), BF16),
            pltpu.VMEM((2 * n, chips), F32),
            pltpu.SemaphoreType.DMA((3,)),
        ],
        mib=40,
        out_specs=(VMEM, HBM, HBM, HBM),
    )
    send, own_part, other_part = call(
        functools.partial(send_kernel, items),
        [shaped((big, LANES), BF16), pltpu.HBM((n, width), F32), pltpu.HBM((n, width), F32)],
        [SMEM, VMEM, VMEM] + [None] * 5,
        (place, stats, swapped(stats), neg_kept, pos_kept, users, slots, neg_exp),
        2 * n * width * owners * 4,
        outward + [pltpu.VMEM((2 * n, width), F32), pltpu.SemaphoreType.DMA((2,))],
        mib=40,
        out_specs=(HBM, HBM, HBM),
    )
    returned = exchange(send, ("z", "items"), (SEATS, CHUNKS, LANES))

    own_grad, near_grad, far_grad, in_part, user_grad = call(
        heads_back_kernel,
        [
            shaped((n, 2 * width), F32),
            shaped((n, 2 * width), BF16),
            shaped((n, 2 * width), BF16),
            shaped((n, width), F32),
            shaped((n, width), F32),
        ],
        [SMEM, SMEM] + [None] * 13,
        (
            place,
            sessions,
            own_part,
            swapped(other_part),
            unit,
            length,
            w_out,
            gate,
            query,
            attn_hat,
            scale_a,
            keys,
            values,
            slope_gq,
            w_in,
        ),
        2 * n * width * width * 12,
    )
    near_back = passed_along(near_grad, -1)
    far_back = passed_along(far_grad, -2)
    table_grad, history_grad = call(
        functools.partial(last_kernel, items),
        [shaped((rows, width), BF16), shaped((n, width), BF16)],
        [VMEM] * 3 + [None] * 8,
        (
            returned,
            near_back,
            far_back,
            asks,
            own_grad,
            slope_vk,
            in_part,
            w_in,
            gain,
            own,
            user_grad,
        ),
        2 * SEATS * chips * rows * width,
        [staging[1], pltpu.VMEM((rows, width), BF16), pltpu.SemaphoreType.DMA(())],
        mib=40,
        out_specs=(HBM, VMEM),
    )
    return history_grad[None], table_grad


def solution(mesh):
    hist, items = mesh.shape["hist"], mesh.shape["items"]
    split = jax.sharding.Mesh(
        mesh.devices.reshape(hist // 2, 2, items), ("z", "core", "items")
    )
    return jax.shard_map(
        on_device,
        mesh=split,
        in_specs=(
            P("items", ("z", "core"), None),
            P(),
            P(),
            P(),
            P(("z", "core", "items"), None),
            P("items", None),
            P("items", ("z", "core"), None),
            P("items", ("z", "core")),
            P("items", None, None),
        ),
        out_specs=(P("items", ("z", "core"), None), P(("z", "core", "items"), None)),
        check_vma=False,
    )
```

```python
import functools
import math

import jax
import jax.numpy as jnp
from jax import lax
from jax.experimental import pallas as pl
from jax.experimental.pallas import tpu as pltpu
from jax.sharding import PartitionSpec as P

HEADS = 8
TAU = 0.05
CAP = 2
CHUNKS = 4
LANES = 128
SEATS = 2 * CAP + 1
PIECES = 2
NBANK = SEATS * CHUNKS
F32 = jnp.float32
BF16 = jnp.bfloat16
VMEM = pl.BlockSpec(memory_space=pltpu.VMEM)
HBM = pl.BlockSpec(memory_space=pltpu.HBM)
SMEM = pl.BlockSpec(memory_space=pltpu.SMEM)


def call(kernel, outs, in_specs, args, flops, scratch=(), mib=60, out_specs=None):
    moved = sum(a.size * a.dtype.itemsize for a in args) + sum(
        math.prod(o.shape) * o.dtype.itemsize for o in outs
    )
    pinned = [i for i, spec in enumerate(in_specs) if spec is None]
    scratch = list(scratch)

    def body(*refs):
        refs = list(refs)
        count = len(pinned)
        if not count:
            return kernel(*refs)
        held, sems = refs[-count - 1 : -1], refs[-1]
        refs = refs[: -count - 1]
        copies = []
        for j, i in enumerate(pinned):
            copies.append(pltpu.make_async_copy(refs[i], held[j], sems.at[j]))
            copies[-1].start()
            refs[i] = held[j]

        waiting = list(copies)

        def loaded(count=len(copies)):
            for copy in waiting[:count]:
                copy.wait()
            del waiting[:count]

        return kernel(loaded, *refs)

    if pinned:
        scratch += [pltpu.VMEM(args[i].shape, args[i].dtype) for i in pinned]
        scratch.append(pltpu.SemaphoreType.DMA((len(pinned),)))
    return pl.pallas_call(
        body,
        out_shape=tuple(outs),
        in_specs=[HBM if spec is None else spec for spec in in_specs],
        out_specs=out_specs or tuple(VMEM for _ in outs),
        scratch_shapes=scratch,
        compiler_params=pltpu.CompilerParams(vmem_limit_bytes=mib * 2**20),
        cost_estimate=pl.CostEstimate(flops=flops, bytes_accessed=moved, transcendentals=0),
    )(
        *[
            pltpu.with_memory_space_constraint(a, pltpu.HBM) if spec is None else a
            for a, spec in zip(args, in_specs)
        ]
    )


def shaped(shape, dtype):
    return jax.ShapeDtypeStruct(shape, dtype)


def dot(a, b, contract=(1, 0)):
    return lax.dot_general(
        a, b, (((contract[0],), (contract[1],)), ((), ())), preferred_element_type=F32
    )


def layer_stats(values):
    center = values - jnp.mean(values, axis=-1, keepdims=True)
    scale_inv = lax.rsqrt(jnp.mean(center * center, axis=-1, keepdims=True) + 1e-05)
    return center * scale_inv, scale_inv


def norm_back(upstream, normed, scale_inv):
    return scale_inv * (
        upstream
        - jnp.mean(upstream, axis=-1, keepdims=True)
        - normed * jnp.mean(upstream * normed, axis=-1, keepdims=True)
    )


def item_norm(rows_in):
    values = rows_in.astype(F32)
    lengths = jnp.sqrt(jnp.sum(values * values, axis=-1, keepdims=True) + 1e-06)
    return values / lengths, lengths


def sigmoid(value):
    return 1.0 / (1.0 + jnp.exp(-value))


def slots_kernel(owner_ref, row_ref, out_ref):
    n = owner_ref.shape[1]
    lead = lax.broadcasted_iota(jnp.int32, (n, n), 0)
    lane = lax.broadcasted_iota(jnp.int32, (n, n), 1)
    owner_r = jnp.broadcast_to(owner_ref[...].astype(F32), (n, n))
    owner_c = as_column(owner_ref[...].astype(F32))
    before = jnp.where((owner_r == owner_c) & (lead < lane), 1.0, 0.0)
    rank = jnp.sum(before, axis=0, keepdims=True)
    out_ref[0:1, :] = owner_ref[...] * CAP + rank.astype(jnp.int32)
    out_ref[1:2, :] = row_ref[...]


def ask_kernel(
    items, loaded, place_ref, mine_ref, other_ref, neg_ref, ask_ref, slots_ref, neg_row_ref
):
    n = mine_ref.shape[1]
    chips = ask_ref.shape[0]
    bits = items.bit_length() - 1
    core_here = place_ref[1]
    first = core_here == 0
    lane = lax.broadcasted_iota(jnp.int32, (n, LANES), 1)
    by_owner = lax.broadcasted_iota(jnp.int32, (chips, n), 0) * CAP
    loaded()
    asked = None
    for core in range(2):
        own, sibling = mine_ref[...], other_ref[...]
        named = jnp.where(first, own, sibling) if core == 0 else jnp.where(first, sibling, own)
        slots_ref[:, core * n : (core + 1) * n] = named[0:1, :]
        slots = local_slots(named[0:1, :], core_here, items)
        rows = as_column(named[1:2, :].astype(F32))
        for k in range(CAP):
            hot = jnp.where(slots == by_owner + k, 1.0, 0.0).astype(BF16)
            part = dot(hot, jnp.where(lane == core * CAP + k, rows, 0.0).astype(BF16))
            asked = part if asked is None else asked + part
    neg_all = jnp.broadcast_to(neg_ref[...].astype(F32), (n, 2 * chips))
    at = lax.broadcasted_iota(jnp.int32, (n, 2 * chips), 0)
    owner = lax.broadcasted_iota(jnp.int32, (n, 2 * chips), 1)
    for c in range(chips // n):
        own = slice(c * n, (c + 1) * n)
        local = at + c * n
        wanted = ((local >> bits) << (bits + 1)) + (core_here << bits) + (local & (items - 1))
        negative = jnp.sum(jnp.where(owner == wanted, neg_all, 0.0), axis=1, keepdims=True)
        ask_ref[own, :] = jnp.where(lane == 2 * CAP, negative, asked[own]).astype(jnp.int32)
        neg_row_ref[:, own] = as_row(negative).astype(jnp.int32)


def spread_slot(wide, base, k, rows):
    for c in range(CHUNKS):
        wide[pl.ds(base + k * CHUNKS + c, rows.shape[0], stride=NBANK), :] = rows[
            :, c * LANES : (c + 1) * LANES
        ]


def slot_rows(wide, base, k, count):
    return jnp.concatenate(
        [wide[pl.ds(base + k * CHUNKS + c, count, stride=NBANK), :] for c in range(CHUNKS)], axis=1
    ).astype(BF16)


def piece(ref, i):
    size = ref.shape[0] // PIECES
    return ref.at[pl.ds(i * size, size), :]


def serve_kernel(loaded, asks_ref, table_ref, out_ref, wide, narrow, sems):
    chips = asks_ref.shape[0]
    part = chips // PIECES
    rows = table_ref.shape[0]
    loaded()
    table = table_ref[...]
    row_id = lax.broadcasted_iota(jnp.int32, (part, rows), 1)
    copies = []
    for i in range(PIECES):
        base = i * part * NBANK
        for seat in range(SEATS):
            asked = asks_ref[i * part : (i + 1) * part, seat : seat + 1]
            hot = jnp.where(asked == row_id, 1.0, 0.0).astype(BF16)
            spread_slot(wide, base, seat, dot(hot, table))
        narrow[base : base + part * NBANK, :] = wide[base : base + part * NBANK, :].astype(BF16)
        copies.append(pltpu.make_async_copy(piece(narrow, i), piece(out_ref, i), sems.at[i]))
        copies[-1].start()
    for copy in copies:
        copy.wait()


def pair_masks(n):
    lane = lax.broadcasted_iota(jnp.int32, (n, LANES), 1)
    return lane < (LANES // 2)


def both_heads(part, low):
    zero = jnp.zeros_like(part)
    return jnp.concatenate([jnp.where(low, part, zero), jnp.where(low, zero, part)], axis=0)


def same_before(place_ref, sess_ref, ahead):
    block = place_ref[0] + ahead
    inside = block < sess_ref.shape[1]
    block = jnp.minimum(block, sess_ref.shape[1] - 1)
    here = sess_ref[0, block]
    near = inside & (block >= 1) & (sess_ref[0, jnp.maximum(block - 1, 0)] == here)
    far = inside & (block >= 2) & (sess_ref[0, jnp.maximum(block - 2, 0)] == here)
    return jnp.where(near, 1, 0), jnp.where(far, 1, 0)


def window_scale(place_ref, sess_ref, n):
    near, far = same_before(place_ref, sess_ref, 0)
    place = lax.broadcasted_iota(jnp.int32, (n, 3 * n), 0)
    lane = lax.broadcasted_iota(jnp.int32, (n, 3 * n), 1)
    count = place + 1 + n * (near + far)
    allowed = jnp.where(
        lane < n, far, jnp.where(lane < 2 * n, near, jnp.where(lane - 2 * n <= place, 1, 0))
    )
    scale = allowed.astype(F32) * (1.0 / count.astype(F32))
    return jnp.concatenate([scale, scale], axis=0)


def forward_kernel(
    loaded,
    place_ref,
    sess_ref,
    far_ref,
    near_ref,
    own_ref,
    gain_ref,
    w_in_ref,
    w_out_ref,
    unit_ref,
    length_ref,
    hat_ref,
    scale_ref,
    gate_ref,
    query_ref,
    slope_gq_ref,
    slope_vk_ref,
    keys_ref,
    values_ref,
    user_ref,
):
    n, width = own_ref.shape
    loaded()
    gain = gain_ref[...]
    hist_f = own_ref[...].astype(F32)

    def normed_in(values):
        return (layer_stats(values)[0] * gain).astype(BF16)

    projected = dot(normed_in(hist_f), w_in_ref[...])
    sigma = sigmoid(projected)
    slope = sigma * (1.0 + projected * (1.0 - sigma))
    slope_gq_ref[:, :width] = slope[:, :width]
    slope_vk_ref[:, :width] = slope[:, width : 2 * width]
    slope_gq_ref[:, width:] = slope[:, 2 * width : 3 * width]
    slope_vk_ref[:, width:] = slope[:, 3 * width :]
    act = (projected * sigma).astype(BF16)
    gate_ref[...] = act[:, :width]
    query_ref[...] = act[:, 2 * width : 3 * width]
    before = jnp.concatenate(
        [normed_in(far_ref[...].astype(F32)), normed_in(near_ref[...].astype(F32))], axis=0
    )
    values_before = dot(before, w_in_ref[:, width : 2 * width])
    keys_before = dot(before, w_in_ref[:, 3 * width :])
    values_ref[: 2 * n, :] = (values_before * sigmoid(values_before)).astype(BF16)
    keys_ref[: 2 * n, :] = (keys_before * sigmoid(keys_before)).astype(BF16)
    values_ref[2 * n :, :] = act[:, width : 2 * width]
    keys_ref[2 * n :, :] = act[:, 3 * width :]
    scale = window_scale(place_ref, sess_ref, n)
    low = pair_masks(n)
    score_scale = 1.0 / math.sqrt(width // HEADS)
    attended = []
    for pair in range(HEADS // 2):
        lanes = slice(pair * LANES, (pair + 1) * LANES)
        queries = both_heads(act[:, 2 * width + pair * LANES : 2 * width + (pair + 1) * LANES], low)
        scores = dot(queries, keys_ref[:, lanes], (1, 1)) * score_scale
        weights = (scores * sigmoid(scores) * scale).astype(BF16)
        both = dot(weights, values_ref[:, lanes])
        attended.append(jnp.where(low, both[:n], both[n:]))
    attn_hat, scale_a = layer_stats(jnp.concatenate(attended, axis=1))
    hat_ref[...] = attn_hat
    scale_ref[...] = jnp.broadcast_to(scale_a, scale_ref.shape)
    gated = (attn_hat * act[:, :width].astype(F32)).astype(BF16)
    user_out = dot(gated, w_out_ref[...]) + hist_f
    user_len = jnp.sqrt(jnp.sum(user_out * user_out, axis=-1, keepdims=True) + 1e-06)
    user_unit = user_out / user_len
    unit_ref[...] = user_unit
    user_ref[...] = user_unit.astype(BF16)
    length_ref[...] = jnp.broadcast_to(user_len, length_ref.shape)


def local_slots(slots, core, items):
    bits = items.bit_length() - 1
    owner = slots >> 1
    local = ((owner >> (bits + 1)) << bits) + (owner & (items - 1))
    return jnp.where(((owner >> bits) & 1) == core, local * CAP + (slots & 1), -1)


def as_column(row):
    n = row.shape[1]
    lead = lax.broadcasted_iota(jnp.int32, (n, n), 0)
    lane = lax.broadcasted_iota(jnp.int32, (n, n), 1)
    spread = jnp.broadcast_to(row, (n, n))
    return jnp.sum(jnp.where(lead == lane, spread, 0.0), axis=1, keepdims=True)


def as_row(column):
    n = column.shape[0]
    lead = lax.broadcasted_iota(jnp.int32, (n, n), 0)
    lane = lax.broadcasted_iota(jnp.int32, (n, n), 1)
    return jnp.sum(jnp.where(lead == lane, column, 0.0), axis=0, keepdims=True)


def halves(convert, values, axis):
    n = values.shape[axis] // 2
    first, second = (values[:, :n], values[:, n:]) if axis else (values[:n], values[n:])
    return jnp.concatenate([convert(first), convert(second)], axis=1 - axis)


def softmax_kernel(
    items,
    loaded,
    place_ref,
    fetched_ref,
    neg_row_ref,
    slots_ref,
    users_ref,
    stats_ref,
    neg_exp_ref,
    neg_rows_ref,
    pos_rows_ref,
    wide,
    held_rows,
    held_exp,
    held_sems,
):
    chips = neg_row_ref.shape[1]
    n = users_ref.shape[0] // 2
    wide[...] = fetched_ref[...].astype(F32)
    neg_rows = slot_rows(wide, 0, 2 * CAP, chips)
    held_rows[:chips, :] = neg_rows
    copies = [
        pltpu.make_async_copy(held_rows.at[pl.ds(0, chips), :], neg_rows_ref, held_sems.at[0]),
        pltpu.make_async_copy(held_exp, neg_exp_ref, held_sems.at[1]),
        pltpu.make_async_copy(
            held_rows.at[pl.ds(chips, 2 * n), :], pos_rows_ref, held_sems.at[2]
        ),
    ]
    copies[0].start()
    neg_bf = item_norm(neg_rows)[0].astype(BF16)
    loaded()
    users = users_ref[...]
    neg_row = neg_row_ref[...] + 1
    exponent = jnp.zeros(neg_row.shape, F32)
    for level in range(1, 8):
        exponent = exponent + jnp.where(neg_row >= (1 << level), 1.0, 0.0)
    shift = math.log(8) + exponent * math.log(2.0)
    neg_exp = jnp.exp(dot(users, neg_bf, (1, 1)) / TAU + shift)
    held_exp[...] = neg_exp
    copies[1].start()
    slots = local_slots(slots_ref[...], place_ref[1], items)
    lane = lax.broadcasted_iota(jnp.int32, (n, chips), 1) * CAP
    pos_rows, here = [], []
    for core in range(2):
        column = as_column(slots[:, core * n : (core + 1) * n].astype(F32)).astype(jnp.int32)
        here.append(jnp.where(column >= 0, 1.0, 0.0))
        hots = [jnp.where(column == lane + k, 1.0, 0.0).astype(BF16) for k in range(CAP)]
        rows = [slot_rows(wide, 0, core * CAP + k, chips) for k in range(CAP)]
        pos_rows.append(dot(jnp.concatenate(hots, axis=1), jnp.concatenate(rows, axis=0)))
    pos_rows = jnp.concatenate(pos_rows, axis=0)
    held_rows[chips:, :] = pos_rows.astype(BF16)
    copies[2].start()
    pos_bf = item_norm(pos_rows)[0].astype(BF16).astype(F32)
    along = jnp.sum(users.astype(F32) * pos_bf, axis=-1, keepdims=True)
    pos_exp = jnp.concatenate(here, axis=0) * jnp.exp(along / TAU)
    total = pos_exp + jnp.sum(neg_exp, axis=-1, keepdims=True)
    stats_ref[0:1, :] = halves(as_row, total, 0)
    stats_ref[1:2, :] = halves(as_row, pos_exp, 0)
    for copy in copies:
        copy.wait()


def send_kernel(
    items,
    loaded,
    place_ref,
    stats_ref,
    stats_other_ref,
    neg_rows_ref,
    pos_rows_ref,
    users_ref,
    slots_ref,
    neg_exp_ref,
    send_ref,
    own_part_ref,
    other_part_ref,
    wide,
    narrow,
    sems,
    held,
    held_sems,
):
    chips = neg_rows_ref.shape[0]
    n = users_ref.shape[0] // 2
    core_here = place_ref[1]
    loaded(2)
    neg_unit, neg_len = item_norm(neg_rows_ref[...])
    neg_bf = neg_unit.astype(BF16)
    pos_unit, pos_len = item_norm(pos_rows_ref[...])
    pos_bf = pos_unit.astype(BF16).astype(F32)
    loaded()
    users = users_ref[...]
    user_f = users.astype(F32)
    slots = local_slots(slots_ref[...], core_here, items)
    total = stats_ref[0:1, :] + stats_other_ref[0:1, :]
    denominator = halves(as_column, total, 1)
    delta = jnp.where(slots >= 0, stats_ref[1:2, :] / total - 1.0, 0.0)
    pos_delta = halves(as_column, delta, 1)
    neg_prob = (neg_exp_ref[...] / denominator).astype(BF16)
    raw_pos = pos_delta * user_f / TAU
    pos_grad = (raw_pos - pos_unit * jnp.sum(pos_unit * raw_pos, axis=-1, keepdims=True)) / pos_len
    pos_grad = pos_grad.astype(BF16)
    unit_part = (pos_delta * pos_bf + dot(neg_prob, neg_bf)) / TAU
    first = core_here == 0
    held[:n, :] = jnp.where(first, unit_part[:n], unit_part[n:])
    held[n:, :] = jnp.where(first, unit_part[n:], unit_part[:n])
    copies = [
        pltpu.make_async_copy(held.at[pl.ds(n, n), :], other_part_ref, held_sems.at[0]),
        pltpu.make_async_copy(held.at[pl.ds(0, n), :], own_part_ref, held_sems.at[1]),
    ]
    for copy in copies:
        copy.start()
    part = chips // PIECES
    lead = lax.broadcasted_iota(jnp.int32, (part, n), 0) * CAP
    for i in range(PIECES):
        base = i * part * NBANK
        for core in range(2):
            row = slots[:, core * n : (core + 1) * n]
            for k in range(CAP):
                hot = jnp.where(row == lead + (i * part * CAP + k), 1.0, 0.0).astype(BF16)
                placed = dot(hot, pos_grad[core * n : (core + 1) * n])
                spread_slot(wide, base, core * CAP + k, placed)
        own = slice(i * part, (i + 1) * part)
        raw_neg = dot(neg_prob[:, own], users, (0, 0)) / TAU
        along = jnp.sum(neg_unit[own] * raw_neg, axis=-1, keepdims=True)
        spread_slot(wide, base, 2 * CAP, (raw_neg - neg_unit[own] * along) / neg_len[own])
        narrow[base : base + part * NBANK, :] = wide[base : base + part * NBANK, :].astype(BF16)
        copies.append(pltpu.make_async_copy(piece(narrow, i), piece(send_ref, i), sems.at[i]))
        copies[-1].start()
    for copy in copies:
        copy.wait()


def heads_back_kernel(
    loaded,
    place_ref,
    sess_ref,
    own_part_ref,
    other_part_ref,
    unit_ref,
    length_ref,
    w_out_ref,
    gate_ref,
    query_ref,
    hat_ref,
    scale_ref,
    keys_ref,
    values_ref,
    slope_ref,
    w_in_ref,
    own_ref,
    near_ref,
    far_ref,
    in_part_ref,
    user_grad_ref,
):
    n, width = hat_ref.shape
    loaded()
    attn_hat = hat_ref[...]
    user_unit = unit_ref[...]
    unit_grad = own_part_ref[...] + other_part_ref[...]
    user_grad = (
        unit_grad - user_unit * jnp.sum(user_unit * unit_grad, axis=-1, keepdims=True)
    ) / length_ref[:, 0:1]
    user_grad_ref[...] = user_grad
    gated_grad = dot(user_grad.astype(BF16), w_out_ref[...], (1, 1))
    hat_grad = gated_grad * gate_ref[...].astype(F32)
    upstream = norm_back(hat_grad, attn_hat, scale_ref[:, 0:1]).astype(BF16)
    scale = window_scale(place_ref, sess_ref, n)
    low = pair_masks(n)
    score_scale = 1.0 / math.sqrt(width // HEADS)
    query_grads = []
    for pair in range(HEADS // 2):
        first = pair * LANES
        lanes = slice(first, first + LANES)
        later = slice(width + first, width + first + LANES)
        queries = both_heads(query_ref[:, lanes], low)
        grads = both_heads(upstream[:, lanes], low)
        keys = keys_ref[:, lanes]
        scores = dot(queries, keys, (1, 1)) * score_scale
        weight_grad = dot(grads, values_ref[:, lanes], (1, 1))
        sigma = sigmoid(scores)
        weights = (scores * sigma * scale).astype(BF16)
        slope = sigma * (1.0 + scores * (1.0 - sigma))
        score_grad = (weight_grad * slope * (scale * score_scale)).astype(BF16)
        both = dot(score_grad, keys)
        query_grads.append(jnp.where(low, both[:n], both[n:]))
        key_grad = dot(score_grad, queries, (0, 0))
        value_grad = dot(weights, grads, (0, 0))
        far_ref[:, lanes] = value_grad[:n].astype(BF16)
        near_ref[:, lanes] = value_grad[n : 2 * n].astype(BF16)
        own_ref[:, lanes] = value_grad[2 * n :]
        far_ref[:, later] = key_grad[:n].astype(BF16)
        near_ref[:, later] = key_grad[n : 2 * n].astype(BF16)
        own_ref[:, later] = key_grad[2 * n :]
    gate_part = (gated_grad * attn_hat * slope_ref[:, :width]).astype(BF16)
    query_part = (jnp.concatenate(query_grads, axis=1) * slope_ref[:, width:]).astype(BF16)
    in_part_ref[...] = dot(gate_part, w_in_ref[:, :width], (1, 1)) + dot(
        query_part, w_in_ref[:, 2 * width : 3 * width], (1, 1)
    )


def last_kernel(
    loaded,
    returned_ref,
    near_ref,
    far_ref,
    asks_ref,
    own_grad_ref,
    slope_ref,
    in_part_ref,
    w_in_ref,
    gain_ref,
    hist_ref,
    user_grad_ref,
    table_grad_ref,
    history_grad_ref,
    wide,
    held,
    held_sem,
):
    width = hist_ref.shape[1]
    chips = asks_ref.shape[0]
    rows = table_grad_ref.shape[0]
    wide[...] = returned_ref[...].astype(F32)
    loaded(1)
    asks = jnp.transpose(asks_ref[...].astype(F32))
    row_id = lax.broadcasted_iota(jnp.int32, (rows, chips), 0).astype(F32)
    hots, parts = [], []
    for seat in range(SEATS):
        hots.append(jnp.where(asks[seat : seat + 1] == row_id, 1.0, 0.0).astype(BF16))
        parts.append(slot_rows(wide, 0, seat, chips))
    total = dot(jnp.concatenate(hots, axis=1), jnp.concatenate(parts, axis=0))
    held[...] = total.astype(BF16)
    copy = pltpu.make_async_copy(held, table_grad_ref, held_sem)
    copy.start()
    loaded()
    come = near_ref[...].astype(F32) + far_ref[...].astype(F32)
    proj_grad = ((own_grad_ref[...] + come) * slope_ref[...]).astype(BF16)
    in_grad = (
        in_part_ref[...]
        + dot(proj_grad[:, :width], w_in_ref[:, width : 2 * width], (1, 1))
        + dot(proj_grad[:, width:], w_in_ref[:, 3 * width :], (1, 1))
    )
    normed_x, scale_x = layer_stats(hist_ref[...].astype(F32))
    back = norm_back(in_grad * gain_ref[...], normed_x, scale_x)
    history_grad_ref[...] = (back + user_grad_ref[...]).astype(BF16)
    copy.wait()


def passed_along(shard, by):
    axes = ("z", "core")
    count = lax.axis_size(axes)
    pairs = [(i, i + by) for i in range(count) if 0 <= i + by < count]
    return lax.ppermute(shard, axes, pairs)


def swapped(shard):
    return lax.ppermute(shard, "core", [(0, 1), (1, 0)])


def on_device(history, ln_gain, w_in, w_out, item_table, sessions, pos_owner, pos_row, neg_rows):
    n, width = history.shape[1:]
    items = lax.axis_size("items")
    chips = lax.axis_size("z") * items
    owners = 2 * chips
    rows = item_table.shape[0]
    core = lax.axis_index("core")
    place = jnp.stack([2 * lax.axis_index("z") + core, core]).astype(jnp.int32)
    own = history[0]
    gain = ln_gain.reshape(1, width)
    neg_row = neg_rows.reshape(1, owners)

    def exchange(shard, axes, chunk):
        shape = shard.shape
        split = shard.reshape((-1,) + chunk)
        return lax.all_to_all(split, axes, split_axis=0, concat_axis=0, tiled=True).reshape(shape)

    def by_core(mine, other, axis):
        return jnp.where(
            core == 0,
            jnp.concatenate([mine, other], axis=axis),
            jnp.concatenate([other, mine], axis=axis),
        )

    (mine,) = call(
        slots_kernel,
        [shaped((2, n), jnp.int32)],
        [VMEM, VMEM],
        (pos_owner.reshape(1, n), pos_row),
        n * n,
    )
    ask, slots, neg_here = call(
        functools.partial(ask_kernel, items),
        [
            pltpu.HBM((chips, LANES), jnp.int32),
            pltpu.HBM((1, 2 * n), jnp.int32),
            pltpu.HBM((1, chips), jnp.int32),
        ],
        [SMEM, None, VMEM, None],
        (place, mine, swapped(mine), neg_row),
        4 * CAP * chips * n * LANES,
        mib=40,
    )
    asks = exchange(ask, ("z", "items"), (1, LANES))
    near = passed_along(own, 1)
    far = passed_along(own, 2)

    big = chips * NBANK
    staging = [
        pltpu.VMEM((big, LANES), BF16),
        pltpu.VMEM((big, LANES), F32),
        pltpu.SemaphoreType.DMA((PIECES,)),
    ]
    outward = [staging[1], staging[0], staging[2]]
    (served,) = call(
        serve_kernel,
        [shaped((big, LANES), BF16)],
        [VMEM, None],
        (asks, item_table),
        2 * SEATS * chips * rows * width,
        outward,
        mib=40,
        out_specs=(HBM,),
    )
    served, near, far = lax.optimization_barrier((served, near, far))
    fetched = exchange(served, ("z", "items"), (SEATS, CHUNKS, LANES))

    unit, length, attn_hat, scale_a, gate, query, slope_gq, slope_vk, keys, values, user = call(
        forward_kernel,
        [
            pltpu.HBM((n, width), F32),
            pltpu.HBM((n, LANES), F32),
            pltpu.HBM((n, width), F32),
            pltpu.HBM((n, LANES), F32),
            pltpu.HBM((n, width), BF16),
            pltpu.HBM((n, width), BF16),
            pltpu.HBM((n, 2 * width), F32),
            pltpu.HBM((n, 2 * width), F32),
            pltpu.HBM((3 * n, width), BF16),
            pltpu.HBM((3 * n, width), BF16),
            pltpu.HBM((n, width), BF16),
        ],
        [SMEM, SMEM, VMEM, VMEM] + [None] * 4,
        (place, sessions, far, near, own, gain, w_in, w_out),
        2 * n * width * width * 12,
        mib=40,
    )

    users = by_core(user, swapped(user), 0)
    stats, neg_exp, neg_kept, pos_kept = call(
        functools.partial(softmax_kernel, items),
        [
            shaped((2, 2 * n), F32),
            pltpu.HBM((2 * n, chips), F32),
            pltpu.HBM((chips, width), BF16),
            pltpu.HBM((2 * n, width), BF16),
        ],
        [SMEM, VMEM] + [None] * 3,
        (place, fetched, neg_here, slots, users),
        2 * n * width * owners * 3,
        [
            staging[1],
            pltpu.VMEM((chips + 2 * n, width), BF16),
            pltpu.VMEM((2 * n, chips), F32),
            pltpu.SemaphoreType.DMA((3,)),
        ],
        mib=40,
        out_specs=(VMEM, HBM, HBM, HBM),
    )
    send, own_part, other_part = call(
        functools.partial(send_kernel, items),
        [shaped((big, LANES), BF16), pltpu.HBM((n, width), F32), pltpu.HBM((n, width), F32)],
        [SMEM, VMEM, VMEM] + [None] * 5,
        (place, stats, swapped(stats), neg_kept, pos_kept, users, slots, neg_exp),
        2 * n * width * owners * 4,
        outward + [pltpu.VMEM((2 * n, width), F32), pltpu.SemaphoreType.DMA((2,))],
        mib=40,
        out_specs=(HBM, HBM, HBM),
    )
    returned = exchange(send, ("z", "items"), (SEATS, CHUNKS, LANES))

    own_grad, near_grad, far_grad, in_part, user_grad = call(
        heads_back_kernel,
        [
            shaped((n, 2 * width), F32),
            shaped((n, 2 * width), BF16),
            shaped((n, 2 * width), BF16),
            shaped((n, width), F32),
            shaped((n, width), F32),
        ],
        [SMEM, SMEM] + [None] * 13,
        (
            place,
            sessions,
            own_part,
            swapped(other_part),
            unit,
            length,
            w_out,
            gate,
            query,
            attn_hat,
            scale_a,
            keys,
            values,
            slope_gq,
            w_in,
        ),
        2 * n * width * width * 12,
    )
    near_back = passed_along(near_grad, -1)
    far_back = passed_along(far_grad, -2)
    table_grad, history_grad = call(
        last_kernel,
        [shaped((rows, width), BF16), shaped((n, width), BF16)],
        [VMEM] * 3 + [None] * 8,
        (
            returned,
            near_back,
            far_back,
            asks,
            own_grad,
            slope_vk,
            in_part,
            w_in,
            gain,
            own,
            user_grad,
        ),
        2 * SEATS * chips * rows * width,
        [staging[1], pltpu.VMEM((rows, width), BF16), pltpu.SemaphoreType.DMA(())],
        mib=40,
        out_specs=(HBM, VMEM),
    )
    return history_grad[None], table_grad


def solution(mesh):
    hist, items = mesh.shape["hist"], mesh.shape["items"]
    split = jax.sharding.Mesh(
        mesh.devices.reshape(hist // 2, 2, items), ("z", "core", "items")
    )
    return jax.shard_map(
        on_device,
        mesh=split,
        in_specs=(
            P("items", ("z", "core"), None),
            P(),
            P(),
            P(),
            P(("z", "core", "items"), None),
            P("items", None),
            P("items", ("z", "core"), None),
            P("items", ("z", "core")),
            P("items", None, None),
        ),
        out_specs=(P("items", ("z", "core"), None), P(("z", "core", "items"), None)),
        check_vma=False,
    )
```

```python
import functools
import math

import jax
import jax.numpy as jnp
from jax import lax
from jax.experimental import pallas as pl
from jax.experimental.pallas import tpu as pltpu
from jax.sharding import PartitionSpec as P

HEADS = 8
TAU = 0.05
CAP = 2
CHUNKS = 4
LANES = 128
SLOTS = CAP + 1
SEATS = 2 * CAP + 1
PIECES = 2
NBANK = SEATS * CHUNKS
F32 = jnp.float32
BF16 = jnp.bfloat16
VMEM = pl.BlockSpec(memory_space=pltpu.VMEM)
HBM = pl.BlockSpec(memory_space=pltpu.HBM)
SMEM = pl.BlockSpec(memory_space=pltpu.SMEM)


def call(kernel, outs, in_specs, args, flops, scratch=(), mib=60, out_specs=None):
    moved = sum(a.size * a.dtype.itemsize for a in args) + sum(
        math.prod(o.shape) * o.dtype.itemsize for o in outs
    )
    pinned = [i for i, spec in enumerate(in_specs) if spec is None]
    scratch = list(scratch)

    def body(*refs):
        refs = list(refs)
        count = len(pinned)
        if not count:
            return kernel(*refs)
        held, sems = refs[-count - 1 : -1], refs[-1]
        refs = refs[: -count - 1]
        copies = []
        for j, i in enumerate(pinned):
            copies.append(pltpu.make_async_copy(refs[i], held[j], sems.at[j]))
            copies[-1].start()
            refs[i] = held[j]

        waiting = list(copies)

        def loaded(count=len(copies)):
            for copy in waiting[:count]:
                copy.wait()
            del waiting[:count]

        return kernel(loaded, *refs)

    if pinned:
        scratch += [pltpu.VMEM(args[i].shape, args[i].dtype) for i in pinned]
        scratch.append(pltpu.SemaphoreType.DMA((len(pinned),)))
    return pl.pallas_call(
        body,
        out_shape=tuple(outs),
        in_specs=[HBM if spec is None else spec for spec in in_specs],
        out_specs=out_specs or tuple(VMEM for _ in outs),
        scratch_shapes=scratch,
        compiler_params=pltpu.CompilerParams(vmem_limit_bytes=mib * 2**20),
        cost_estimate=pl.CostEstimate(flops=flops, bytes_accessed=moved, transcendentals=0),
    )(
        *[
            pltpu.with_memory_space_constraint(a, pltpu.HBM) if spec is None else a
            for a, spec in zip(args, in_specs)
        ]
    )


def shaped(shape, dtype):
    return jax.ShapeDtypeStruct(shape, dtype)


def dot(a, b, contract=(1, 0)):
    return lax.dot_general(
        a, b, (((contract[0],), (contract[1],)), ((), ())), preferred_element_type=F32
    )


def layer_stats(values):
    center = values - jnp.mean(values, axis=-1, keepdims=True)
    scale_inv = lax.rsqrt(jnp.mean(center * center, axis=-1, keepdims=True) + 1e-05)
    return center * scale_inv, scale_inv


def norm_back(upstream, normed, scale_inv):
    return scale_inv * (
        upstream
        - jnp.mean(upstream, axis=-1, keepdims=True)
        - normed * jnp.mean(upstream * normed, axis=-1, keepdims=True)
    )


def item_norm(rows_in):
    values = rows_in.astype(F32)
    lengths = jnp.sqrt(jnp.sum(values * values, axis=-1, keepdims=True) + 1e-06)
    return values / lengths, lengths


def sigmoid(value):
    return 1.0 / (1.0 + jnp.exp(-value))


def ask_kernel(owner_ref, row_ref, neg_ref, ask_ref, slot_row_ref, slot_col_ref):
    n = owner_ref.shape[1]
    owners = ask_ref.shape[0]
    lead = lax.broadcasted_iota(jnp.int32, (n, n), 0)
    lane = lax.broadcasted_iota(jnp.int32, (n, n), 1)

    def column(row):
        spread = jnp.broadcast_to(row.astype(F32), (n, n))
        return jnp.sum(jnp.where(lead == lane, spread, 0.0), axis=1, keepdims=True)

    owner_r = jnp.broadcast_to(owner_ref[...].astype(F32), (n, n))
    owner_c = column(owner_ref[...])
    same = owner_r == owner_c
    rank_r = jnp.sum(jnp.where(same & (lead < lane), 1.0, 0.0), axis=0, keepdims=True)
    rank_c = jnp.sum(jnp.where(same & (lane < lead), 1.0, 0.0), axis=1, keepdims=True)
    slot_r = owner_ref[...] * CAP + rank_r.astype(jnp.int32)
    slot_row_ref[...] = slot_r
    slot_col_ref[...] = (owner_c * CAP + rank_c).astype(jnp.int32)
    rows = jnp.broadcast_to(column(row_ref[...]), (n, LANES))
    by_owner = lax.broadcasted_iota(jnp.int32, (owners, n), 0) * CAP
    asked = None
    for k in range(CAP):
        hot = jnp.where(slot_r == by_owner + k, 1.0, 0.0).astype(BF16)
        part = dot(hot, jnp.where(lane == k, rows, 0.0).astype(BF16))
        asked = part if asked is None else asked + part
    for c in range(owners // n):
        negative = column(neg_ref[:, c * n : (c + 1) * n])
        ask_ref[c * n : (c + 1) * n, :] = jnp.where(
            lane == CAP, negative, asked[c * n : (c + 1) * n]
        ).astype(jnp.int32)


def spread_slot(wide, base, k, rows):
    for c in range(CHUNKS):
        wide[pl.ds(base + k * CHUNKS + c, rows.shape[0], stride=NBANK), :] = rows[
            :, c * LANES : (c + 1) * LANES
        ]


def slot_rows(wide, base, k, count):
    return jnp.concatenate(
        [wide[pl.ds(base + k * CHUNKS + c, count, stride=NBANK), :] for c in range(CHUNKS)], axis=1
    ).astype(BF16)


def piece(ref, i):
    size = ref.shape[0] // PIECES
    return ref.at[pl.ds(i * size, size), :]


def by_chip(asks_ref, core, items):
    count = asks_ref.shape[0] // (2 * items)
    return jnp.concatenate(
        [
            asks_ref[(2 * z + core) * items : (2 * z + core + 1) * items, :]
            for z in range(count)
        ],
        axis=0,
    )


def serve_kernel(items, loaded, asks_ref, table_ref, out_ref, wide, narrow, sems):
    chips = asks_ref.shape[0] // 2
    part = chips // PIECES
    rows = table_ref.shape[0]
    asks = [by_chip(asks_ref, core, items) for core in range(2)]
    loaded()
    table = table_ref[...]
    row_id = lax.broadcasted_iota(jnp.int32, (part, rows), 1)
    copies = []
    for i in range(PIECES):
        base = i * part * NBANK
        for seat in range(SEATS):
            core, k = (0, CAP) if seat == 2 * CAP else divmod(seat, CAP)
            asked = asks[core][i * part : (i + 1) * part, k : k + 1]
            hot = jnp.where(asked == row_id, 1.0, 0.0).astype(BF16)
            spread_slot(wide, base, seat, dot(hot, table))
        narrow[base : base + part * NBANK, :] = wide[base : base + part * NBANK, :].astype(BF16)
        copies.append(pltpu.make_async_copy(piece(narrow, i), piece(out_ref, i), sems.at[i]))
        copies[-1].start()
    for copy in copies:
        copy.wait()


def pair_masks(n):
    lane = lax.broadcasted_iota(jnp.int32, (n, LANES), 1)
    return lane < (LANES // 2)


def both_heads(part, low):
    zero = jnp.zeros_like(part)
    return jnp.concatenate([jnp.where(low, part, zero), jnp.where(low, zero, part)], axis=0)


def same_before(place_ref, sess_ref, ahead):
    block = place_ref[0] + ahead
    inside = block < sess_ref.shape[1]
    block = jnp.minimum(block, sess_ref.shape[1] - 1)
    here = sess_ref[0, block]
    near = inside & (block >= 1) & (sess_ref[0, jnp.maximum(block - 1, 0)] == here)
    far = inside & (block >= 2) & (sess_ref[0, jnp.maximum(block - 2, 0)] == here)
    return jnp.where(near, 1, 0), jnp.where(far, 1, 0)


def window_scale(place_ref, sess_ref, n):
    near, far = same_before(place_ref, sess_ref, 0)
    place = lax.broadcasted_iota(jnp.int32, (n, 3 * n), 0)
    lane = lax.broadcasted_iota(jnp.int32, (n, 3 * n), 1)
    count = place + 1 + n * (near + far)
    allowed = jnp.where(
        lane < n, far, jnp.where(lane < 2 * n, near, jnp.where(lane - 2 * n <= place, 1, 0))
    )
    scale = allowed.astype(F32) * (1.0 / count.astype(F32))
    return jnp.concatenate([scale, scale], axis=0)


def forward_kernel(
    loaded,
    place_ref,
    sess_ref,
    far_ref,
    near_ref,
    own_ref,
    gain_ref,
    w_in_ref,
    w_out_ref,
    unit_ref,
    length_ref,
    hat_ref,
    scale_ref,
    gate_ref,
    query_ref,
    slope_gq_ref,
    slope_vk_ref,
    keys_ref,
    values_ref,
    user_ref,
):
    n, width = own_ref.shape
    loaded()
    gain = gain_ref[...]
    hist_f = own_ref[...].astype(F32)

    def normed_in(values):
        return (layer_stats(values)[0] * gain).astype(BF16)

    projected = dot(normed_in(hist_f), w_in_ref[...])
    sigma = sigmoid(projected)
    slope = sigma * (1.0 + projected * (1.0 - sigma))
    slope_gq_ref[:, :width] = slope[:, :width]
    slope_vk_ref[:, :width] = slope[:, width : 2 * width]
    slope_gq_ref[:, width:] = slope[:, 2 * width : 3 * width]
    slope_vk_ref[:, width:] = slope[:, 3 * width :]
    act = (projected * sigma).astype(BF16)
    gate_ref[...] = act[:, :width]
    query_ref[...] = act[:, 2 * width : 3 * width]
    before = jnp.concatenate(
        [normed_in(far_ref[...].astype(F32)), normed_in(near_ref[...].astype(F32))], axis=0
    )
    values_before = dot(before, w_in_ref[:, width : 2 * width])
    keys_before = dot(before, w_in_ref[:, 3 * width :])
    values_ref[: 2 * n, :] = (values_before * sigmoid(values_before)).astype(BF16)
    keys_ref[: 2 * n, :] = (keys_before * sigmoid(keys_before)).astype(BF16)
    values_ref[2 * n :, :] = act[:, width : 2 * width]
    keys_ref[2 * n :, :] = act[:, 3 * width :]
    scale = window_scale(place_ref, sess_ref, n)
    low = pair_masks(n)
    score_scale = 1.0 / math.sqrt(width // HEADS)
    attended = []
    for pair in range(HEADS // 2):
        lanes = slice(pair * LANES, (pair + 1) * LANES)
        queries = both_heads(act[:, 2 * width + pair * LANES : 2 * width + (pair + 1) * LANES], low)
        scores = dot(queries, keys_ref[:, lanes], (1, 1)) * score_scale
        weights = (scores * sigmoid(scores) * scale).astype(BF16)
        both = dot(weights, values_ref[:, lanes])
        attended.append(jnp.where(low, both[:n], both[n:]))
    attn_hat, scale_a = layer_stats(jnp.concatenate(attended, axis=1))
    hat_ref[...] = attn_hat
    scale_ref[...] = jnp.broadcast_to(scale_a, scale_ref.shape)
    gated = (attn_hat * act[:, :width].astype(F32)).astype(BF16)
    user_out = dot(gated, w_out_ref[...]) + hist_f
    user_len = jnp.sqrt(jnp.sum(user_out * user_out, axis=-1, keepdims=True) + 1e-06)
    user_unit = user_out / user_len
    unit_ref[...] = user_unit
    user_ref[...] = user_unit.astype(BF16)
    length_ref[...] = jnp.broadcast_to(user_len, length_ref.shape)


def local_slots(slots, core, items):
    bits = items.bit_length() - 1
    owner = slots >> 1
    local = ((owner >> (bits + 1)) << bits) + (owner & (items - 1))
    return jnp.where(((owner >> bits) & 1) == core, local * CAP + (slots & 1), -1)


def as_column(row):
    n = row.shape[1]
    lead = lax.broadcasted_iota(jnp.int32, (n, n), 0)
    lane = lax.broadcasted_iota(jnp.int32, (n, n), 1)
    spread = jnp.broadcast_to(row, (n, n))
    return jnp.sum(jnp.where(lead == lane, spread, 0.0), axis=1, keepdims=True)


def as_row(column):
    n = column.shape[0]
    lead = lax.broadcasted_iota(jnp.int32, (n, n), 0)
    lane = lax.broadcasted_iota(jnp.int32, (n, n), 1)
    return jnp.sum(jnp.where(lead == lane, column, 0.0), axis=0, keepdims=True)


def halves(convert, values, axis):
    n = values.shape[axis] // 2
    first, second = (values[:, :n], values[:, n:]) if axis else (values[:n], values[n:])
    return jnp.concatenate([convert(first), convert(second)], axis=1 - axis)


def softmax_kernel(
    items,
    loaded,
    place_ref,
    fetched_ref,
    neg_row_ref,
    slots_ref,
    users_ref,
    stats_ref,
    neg_exp_ref,
    neg_rows_ref,
    pos_rows_ref,
    wide,
    held_rows,
    held_exp,
    held_sems,
):
    chips = neg_row_ref.shape[1]
    n = users_ref.shape[0] // 2
    wide[...] = fetched_ref[...].astype(F32)
    neg_rows = slot_rows(wide, 0, 2 * CAP, chips)
    held_rows[:chips, :] = neg_rows
    copies = [
        pltpu.make_async_copy(held_rows.at[pl.ds(0, chips), :], neg_rows_ref, held_sems.at[0]),
        pltpu.make_async_copy(held_exp, neg_exp_ref, held_sems.at[1]),
        pltpu.make_async_copy(
            held_rows.at[pl.ds(chips, 2 * n), :], pos_rows_ref, held_sems.at[2]
        ),
    ]
    copies[0].start()
    neg_bf = item_norm(neg_rows)[0].astype(BF16)
    loaded()
    users = users_ref[...]
    neg_row = neg_row_ref[...] + 1
    exponent = jnp.zeros(neg_row.shape, F32)
    for level in range(1, 8):
        exponent = exponent + jnp.where(neg_row >= (1 << level), 1.0, 0.0)
    shift = math.log(8) + exponent * math.log(2.0)
    neg_exp = jnp.exp(dot(users, neg_bf, (1, 1)) / TAU + shift)
    held_exp[...] = neg_exp
    copies[1].start()
    slots = local_slots(slots_ref[...], place_ref[1], items)
    lane = lax.broadcasted_iota(jnp.int32, (n, chips), 1) * CAP
    pos_rows, here = [], []
    for core in range(2):
        column = as_column(slots[:, core * n : (core + 1) * n].astype(F32)).astype(jnp.int32)
        here.append(jnp.where(column >= 0, 1.0, 0.0))
        hots = [jnp.where(column == lane + k, 1.0, 0.0).astype(BF16) for k in range(CAP)]
        rows = [slot_rows(wide, 0, core * CAP + k, chips) for k in range(CAP)]
        pos_rows.append(dot(jnp.concatenate(hots, axis=1), jnp.concatenate(rows, axis=0)))
    pos_rows = jnp.concatenate(pos_rows, axis=0)
    held_rows[chips:, :] = pos_rows.astype(BF16)
    copies[2].start()
    pos_bf = item_norm(pos_rows)[0].astype(BF16).astype(F32)
    along = jnp.sum(users.astype(F32) * pos_bf, axis=-1, keepdims=True)
    pos_exp = jnp.concatenate(here, axis=0) * jnp.exp(along / TAU)
    total = pos_exp + jnp.sum(neg_exp, axis=-1, keepdims=True)
    stats_ref[0:1, :] = halves(as_row, total, 0)
    stats_ref[1:2, :] = halves(as_row, pos_exp, 0)
    for copy in copies:
        copy.wait()


def send_kernel(
    items,
    loaded,
    place_ref,
    stats_ref,
    stats_other_ref,
    neg_rows_ref,
    pos_rows_ref,
    users_ref,
    slots_ref,
    neg_exp_ref,
    send_ref,
    own_part_ref,
    other_part_ref,
    wide,
    narrow,
    sems,
    held,
    held_sems,
):
    chips = neg_rows_ref.shape[0]
    n = users_ref.shape[0] // 2
    core_here = place_ref[1]
    loaded(2)
    neg_unit, neg_len = item_norm(neg_rows_ref[...])
    neg_bf = neg_unit.astype(BF16)
    pos_unit, pos_len = item_norm(pos_rows_ref[...])
    pos_bf = pos_unit.astype(BF16).astype(F32)
    loaded()
    users = users_ref[...]
    user_f = users.astype(F32)
    slots = local_slots(slots_ref[...], core_here, items)
    total = stats_ref[0:1, :] + stats_other_ref[0:1, :]
    denominator = halves(as_column, total, 1)
    delta = jnp.where(slots >= 0, stats_ref[1:2, :] / total - 1.0, 0.0)
    pos_delta = halves(as_column, delta, 1)
    neg_prob = (neg_exp_ref[...] / denominator).astype(BF16)
    raw_pos = pos_delta * user_f / TAU
    pos_grad = (raw_pos - pos_unit * jnp.sum(pos_unit * raw_pos, axis=-1, keepdims=True)) / pos_len
    pos_grad = pos_grad.astype(BF16)
    unit_part = (pos_delta * pos_bf + dot(neg_prob, neg_bf)) / TAU
    first = core_here == 0
    held[:n, :] = jnp.where(first, unit_part[:n], unit_part[n:])
    held[n:, :] = jnp.where(first, unit_part[n:], unit_part[:n])
    copies = [
        pltpu.make_async_copy(held.at[pl.ds(n, n), :], other_part_ref, held_sems.at[0]),
        pltpu.make_async_copy(held.at[pl.ds(0, n), :], own_part_ref, held_sems.at[1]),
    ]
    for copy in copies:
        copy.start()
    part = chips // PIECES
    lead = lax.broadcasted_iota(jnp.int32, (part, n), 0) * CAP
    for i in range(PIECES):
        base = i * part * NBANK
        for core in range(2):
            row = slots[:, core * n : (core + 1) * n]
            for k in range(CAP):
                hot = jnp.where(row == lead + (i * part * CAP + k), 1.0, 0.0).astype(BF16)
                placed = dot(hot, pos_grad[core * n : (core + 1) * n])
                spread_slot(wide, base, core * CAP + k, placed)
        own = slice(i * part, (i + 1) * part)
        raw_neg = dot(neg_prob[:, own], users, (0, 0)) / TAU
        along = jnp.sum(neg_unit[own] * raw_neg, axis=-1, keepdims=True)
        spread_slot(wide, base, 2 * CAP, (raw_neg - neg_unit[own] * along) / neg_len[own])
        narrow[base : base + part * NBANK, :] = wide[base : base + part * NBANK, :].astype(BF16)
        copies.append(pltpu.make_async_copy(piece(narrow, i), piece(send_ref, i), sems.at[i]))
        copies[-1].start()
    for copy in copies:
        copy.wait()


def heads_back_kernel(
    loaded,
    place_ref,
    sess_ref,
    own_part_ref,
    other_part_ref,
    unit_ref,
    length_ref,
    w_out_ref,
    gate_ref,
    query_ref,
    hat_ref,
    scale_ref,
    keys_ref,
    values_ref,
    slope_ref,
    w_in_ref,
    own_ref,
    near_ref,
    far_ref,
    in_part_ref,
    user_grad_ref,
):
    n, width = hat_ref.shape
    loaded()
    attn_hat = hat_ref[...]
    user_unit = unit_ref[...]
    unit_grad = own_part_ref[...] + other_part_ref[...]
    user_grad = (
        unit_grad - user_unit * jnp.sum(user_unit * unit_grad, axis=-1, keepdims=True)
    ) / length_ref[:, 0:1]
    user_grad_ref[...] = user_grad
    gated_grad = dot(user_grad.astype(BF16), w_out_ref[...], (1, 1))
    hat_grad = gated_grad * gate_ref[...].astype(F32)
    upstream = norm_back(hat_grad, attn_hat, scale_ref[:, 0:1]).astype(BF16)
    scale = window_scale(place_ref, sess_ref, n)
    low = pair_masks(n)
    score_scale = 1.0 / math.sqrt(width // HEADS)
    query_grads = []
    for pair in range(HEADS // 2):
        first = pair * LANES
        lanes = slice(first, first + LANES)
        later = slice(width + first, width + first + LANES)
        queries = both_heads(query_ref[:, lanes], low)
        grads = both_heads(upstream[:, lanes], low)
        keys = keys_ref[:, lanes]
        scores = dot(queries, keys, (1, 1)) * score_scale
        weight_grad = dot(grads, values_ref[:, lanes], (1, 1))
        sigma = sigmoid(scores)
        weights = (scores * sigma * scale).astype(BF16)
        slope = sigma * (1.0 + scores * (1.0 - sigma))
        score_grad = (weight_grad * slope * (scale * score_scale)).astype(BF16)
        both = dot(score_grad, keys)
        query_grads.append(jnp.where(low, both[:n], both[n:]))
        key_grad = dot(score_grad, queries, (0, 0))
        value_grad = dot(weights, grads, (0, 0))
        far_ref[:, lanes] = value_grad[:n].astype(BF16)
        near_ref[:, lanes] = value_grad[n : 2 * n].astype(BF16)
        own_ref[:, lanes] = value_grad[2 * n :]
        far_ref[:, later] = key_grad[:n].astype(BF16)
        near_ref[:, later] = key_grad[n : 2 * n].astype(BF16)
        own_ref[:, later] = key_grad[2 * n :]
    gate_part = (gated_grad * attn_hat * slope_ref[:, :width]).astype(BF16)
    query_part = (jnp.concatenate(query_grads, axis=1) * slope_ref[:, width:]).astype(BF16)
    in_part_ref[...] = dot(gate_part, w_in_ref[:, :width], (1, 1)) + dot(
        query_part, w_in_ref[:, 2 * width : 3 * width], (1, 1)
    )


def last_kernel(
    items,
    loaded,
    place_ref,
    returned_ref,
    summed_ref,
    far_ref,
    asks_ref,
    own_grad_ref,
    slope_ref,
    in_part_ref,
    w_in_ref,
    gain_ref,
    hist_ref,
    user_grad_ref,
    near_ref,
    table_grad_ref,
    history_grad_ref,
    wide,
    held,
    held_sem,
):
    width = hist_ref.shape[1]
    chips = asks_ref.shape[0] // 2
    rows = table_grad_ref.shape[0]
    wide[...] = returned_ref[...].astype(F32)
    loaded(1)
    asks = [jnp.transpose(by_chip(asks_ref, core, items).astype(F32)) for core in range(2)]
    row_id = lax.broadcasted_iota(jnp.int32, (rows, chips), 0).astype(F32)
    hots, parts = [], []
    for seat in range(SEATS):
        core, k = (0, CAP) if seat == 2 * CAP else divmod(seat, CAP)
        hots.append(jnp.where(asks[core][k : k + 1] == row_id, 1.0, 0.0).astype(BF16))
        parts.append(slot_rows(wide, 0, seat, chips))
    total = dot(jnp.concatenate(hots, axis=1), jnp.concatenate(parts, axis=0))
    held[...] = total.astype(BF16)
    copy = pltpu.make_async_copy(held, table_grad_ref, held_sem)
    copy.start()
    loaded()
    near = jnp.where(place_ref[1] == 0, near_ref[...].astype(F32), summed_ref[...].astype(F32))
    come = near + far_ref[...].astype(F32)
    proj_grad = ((own_grad_ref[...] + come) * slope_ref[...]).astype(BF16)
    in_grad = (
        in_part_ref[...]
        + dot(proj_grad[:, :width], w_in_ref[:, width : 2 * width], (1, 1))
        + dot(proj_grad[:, width:], w_in_ref[:, 3 * width :], (1, 1))
    )
    normed_x, scale_x = layer_stats(hist_ref[...].astype(F32))
    back = norm_back(in_grad * gain_ref[...], normed_x, scale_x)
    history_grad_ref[...] = (back + user_grad_ref[...]).astype(BF16)
    copy.wait()


def passed_along(shard, by):
    axes = ("z", "core")
    count = lax.axis_size(axes)
    pairs = [(i, i + by) for i in range(count) if 0 <= i + by < count]
    return lax.ppermute(shard, axes, pairs)


def from_first_core(shard, by):
    axes = ("z", "core")
    count = lax.axis_size(axes)
    return lax.ppermute(shard, axes, [(i, i - by) for i in range(0, count, 2) if i >= by])


def swapped(shard):
    return lax.ppermute(shard, "core", [(0, 1), (1, 0)])


def on_device(history, ln_gain, w_in, w_out, item_table, sessions, pos_owner, pos_row, neg_rows):
    n, width = history.shape[1:]
    items = lax.axis_size("items")
    chips = lax.axis_size("z") * items
    owners = 2 * chips
    rows = item_table.shape[0]
    core = lax.axis_index("core")
    place = jnp.stack([2 * lax.axis_index("z") + core, core]).astype(jnp.int32)
    own = history[0]
    gain = ln_gain.reshape(1, width)
    neg_row = neg_rows.reshape(1, owners)

    def exchange(shard, axes, chunk):
        shape = shard.shape
        split = shard.reshape((-1,) + chunk)
        return lax.all_to_all(split, axes, split_axis=0, concat_axis=0, tiled=True).reshape(shape)

    def by_core(mine, other, axis):
        return jnp.where(
            core == 0,
            jnp.concatenate([mine, other], axis=axis),
            jnp.concatenate([other, mine], axis=axis),
        )

    ask, slot_row, slot_col = call(
        ask_kernel,
        [shaped((owners, LANES), jnp.int32), shaped((1, n), jnp.int32), shaped((n, 1), jnp.int32)],
        [VMEM, VMEM, VMEM],
        (pos_owner.reshape(1, n), pos_row, neg_row),
        2 * CAP * owners * n * LANES,
    )
    asks = exchange(ask, ("z", "core", "items"), (1, LANES))
    near = passed_along(own, 1)
    far = passed_along(own, 2)

    big = chips * NBANK
    staging = [
        pltpu.VMEM((big, LANES), BF16),
        pltpu.VMEM((big, LANES), F32),
        pltpu.SemaphoreType.DMA((PIECES,)),
    ]
    outward = [staging[1], staging[0], staging[2]]
    (served,) = call(
        functools.partial(serve_kernel, items),
        [shaped((big, LANES), BF16)],
        [VMEM, None],
        (asks, item_table),
        2 * SEATS * chips * rows * width,
        outward,
        mib=40,
        out_specs=(HBM,),
    )
    served, near, far = lax.optimization_barrier((served, near, far))
    fetched = exchange(served, ("z", "items"), (SEATS, CHUNKS, LANES))

    unit, length, attn_hat, scale_a, gate, query, slope_gq, slope_vk, keys, values, user = call(
        forward_kernel,
        [
            pltpu.HBM((n, width), F32),
            pltpu.HBM((n, LANES), F32),
            pltpu.HBM((n, width), F32),
            pltpu.HBM((n, LANES), F32),
            pltpu.HBM((n, width), BF16),
            pltpu.HBM((n, width), BF16),
            pltpu.HBM((n, 2 * width), F32),
            pltpu.HBM((n, 2 * width), F32),
            pltpu.HBM((3 * n, width), BF16),
            pltpu.HBM((3 * n, width), BF16),
            pltpu.HBM((n, width), BF16),
        ],
        [SMEM, SMEM, VMEM, VMEM] + [None] * 4,
        (place, sessions, far, near, own, gain, w_in, w_out),
        2 * n * width * width * 12,
        mib=40,
    )

    users = by_core(user, swapped(user), 0)
    slots = by_core(slot_row, swapped(slot_row), 1)
    neg_here = lax.dynamic_index_in_dim(
        neg_rows.reshape(chips // items, 2, items), core, axis=1, keepdims=False
    ).reshape(1, chips)
    stats, neg_exp, neg_kept, pos_kept = call(
        functools.partial(softmax_kernel, items),
        [
            shaped((2, 2 * n), F32),
            pltpu.HBM((2 * n, chips), F32),
            pltpu.HBM((chips, width), BF16),
            pltpu.HBM((2 * n, width), BF16),
        ],
        [SMEM, VMEM] + [None] * 3,
        (place, fetched, neg_here, slots, users),
        2 * n * width * owners * 3,
        [
            staging[1],
            pltpu.VMEM((chips + 2 * n, width), BF16),
            pltpu.VMEM((2 * n, chips), F32),
            pltpu.SemaphoreType.DMA((3,)),
        ],
        mib=40,
        out_specs=(VMEM, HBM, HBM, HBM),
    )
    send, own_part, other_part = call(
        functools.partial(send_kernel, items),
        [shaped((big, LANES), BF16), pltpu.HBM((n, width), F32), pltpu.HBM((n, width), F32)],
        [SMEM, VMEM, VMEM] + [None] * 5,
        (place, stats, swapped(stats), neg_kept, pos_kept, users, slots, neg_exp),
        2 * n * width * owners * 4,
        outward + [pltpu.VMEM((2 * n, width), F32), pltpu.SemaphoreType.DMA((2,))],
        mib=40,
        out_specs=(HBM, HBM, HBM),
    )
    returned = exchange(send, ("z", "items"), (SEATS, CHUNKS, LANES))

    own_grad, near_grad, far_grad, in_part, user_grad = call(
        heads_back_kernel,
        [
            shaped((n, 2 * width), F32),
            shaped((n, 2 * width), BF16),
            shaped((n, 2 * width), BF16),
            shaped((n, width), F32),
            shaped((n, width), F32),
        ],
        [SMEM, SMEM] + [None] * 13,
        (
            place,
            sessions,
            own_part,
            swapped(other_part),
            unit,
            length,
            w_out,
            gate,
            query,
            attn_hat,
            scale_a,
            keys,
            values,
            slope_gq,
            w_in,
        ),
        2 * n * width * width * 12,
    )
    near_chip = swapped(near_grad)
    summed = (near_grad.astype(F32) + swapped(far_grad).astype(F32)).astype(BF16)
    summed_back = from_first_core(summed, 1)
    far_back = from_first_core(far_grad, 2)
    table_grad, history_grad = call(
        functools.partial(last_kernel, items),
        [shaped((rows, width), BF16), shaped((n, width), BF16)],
        [SMEM] + [VMEM] * 3 + [None] * 9,
        (
            place,
            returned,
            summed_back,
            far_back,
            asks,
            own_grad,
            slope_vk,
            in_part,
            w_in,
            gain,
            own,
            user_grad,
            near_chip,
        ),
        2 * SEATS * chips * rows * width,
        [staging[1], pltpu.VMEM((rows, width), BF16), pltpu.SemaphoreType.DMA(())],
        mib=40,
        out_specs=(HBM, VMEM),
    )
    return history_grad[None], table_grad


def solution(mesh):
    hist, items = mesh.shape["hist"], mesh.shape["items"]
    split = jax.sharding.Mesh(
        mesh.devices.reshape(hist // 2, 2, items), ("z", "core", "items")
    )
    return jax.shard_map(
        on_device,
        mesh=split,
        in_specs=(
            P("items", ("z", "core"), None),
            P(),
            P(),
            P(),
            P(("z", "core", "items"), None),
            P("items", None),
            P("items", ("z", "core"), None),
            P("items", ("z", "core")),
            P("items", None, None),
        ),
        out_specs=(P("items", ("z", "core"), None), P(("z", "core", "items"), None)),
        check_vma=False,
    )
```
